512 devices in a mesh: dp: 32 (over z, x), chan: 16 (over y, core).
Axes of the slice: x: 4, y: 8, z: 8, core: 2. Of those that a mesh axis runs over, the one named last changes fastest.
Arguments:
- spec_u: float32 [2, 32768, 4096], P(None, 'dp', 'chan'), may hold values from -60 to 60
- spec_g: float32 [2, 32768, 4096], P(None, 'dp', 'chan'), may hold values from -60 to 60
- decay_length: float32 [4096], P('chan'), may hold values from 32 to 32768
- w_first: float32 [33, 64], replicated, may hold values from -1 to 1
- w_second: float32 [64, 64], replicated, may hold values from -0.75 to 0.75
- w_out: float32 [64, 4096], P(None, 'chan'), may hold values from -0.75 to 0.75
- moments_first: float32 [2, 33, 64], replicated, may hold values from -0.006 to 0.006, as said below
- moments_second: float32 [2, 64, 64], replicated, may hold values from -0.006 to 0.006, as said below
- moments_out: float32 [2, 64, 4096], P(None, None, 'chan'), may hold values from -0.006 to 0.006, as said below
Outputs:
- step_first: float32 [33, 64], replicated
- step_second: float32 [64, 64], replicated
- step_out: float32 [64, 4096], P(None, 'chan')
The draws below stay inside these ranges and needn't reach their ends.
Inputs may be any that keep to these rules, and one draw needn't show every extreme that they name: `moments_first`: entry 0 is the first moment, entry 1 the second moment, which is positive. `moments_second`: entry 0 is the first moment, entry 1 the second moment, which is positive. `moments_out`: entry 0 is the first moment, entry 1 the second moment, which is positive.
All inputs are finite; a program needn't handle non-finite values.
Results may differ from the reference program's by a relative error of at most 0.00025.
Values sent between devices are 32-bit elements; how exact they have to be, the bound alone decides.
A program may use at most 64 MiB of HBM per device.

```python
import math
import jax
import jax.numpy as jnp
from jax import lax

D = 4096
SEQ = 16384
FREQS = 32768
BANDS = 16
EMB = 33
HID = 64


def spectrum_scales(key):
    keys = jax.random.split(key, 2)
    chan = jnp.arange(D, dtype=jnp.float32) / D
    chan_scale = jnp.exp(0.5 * math.log(10.0) * (0.7 * chan + 0.3 * jax.random.uniform(keys[0], (D,))))
    freq_scale = jnp.exp(0.5 * math.log(10.0) * jax.random.uniform(keys[1], (FREQS,)))
    return freq_scale[None, :, None] * chan_scale[None, None, :]


def draw_spec_u(key, part):
    key = jax.random.fold_in(key, 11)
    keys = jax.random.split(key, 2)
    scales = spectrum_scales(keys[0])
    base = jnp.clip(jax.random.normal(keys[1], (2, FREQS, D)), -6.0, 6.0)
    return (base * scales).astype(jnp.float32)


def draw_spec_g(key, part):
    key = jax.random.fold_in(key, 23)
    keys = jax.random.split(key, 2)
    scales = spectrum_scales(keys[0])
    base = jnp.clip(jax.random.normal(keys[1], (2, FREQS, D)), -6.0, 6.0)
    return (base * scales).astype(jnp.float32)


def second_moment(key, shape):
    return jnp.exp(jax.random.uniform(key, shape, minval=math.log(1e-09), maxval=math.log(1e-07)))


def draw_moments_first(key, part):
    key = jax.random.fold_in(key, 37)
    keys = jax.random.split(key, 2)
    shape = (EMB, HID)
    first = jnp.clip(0.001 * jax.random.normal(keys[0], shape), -0.006, 0.006)
    return jnp.stack([first, second_moment(keys[1], shape)]).astype(jnp.float32)


def draw_moments_second(key, part):
    key = jax.random.fold_in(key, 41)
    keys = jax.random.split(key, 2)
    shape = (HID, HID)
    first = jnp.clip(0.001 * jax.random.normal(keys[0], shape), -0.006, 0.006)
    return jnp.stack([first, second_moment(keys[1], shape)]).astype(jnp.float32)


def draw_moments_out(key, part):
    key = jax.random.fold_in(key, 53)
    keys = jax.random.split(key, 2)
    shape = (HID, D)
    first = jnp.clip(0.001 * jax.random.normal(keys[0], shape), -0.006, 0.006)
    return jnp.stack([first, second_moment(keys[1], shape)]).astype(jnp.float32)


def block_scale(stream_key, dims, cuts, low, largest):
    gain = 1.0
    for dim, blocks in cuts:
        steps = jax.random.uniform(jax.random.fold_in(jax.random.fold_in(stream_key, 6), dim), (blocks,), jnp.float32, low / len(cuts), largest / len(cuts))
        gain = gain * jnp.repeat(jnp.exp(steps), dims[dim] // blocks).reshape((-1,) + (1,) * (len(dims) - 1 - dim))
    return gain


def centred(key, extent, deviation, most, shards=(), kind=jnp.bfloat16):
    loudness = block_scale(key, extent, shards, -0.22, 0.18) if shards else 1.0
    values = jax.random.normal(key, extent, jnp.float32) * deviation * loudness
    return jnp.minimum(jnp.maximum(values, -most), most).astype(kind)


def setup_inputs(seed: int = 0) -> dict:
    arg_keys = jax.random.split(jax.random.key(seed), 10)
    spec_u = draw_spec_u(jax.random.fold_in(arg_keys[9], 71), 0)
    spec_g = draw_spec_g(jax.random.fold_in(arg_keys[9], 71), 0)
    decay_length = jnp.clip(jnp.exp(math.log(32768.0) - 6.931472 * jax.random.uniform(arg_keys[2], (D,), jnp.float32) ** block_scale(arg_keys[2], (D,), ((0, 16),), -0.2, 0.2)), 32.0, 32768.0)
    w_first = centred(arg_keys[3], (EMB, HID), EMB ** -0.5, 1.0, (), jnp.float32)
    w_second = centred(arg_keys[4], (HID, HID), HID ** -0.5, 0.75, (), jnp.float32)
    w_out = centred(arg_keys[5], (HID, D), HID ** -0.5, 0.75, ((1, 16),), jnp.float32)
    moments_first = draw_moments_first(jax.random.fold_in(arg_keys[9], 71), 0)
    moments_second = draw_moments_second(jax.random.fold_in(arg_keys[9], 71), 0)
    moments_out = draw_moments_out(jax.random.fold_in(arg_keys[9], 71), 0)
    return dict(spec_u=spec_u, spec_g=spec_g, decay_length=decay_length, w_first=w_first, w_second=w_second, w_out=w_out, moments_first=moments_first, moments_second=moments_second, moments_out=moments_out)


beta_one = 0.9
beta_two = 0.999
adam_count = 10.0
adam_eps = 1e-08
weight_decay = 0.1
clip_norm = 1.0

def features(positions, length):
    bands = jnp.arange(1, BANDS + 1, dtype=jnp.int32)
    phase = bands[:, None] * positions[None, :] % length
    angle = 2.0 * math.pi / length * phase.astype(jnp.float32)
    first = (positions.astype(jnp.float32) / length)[None, :]
    return jnp.concatenate([first, jnp.cos(angle), jnp.sin(angle)], axis=0)

def adam_step(grad, weight, moments, scale):
    g = grad * scale
    first = beta_one * moments[0] + (1.0 - beta_one) * g
    second = beta_two * moments[1] + (1.0 - beta_two) * g * g
    first_hat = first / (1.0 - beta_one ** adam_count)
    second_hat = second / (1.0 - beta_two ** adam_count)
    return first_hat / (jnp.sqrt(second_hat) + adam_eps) + weight_decay * weight

def reference(spec_u, spec_g, decay_length, w_first, w_second, w_out, moments_first, moments_second, moments_out):
    highest = lax.Precision.HIGHEST
    prod_re = spec_g[0] * spec_u[0] + spec_g[1] * spec_u[1]
    prod_im = spec_g[1] * spec_u[0] - spec_g[0] * spec_u[1]
    signal = jnp.fft.ifft(prod_re + 1j * prod_im, axis=0)
    filter_grad = jnp.real(signal[:SEQ]).astype(jnp.float32)
    positions = jnp.arange(SEQ, dtype=jnp.int32)
    feats = features(positions, SEQ)
    pre_one = jnp.dot(w_first.T, feats, precision=highest)
    act_one = jnp.sin(pre_one)
    pre_two = jnp.dot(w_second.T, act_one, precision=highest)
    act_two = jnp.sin(pre_two)
    window = jnp.exp(-positions.astype(jnp.float32)[:, None] / decay_length[None, :])
    out_grad = filter_grad * window
    grad_out = jnp.dot(act_two, out_grad, precision=highest)
    back_two = jnp.dot(w_out, out_grad.T, precision=highest) * jnp.cos(pre_two)
    grad_second = jnp.dot(act_one, back_two.T, precision=highest)
    back_one = jnp.dot(w_second, back_two, precision=highest) * jnp.cos(pre_one)
    grad_first = jnp.dot(feats, back_one.T, precision=highest)
    total = jnp.sum(grad_first * grad_first) + jnp.sum(grad_second * grad_second) + jnp.sum(grad_out * grad_out)
    scale = jnp.minimum(1.0, clip_norm / (jnp.sqrt(total) + 1e-06))
    step_first = adam_step(grad_first, w_first, moments_first, scale)
    step_second = adam_step(grad_second, w_second, moments_second, scale)
    step_out = adam_step(grad_out, w_out, moments_out, scale)
    return (step_first, step_second, step_out)
```

```python
import functools
import math

import jax
import jax.numpy as jnp
import numpy as np
from jax import lax
from jax.experimental import pallas as pl
from jax.experimental.pallas import tpu as pltpu
from jax.sharding import PartitionSpec as P

MESH = pl.DeviceIdType.MESH
HIGHEST = lax.Precision.HIGHEST

BANDS = 16
HID = 64
DP = 32
CHAN = 16
FREQS = 32768
SEQ = 16384
ROWS = 1024
COLS = 256

beta_one = 0.9
beta_two = 0.999
adam_count = 10.0
adam_eps = 1e-08
weight_decay = 0.1
clip_norm = 1.0


def adam_step(grad, weight, first, second, scale):
    g = grad * scale
    first = beta_one * first + (1.0 - beta_one) * g
    second = beta_two * second + (1.0 - beta_two) * g * g
    first_hat = first / (1.0 - beta_one**adam_count)
    second_hat = second / (1.0 - beta_two**adam_count)
    return first_hat / (jnp.sqrt(second_hat) + adam_eps) + weight_decay * weight


def split(x):
    high = x.astype(jnp.bfloat16)
    low = (x - high.astype(jnp.float32)).astype(jnp.bfloat16)
    return high, low


def dot3(a, b, dims):
    def one(x, y):
        return lax.dot_general(x, y, (dims, ((), ())), preferred_element_type=jnp.float32)

    return one(a[0], b[0]) + one(a[0], b[1]) + one(a[1], b[0])


NN = ((1,), (0,))
NT = ((1,), (1,))


def times(z, angle_num, angle_den):
    re, im = z
    k = angle_num % angle_den
    if k == 0:
        return re, im
    if 4 * k == angle_den:
        return -im, re
    if 2 * k == angle_den:
        return -re, -im
    if 4 * k == 3 * angle_den:
        return im, -re
    if 8 * k == angle_den:
        r = math.sqrt(0.5)
        return (re - im) * r, (re + im) * r
    if 8 * k == 3 * angle_den:
        r = math.sqrt(0.5)
        return (re + im) * (-r), (re - im) * r
    c, s = math.cos(2 * math.pi * k / angle_den), math.sin(2 * math.pi * k / angle_den)
    return re * c - im * s, re * s + im * c


def dft(values):
    n = len(values)
    if n == 1:
        return values
    even, odd = dft(values[0::2]), dft(values[1::2])
    low, high = [], []
    for k in range(n // 2):
        t = times(odd[k], k, n)
        low.append((even[k][0] + t[0], even[k][1] + t[1]))
        high.append((even[k][0] - t[0], even[k][1] - t[1]))
    return low + high


def constants():
    lane = np.arange(256)[:, None] * np.arange(128)[None, :] % 256
    angle = 2.0 * np.pi / 256 * lane
    table = np.concatenate([np.cos(angle), -np.sin(angle)], axis=0).astype(np.float32)
    high = table.astype(jnp.bfloat16)
    low = (table - high.astype(np.float32)).astype(jnp.bfloat16)
    v = np.arange(16)[:, None] + 16 * np.arange(8)[None, :]
    angle = 2.0 * np.pi / FREQS * (v[:, :, None] * np.arange(256)[None, None, :])
    last = (np.stack([np.cos(angle), np.sin(angle)]) / FREQS).astype(np.float32)
    angle = 2.0 * np.pi / 128 * (np.arange(8)[:, None] * np.arange(16)[None, :])
    first = np.stack([np.cos(angle), np.sin(angle)], axis=-1).astype(np.float32)
    return high, low, last, first.reshape(-1)


def kernel(
    u_hbm, g_hbm, decay_ref, w_first_ref, w_second_ref, w_out_ref, m_first_ref, m_second_ref, m_out_ref,
    dft_high_ref, dft_low_ref, last_ref, first_ref,
    step_first_ref, step_second_ref, step_out_ref,
    u_buf, g_buf, in_sem,
    send1, recv1, ssem1, rsem1,
    mid, x_high, x_low, decay_rows, window,
    feats, wf, act_one, cos_one, act_two, cos_two,
    send2, recv2, ssem2, rsem2,
    go_send, go_recv, ssem3, rsem3,
    go_sum, go_all, ssem4, rsem4,
    pay, ar_send, ar_recv, ssem5, rsem5,
    ch_send, ch_recv, ssem6, rsem6,
    ag_send, ag_recv, ssem7, rsem7,
):
    me = lax.axis_index("dp")
    col = lax.axis_index("chan")

    def dp_peer(i):
        return lax.rem(me + i, DP)

    def ch_peer(i):
        return lax.rem(col + i, CHAN)

    def to_dp(src, dst, ssem, rsem, peer):
        return pltpu.make_async_remote_copy(
            src_ref=src, dst_ref=dst, send_sem=ssem, recv_sem=rsem, device_id=(peer, col), device_id_type=MESH
        )

    def to_ch(src, dst, ssem, rsem, peer):
        return pltpu.make_async_remote_copy(
            src_ref=src, dst_ref=dst, send_sem=ssem, recv_sem=rsem, device_id=(me, peer), device_id_type=MESH
        )

    def loop(low, high, body):
        def wrapped(i, carry):
            body(i)
            return carry

        lax.fori_loop(low, high, wrapped, 0)

    def in_copy(block, which):
        hbm, buf = ((u_hbm, u_buf), (g_hbm, g_buf))[which]
        lanes = pl.ds(block * 128, 128)
        return pltpu.make_async_copy(hbm.at[:, :, lanes], buf.at[:, :, lanes], in_sem.at[2 * block + which])

    for block in range(2):
        for which in range(2):
            in_copy(block, which).start()

    barrier = pltpu.get_barrier_semaphore()

    def greet_dp(i):
        pl.semaphore_signal(barrier, inc=1, device_id=(dp_peer(i), col), device_id_type=MESH)

    def greet_ch(i):
        pl.semaphore_signal(barrier, inc=1, device_id=(me, ch_peer(i)), device_id_type=MESH)

    loop(1, DP, greet_dp)
    loop(1, CHAN, greet_ch)

    for block in range(2):
        for which in range(2):
            in_copy(block, which).wait()

        def product(kt, block=block):
            rows = pl.ds(pl.multiple_of(kt * 128, 128), 128)
            lanes = pl.ds(block * 128, 128)
            u_re, u_im = u_buf[0, rows, lanes], u_buf[1, rows, lanes]
            g_re, g_im = g_buf[0, rows, lanes], g_buf[1, rows, lanes]
            re = g_re * u_re + g_im * u_im
            im = g_im * u_re - g_re * u_im
            owners = pl.ds(block * 16, 16)
            send1[owners, 0, :, rows] = re.T.reshape(16, 8, 128)
            send1[owners, 1, :, rows] = im.T.reshape(16, 8, 128)

        loop(0, ROWS // 128, product)
        if block == 0:
            pl.semaphore_wait(barrier, DP - 1 + CHAN - 1)

        def send(i, block=block):
            peer = block * 16 + lax.rem(me + i, 16)

            @pl.when(peer != me)
            def _():
                to_dp(send1.at[peer], recv1.at[me], ssem1.at[peer], rsem1.at[me], peer).start()

        loop(0, 16, send)
    recv1[me] = send1[me]

    decay_rows[...] = jnp.broadcast_to(decay_ref[...], (128, COLS)).T
    decay = decay_rows[pl.ds(pl.multiple_of(me * 8, 8), 8), :]
    lane = lax.broadcasted_iota(jnp.int32, (8, 128), 1)

    def make_window(v):
        t = lax.div(v, 8) + 16 * lax.rem(v, 8) + 128 * lane
        window[pl.ds(pl.multiple_of(v * 8, 8), 8), :] = jnp.exp(-t.astype(jnp.float32) / decay)

    loop(0, 128, make_window)

    column = lax.broadcasted_iota(jnp.int32, (16, 512), 1)
    position = lax.div(me, 2) + 16 * (4 * lax.rem(me, 2) + (column >> 7)) + 128 * (column & 127)
    band = lax.broadcasted_iota(jnp.int32, (16, 512), 0) + 1
    angle = 2.0 * math.pi / SEQ * ((band * position) & (SEQ - 1)).astype(jnp.float32)
    feats[...] = jnp.zeros_like(feats)
    feats[0:16, :] = jnp.cos(angle)
    feats[16:32, :] = jnp.sin(angle)
    feats[32:33, :] = position[0:1, :].astype(jnp.float32) / SEQ
    wf[...] = jnp.zeros_like(wf)
    wf[0:32, 0:HID] = w_first_ref[1:33, :]
    wf[32:33, 0:HID] = w_first_ref[0:1, :]
    pre_one = jnp.dot(wf[...].T[0:HID, :], feats[...], precision=HIGHEST, preferred_element_type=jnp.float32)
    act_one[...] = jnp.sin(pre_one)
    cos_one[...] = jnp.cos(pre_one)
    wf[0:HID, 0:HID] = w_second_ref[...]
    wf[HID:, :] = jnp.zeros((128 - HID, 128), jnp.float32)
    pre_two = jnp.dot(
        wf[...].T[0:HID, 0:HID], act_one[...], precision=HIGHEST, preferred_element_type=jnp.float32
    )
    act_two[...] = jnp.sin(pre_two)
    cos_two[...] = jnp.cos(pre_two)
    go_send[...] = jnp.zeros_like(go_send)
    pay[...] = jnp.zeros_like(pay)

    def arrived1(i):
        peer = dp_peer(i)
        to_dp(send1.at[peer], recv1.at[peer], ssem1.at[peer], rsem1.at[peer], peer).wait_recv()

    loop(1, DP, arrived1)

    def pass_one(n):
        q0, lt = lax.div(n, 2), lax.rem(n, 2)
        half, k1 = lax.div(q0, 4), lax.rem(q0, 4)
        lanes = pl.ds(pl.multiple_of(k1 * 256 + lt * 128, 128), 128)
        out_lanes = pl.ds(pl.multiple_of(lt * 128, 128), 128)
        values = dft([(recv1[2 * q + half, 0, :, lanes], recv1[2 * q + half, 1, :, lanes]) for q in range(16)])
        for v1 in range(16):
            re, im = values[v1]
            if v1 > 0:
                c, s = first_ref[q0 * 32 + 2 * v1], first_ref[q0 * 32 + 2 * v1 + 1]
                re, im = re * c - im * s, re * s + im * c
            mid[v1, q0, 0, :, out_lanes] = re
            mid[v1, q0, 1, :, out_lanes] = im

    loop(0, 16, pass_one)

    def pass_two(n):
        v1, lt = lax.div(n, 2), lax.rem(n, 2)
        lanes = pl.ds(pl.multiple_of(lt * 128, 128), 128)
        im_lanes = pl.ds(pl.multiple_of(256 + lt * 128, 128), 128)
        values = dft([(mid[v1, q0, 0, :, lanes], mid[v1, q0, 1, :, lanes]) for q0 in range(8)])
        turned = []
        for v2 in range(8):
            re, im = values[v2]
            c = last_ref[0, v1, v2 : v2 + 1, lanes]
            s = last_ref[1, v1, v2 : v2 + 1, lanes]
            turned.append((re * c - im * s, re * s + im * c))
        for pair in range(4):
            rows = pl.ds(pl.multiple_of(v1 * 64 + pair * 16, 16), 16)
            for part, where in ((0, lanes), (1, im_lanes)):
                x = jnp.concatenate([turned[2 * pair][part], turned[2 * pair + 1][part]], axis=0)
                high, low = split(x)
                x_high[rows, where] = high
                x_low[rows, where] = low

    loop(0, 32, pass_two)

    def out_block(n):
        rows = pl.ds(pl.multiple_of(n * 256, 256), 256)
        x = (x_high[rows, :], x_low[rows, :])
        y = dot3(x, (dft_high_ref[...], dft_low_ref[...]), NN) * window[rows, :]
        send2[pl.ds(n * 8, 8), :, :] = y.reshape(8, 32, 128)

        def send(i):
            peer = n * 8 + lax.rem(me + i, 8)

            @pl.when(peer != me)
            def _():
                to_dp(send2.at[peer], recv2.at[me], ssem2.at[peer], rsem2.at[me], peer).start()

        loop(0, 8, send)

    loop(0, 4, out_block)
    recv2[me] = send2[me]

    def arrived2(i):
        peer = dp_peer(i)
        to_dp(send2.at[peer], recv2.at[peer], ssem2.at[peer], rsem2.at[peer], peer).wait_recv()

    loop(1, DP, arrived2)

    out_grad = [split(recv2[:, 8 * j : 8 * j + 8, :].reshape(COLS, 128)) for j in range(4)]
    grad_out = jnp.zeros((COLS, HID), jnp.float32)
    for j in range(4):
        grad_out += dot3(out_grad[j], split(act_two[:, 128 * j : 128 * j + 128]), NT)
    go_send[:, :, 0:HID] = grad_out.reshape(DP, 8, HID)

    def send_go(i):
        peer = dp_peer(i)
        to_dp(go_send.at[peer], go_recv.at[me], ssem3.at[peer], rsem3.at[me], peer).start()

    loop(1, DP, send_go)
    go_recv[me] = go_send[me]

    w_out_parts = split(w_out_ref[...])
    w_second_parts = split(w_second_ref[...])
    grad_second = jnp.zeros((HID, HID), jnp.float32)
    grad_first = jnp.zeros((40, HID), jnp.float32)
    for j in range(4):
        cols = slice(128 * j, 128 * j + 128)
        hidden = dot3(w_out_parts, out_grad[j], NN)
        back_two = split(hidden * cos_two[:, cols])
        grad_second += dot3(split(act_one[:, cols]), back_two, NT)
        back_one = split(dot3(w_second_parts, back_two, NN) * cos_one[:, cols])
        grad_first += dot3(split(feats[0:40, cols]), back_one, NT)
    pay[0:32, :] = jnp.concatenate([grad_second[0:32], grad_second[32:64]], axis=1)
    pay[32:48, :] = jnp.concatenate([grad_first[0:16], grad_first[16:32]], axis=1)
    pay[48:49, 0:HID] = grad_first[32:33]

    def arrived_go(i):
        peer = dp_peer(i)
        to_dp(go_send.at[peer], go_recv.at[peer], ssem3.at[peer], rsem3.at[peer], peer).wait_recv()

    loop(1, DP, arrived_go)
    total_out = jnp.sum(go_recv[...], axis=0)
    go_sum[...] = total_out
    go_all[me] = total_out

    def send_go_all(i):
        peer = dp_peer(i)
        to_dp(go_sum, go_all.at[me], ssem4.at[peer], rsem4.at[me], peer).start()

    loop(1, DP, send_go_all)
    pay[49:50, :] = jnp.sum(total_out * total_out, axis=0, keepdims=True)

    for i in range(DP):
        ar_send[i] = pay[2 * i : 2 * i + 2, :]

    def send_ar(i):
        peer = dp_peer(i)
        to_dp(ar_send.at[peer], ar_recv.at[me], ssem5.at[peer], rsem5.at[me], peer).start()

    loop(1, DP, send_ar)
    ar_recv[me] = ar_send[me]

    def arrived_ar(i):
        peer = dp_peer(i)
        to_dp(ar_send.at[peer], ar_recv.at[peer], ssem5.at[peer], rsem5.at[peer], peer).wait_recv()

    loop(1, DP, arrived_ar)
    ch_send[...] = jnp.sum(ar_recv[...], axis=0)

    def send_ch(i):
        peer = ch_peer(i)
        to_ch(ch_send, ch_recv.at[col], ssem6.at[peer], rsem6.at[col], peer).start()

    loop(1, CHAN, send_ch)
    ch_recv[col] = ch_send[...]

    def arrived_ch(i):
        peer = ch_peer(i)
        to_ch(ch_send, ch_recv.at[peer], ssem6.at[peer], rsem6.at[peer], peer).wait_recv()

    loop(1, CHAN, arrived_ch)
    ag_send[...] = jnp.sum(ch_recv[...], axis=0)

    def send_ag(i):
        peer = dp_peer(i)
        to_dp(ag_send, ag_recv.at[me], ssem7.at[peer], rsem7.at[me], peer).start()

    loop(1, DP, send_ag)
    ag_recv[me] = ag_send[...]

    def arrived_go_all(i):
        peer = dp_peer(i)
        to_dp(go_sum, go_all.at[peer], ssem4.at[peer], rsem4.at[peer], peer).wait_recv()

    loop(1, DP, arrived_go_all)
    full_out = go_all[...].reshape(COLS, 128).T[0:HID, :]

    def arrived_ag(i):
        peer = dp_peer(i)
        to_dp(ag_send, ag_recv.at[peer], ssem7.at[peer], rsem7.at[peer], peer).wait_recv()

    loop(1, DP, arrived_ag)
    for i in range(DP):
        pay[2 * i : 2 * i + 2, :] = ag_recv[i]
    second = pay[0:32, :]
    first = pay[32:48, :]
    line = pay[48:49, 0:HID]
    total = (
        jnp.sum(second * second, keepdims=True)
        + jnp.sum(first * first, keepdims=True)
        + jnp.sum(line * line, keepdims=True)
        + jnp.sum(pay[49:50, :], keepdims=True)
    )
    scale = jnp.minimum(1.0, clip_norm / (jnp.sqrt(total) + 1e-06))
    step_out_ref[...] = adam_step(full_out, w_out_ref[...], m_out_ref[0], m_out_ref[1], scale)
    for part in range(2):
        rows, lanes = slice(32 * part, 32 * part + 32), slice(HID * part, HID * part + HID)
        step_second_ref[rows, :] = adam_step(
            second[:, lanes], w_second_ref[rows, :], m_second_ref[0, rows, :], m_second_ref[1, rows, :], scale
        )
        rows = slice(16 * part + 1, 16 * part + 17)
        step_first_ref[rows, :] = adam_step(
            first[:, lanes], w_first_ref[rows, :], m_first_ref[0, rows, :], m_first_ref[1, rows, :], scale
        )
    step_first_ref[0:1, :] = adam_step(
        line, w_first_ref[0:1, :], m_first_ref[0, 0:1, :], m_first_ref[1, 0:1, :], scale
    )

    def sent_dp(i):
        peer = dp_peer(i)
        to_dp(send1.at[peer], recv1.at[me], ssem1.at[peer], rsem1.at[me], peer).wait_send()
        to_dp(send2.at[peer], recv2.at[me], ssem2.at[peer], rsem2.at[me], peer).wait_send()
        to_dp(go_send.at[peer], go_recv.at[me], ssem3.at[peer], rsem3.at[me], peer).wait_send()
        to_dp(go_sum, go_all.at[me], ssem4.at[peer], rsem4.at[me], peer).wait_send()
        to_dp(ar_send.at[peer], ar_recv.at[me], ssem5.at[peer], rsem5.at[me], peer).wait_send()
        to_dp(ag_send, ag_recv.at[me], ssem7.at[peer], rsem7.at[me], peer).wait_send()

    loop(1, DP, sent_dp)

    def sent_ch(i):
        peer = ch_peer(i)
        to_ch(ch_send, ch_recv.at[col], ssem6.at[peer], rsem6.at[col], peer).wait_send()

    loop(1, CHAN, sent_ch)


def local(spec_u, spec_g, decay_length, w_first, w_second, w_out, moments_first, moments_second, moments_out):
    dft_high, dft_low, last, first = constants()
    f32, bf16 = jnp.float32, jnp.bfloat16
    vmem, sem = pltpu.VMEM, pltpu.SemaphoreType.DMA
    in_vmem = pl.BlockSpec(memory_space=pltpu.VMEM)
    anywhere = pl.BlockSpec(memory_space=pl.ANY)

    def pair(n):
        return [sem((n,)), sem((n,))]

    return pl.pallas_call(
        kernel,
        out_shape=(
            jax.ShapeDtypeStruct(w_first.shape, f32),
            jax.ShapeDtypeStruct(w_second.shape, f32),
            jax.ShapeDtypeStruct(w_out.shape, f32),
        ),
        in_specs=[anywhere] * 2 + [in_vmem] * 10 + [pl.BlockSpec(memory_space=pltpu.SMEM)],
        out_specs=(in_vmem,) * 3,
        scratch_shapes=[
            vmem((2, ROWS, COLS), f32), vmem((2, ROWS, COLS), f32), sem((4,)),
            vmem((DP, 2, 8, ROWS), f32), vmem((DP, 2, 8, ROWS), f32), *pair(DP),
            vmem((16, 8, 2, 8, 256), f32), vmem((1024, 512), bf16), vmem((1024, 512), bf16),
            vmem((COLS, 128), f32), vmem((1024, 128), f32),
            vmem((128, 512), f32), vmem((128, 128), f32),
            vmem((HID, 512), f32), vmem((HID, 512), f32), vmem((HID, 512), f32), vmem((HID, 512), f32),
            vmem((DP, 32, 128), f32), vmem((DP, 32, 128), f32), *pair(DP),
            vmem((DP, 8, 128), f32), vmem((DP, 8, 128), f32), *pair(DP),
            vmem((8, 128), f32), vmem((DP, 8, 128), f32), *pair(DP),
            vmem((64, 128), f32), vmem((DP, 2, 128), f32), vmem((DP, 2, 128), f32), *pair(DP),
            vmem((2, 128), f32), vmem((CHAN, 2, 128), f32), *pair(CHAN),
            vmem((2, 128), f32), vmem((DP, 2, 128), f32), *pair(DP),
        ],
        compiler_params=pltpu.CompilerParams(
            collective_id=0, has_side_effects=True, vmem_limit_bytes=40 * 1024 * 1024
        ),
        name="hyena_step",
    )(
        spec_u, spec_g, decay_length.reshape(1, COLS), w_first, w_second, w_out,
        moments_first, moments_second, moments_out,
        jnp.asarray(dft_high), jnp.asarray(dft_low), jnp.asarray(last), jnp.asarray(first),
    )


def solution(mesh):
    return jax.shard_map(
        local,
        mesh=mesh,
        in_specs=(
            P(None, "dp", "chan"),
            P(None, "dp", "chan"),
            P("chan"),
            P(),
            P(),
            P(None, "chan"),
            P(),
            P(),
            P(None, None, "chan"),
        ),
        out_specs=(P(), P(), P(None, "chan")),
        check_vma=False,
    )
```

```python
import functools
import math

import jax
import jax.numpy as jnp
import numpy as np
from jax import lax
from jax.experimental import pallas as pl
from jax.experimental.pallas import tpu as pltpu
from jax.sharding import PartitionSpec as P

MESH = pl.DeviceIdType.MESH
HIGHEST = lax.Precision.HIGHEST

BANDS = 16
HID = 64
DP = 32
CHAN = 16
FREQS = 32768
SEQ = 16384
ROWS = 1024
COLS = 256

beta_one = 0.9
beta_two = 0.999
adam_count = 10.0
adam_eps = 1e-08
weight_decay = 0.1
clip_norm = 1.0


def adam_step(grad, weight, first, second, scale):
    g = grad * scale
    first = beta_one * first + (1.0 - beta_one) * g
    second = beta_two * second + (1.0 - beta_two) * g * g
    first_hat = first / (1.0 - beta_one**adam_count)
    second_hat = second / (1.0 - beta_two**adam_count)
    return first_hat / (jnp.sqrt(second_hat) + adam_eps) + weight_decay * weight


def split(x):
    high = x.astype(jnp.bfloat16)
    low = (x - high.astype(jnp.float32)).astype(jnp.bfloat16)
    return high, low


def dot3(a, b, dims):
    def one(x, y):
        return lax.dot_general(x, y, (dims, ((), ())), preferred_element_type=jnp.float32)

    return one(a[0], b[0]) + one(a[0], b[1]) + one(a[1], b[0])


NN = ((1,), (0,))
NT = ((1,), (1,))


def times(z, angle_num, angle_den):
    re, im = z
    k = angle_num % angle_den
    if k == 0:
        return re, im
    if 4 * k == angle_den:
        return -im, re
    if 2 * k == angle_den:
        return -re, -im
    if 4 * k == 3 * angle_den:
        return im, -re
    if 8 * k == angle_den:
        r = math.sqrt(0.5)
        return (re - im) * r, (re + im) * r
    if 8 * k == 3 * angle_den:
        r = math.sqrt(0.5)
        return (re + im) * (-r), (re - im) * r
    c, s = math.cos(2 * math.pi * k / angle_den), math.sin(2 * math.pi * k / angle_den)
    return re * c - im * s, re * s + im * c


def dft(values):
    n = len(values)
    if n == 1:
        return values
    even, odd = dft(values[0::2]), dft(values[1::2])
    low, high = [], []
    for k in range(n // 2):
        t = times(odd[k], k, n)
        low.append((even[k][0] + t[0], even[k][1] + t[1]))
        high.append((even[k][0] - t[0], even[k][1] - t[1]))
    return low + high


def constants():
    lane = np.arange(256)[:, None] * np.arange(128)[None, :] % 256
    angle = 2.0 * np.pi / 256 * lane
    table = np.concatenate([np.cos(angle), -np.sin(angle)], axis=0).astype(np.float32)
    high = table.astype(jnp.bfloat16)
    low = (table - high.astype(np.float32)).astype(jnp.bfloat16)
    v = np.arange(16)[:, None] + 16 * np.arange(8)[None, :]
    angle = 2.0 * np.pi / FREQS * (v[:, :, None] * np.arange(256)[None, None, :])
    last = (np.stack([np.cos(angle), np.sin(angle)]) / FREQS).astype(np.float32)
    angle = 2.0 * np.pi / 128 * (np.arange(8)[:, None] * np.arange(16)[None, :])
    first = np.stack([np.cos(angle), np.sin(angle)], axis=-1).astype(np.float32)
    return high, low, last, first.reshape(-1)


def kernel(
    u_hbm, g_hbm, decay_hbm, w_first_hbm, w_second_hbm, w_out_hbm, m_first_hbm, m_second_hbm, m_out_hbm,
    dft_high_hbm, dft_low_hbm, last_hbm, first_hbm,
    step_first_ref, step_second_ref, step_out_ref,
    u_buf, g_buf, in_sem,
    decay_ref, w_first_ref, w_second_ref, w_out_ref, m_first_ref, m_second_ref, m_out_ref,
    dft_high_ref, dft_low_ref, last_ref, first_ref, small_sem,
    send1, recv1, ssem1, rsem1,
    mid, x_high, x_low, decay_rows, window,
    feats, wf, act_one, cos_one, act_two, cos_two,
    send2, recv2, ssem2, rsem2,
    go_send, go_recv, ssem3, rsem3,
    go_sum, go_all, ssem4, rsem4,
    pay, ar_send, ar_recv, ssem5, rsem5,
    ch_send, ch_recv, ssem6, rsem6,
    ag_send, ag_recv, ssem7, rsem7,
):
    me = lax.axis_index("dp")
    col = lax.axis_index("chan")

    def dp_peer(i):
        return lax.rem(me + i, DP)

    def ch_peer(i):
        return lax.rem(col + i, CHAN)

    def chunk_of(device):
        return lax.rem(device, 2) * 16 + lax.div(device, 2)

    def places_of(device):
        return lax.rem(device, 4) * 8 + lax.div(device, 4)

    mine = chunk_of(me)

    def to_dp(src, dst, ssem, rsem, peer):
        return pltpu.make_async_remote_copy(
            src_ref=src, dst_ref=dst, send_sem=ssem, recv_sem=rsem, device_id=(peer, col), device_id_type=MESH
        )

    def to_ch(src, dst, ssem, rsem, peer):
        return pltpu.make_async_remote_copy(
            src_ref=src, dst_ref=dst, send_sem=ssem, recv_sem=rsem, device_id=(me, peer), device_id_type=MESH
        )

    def loop(low, high, body):
        def wrapped(i, carry):
            body(i)
            return carry

        lax.fori_loop(low, high, wrapped, 0)

    def sent(phases):
        def sent_dp(i):
            peer = dp_peer(i)
            copies = [
                (send1.at[peer], recv1, ssem1, rsem1), (send2.at[peer], recv2, ssem2, rsem2),
                (go_send.at[peer], go_recv, ssem3, rsem3), (go_sum, go_all, ssem4, rsem4),
                (ar_send.at[peer], ar_recv, ssem5, rsem5), (ag_send, ag_recv, ssem7, rsem7),
            ]
            for src, dst, ssem, rsem in copies[: min(phases, 6)]:
                to_dp(src, dst.at[me], ssem.at[peer], rsem.at[me], peer).wait_send()

        loop(1, DP, sent_dp)

        def sent_ch(i):
            peer = ch_peer(i)
            to_ch(ch_send, ch_recv.at[col], ssem6.at[peer], rsem6.at[col], peer).wait_send()

        loop(1, CHAN, sent_ch)

    def in_copy(block, which):
        hbm, buf = ((u_hbm, u_buf), (g_hbm, g_buf))[which]
        lanes = pl.ds(block * 128, 128)
        return pltpu.make_async_copy(hbm.at[:, :, lanes], buf.at[:, :, lanes], in_sem.at[2 * block + which])

    for block in range(2):
        for which in range(2):
            in_copy(block, which).start()

    small = [
        pltpu.make_async_copy(src, dst, small_sem.at[n])
        for n, (src, dst) in enumerate((
            (decay_hbm, decay_ref), (w_first_hbm, w_first_ref), (w_second_hbm, w_second_ref),
            (w_out_hbm, w_out_ref), (m_first_hbm, m_first_ref), (m_second_hbm, m_second_ref),
            (m_out_hbm, m_out_ref), (dft_high_hbm, dft_high_ref), (dft_low_hbm, dft_low_ref),
            (last_hbm, last_ref), (first_hbm, first_ref),
        ))
    ]

    barrier = pltpu.get_barrier_semaphore()

    def greet_dp(i):
        pl.semaphore_signal(barrier, inc=1, device_id=(dp_peer(i), col), device_id_type=MESH)

    def greet_ch(i):
        pl.semaphore_signal(barrier, inc=1, device_id=(me, ch_peer(i)), device_id_type=MESH)

    loop(1, DP, greet_dp)
    loop(1, CHAN, greet_ch)

    for block in range(2):
        for which in range(2):
            in_copy(block, which).wait()

        def product(kt, block=block):
            rows = pl.ds(pl.multiple_of(kt * 128, 128), 128)
            lanes = pl.ds(block * 128, 128)
            u_re, u_im = u_buf[0, rows, lanes], u_buf[1, rows, lanes]
            g_re, g_im = g_buf[0, rows, lanes], g_buf[1, rows, lanes]
            re = g_re * u_re + g_im * u_im
            im = g_im * u_re - g_re * u_im
            owners = pl.ds(block * 16, 16)
            send1[owners, 0, :, rows] = re.T.reshape(16, 8, 128)
            send1[owners, 1, :, rows] = im.T.reshape(16, 8, 128)

        loop(0, ROWS // 128, product)
        if block == 0:
            pl.semaphore_wait(barrier, DP - 1 + CHAN - 1)

        def send(i, block=block):
            n = lax.rem(lax.div(me, 2) + i, 16)
            peer = 2 * n + block

            @pl.when(peer != me)
            def _():
                to_dp(send1.at[block * 16 + n], recv1.at[me], ssem1.at[peer], rsem1.at[me], peer).start()

        loop(0, 16, send)
    for copy in small:
        copy.start()
    recv1[me] = send1[mine]
    for copy in small:
        copy.wait()

    decay_rows[...] = jnp.broadcast_to(decay_ref[...], (128, COLS)).T
    decay = decay_rows[pl.ds(pl.multiple_of(mine * 8, 8), 8), :]
    lane = lax.broadcasted_iota(jnp.int32, (8, 128), 1)

    def make_window(v):
        t = lax.div(v, 8) + 16 * lax.rem(v, 8) + 128 * lane
        window[pl.ds(pl.multiple_of(v * 8, 8), 8), :] = jnp.exp(-t.astype(jnp.float32) / decay)

    loop(0, 128, make_window)

    column = lax.broadcasted_iota(jnp.int32, (16, 512), 1)
    place = places_of(me)
    position = lax.div(place, 2) + 16 * (4 * lax.rem(place, 2) + (column >> 7)) + 128 * (column & 127)
    band = lax.broadcasted_iota(jnp.int32, (16, 512), 0) + 1
    angle = 2.0 * math.pi / SEQ * ((band * position) & (SEQ - 1)).astype(jnp.float32)
    feats[...] = jnp.zeros_like(feats)
    feats[0:16, :] = jnp.cos(angle)
    feats[16:32, :] = jnp.sin(angle)
    feats[32:33, :] = position[0:1, :].astype(jnp.float32) / SEQ
    wf[...] = jnp.zeros_like(wf)
    wf[0:32, 0:HID] = w_first_ref[1:33, :]
    wf[32:33, 0:HID] = w_first_ref[0:1, :]
    pre_one = jnp.dot(wf[...].T[0:HID, :], feats[...], precision=HIGHEST, preferred_element_type=jnp.float32)
    act_one[...] = jnp.sin(pre_one)
    cos_one[...] = jnp.cos(pre_one)
    wf[0:HID, 0:HID] = w_second_ref[...]
    wf[HID:, :] = jnp.zeros((128 - HID, 128), jnp.float32)
    pre_two = jnp.dot(
        wf[...].T[0:HID, 0:HID], act_one[...], precision=HIGHEST, preferred_element_type=jnp.float32
    )
    act_two[...] = jnp.sin(pre_two)
    cos_two[...] = jnp.cos(pre_two)
    go_send[...] = jnp.zeros_like(go_send)
    pay[...] = jnp.zeros_like(pay)
    ch_send[...] = jnp.zeros_like(ch_send)

    def arrived1(i):
        peer = dp_peer(i)
        to_dp(send1.at[peer], recv1.at[peer], ssem1.at[peer], rsem1.at[peer], peer).wait_recv()

    loop(1, DP, arrived1)

    def pass_one(n):
        q0, lt = lax.div(n, 2), lax.rem(n, 2)
        half, k1 = lax.div(q0, 4), lax.rem(q0, 4)
        lanes = pl.ds(pl.multiple_of(k1 * 256 + lt * 128, 128), 128)
        out_lanes = pl.ds(pl.multiple_of(lt * 128, 128), 128)
        values = dft([(recv1[2 * q + half, 0, :, lanes], recv1[2 * q + half, 1, :, lanes]) for q in range(16)])
        for v1 in range(16):
            re, im = values[v1]
            if v1 > 0:
                c, s = first_ref[q0 * 32 + 2 * v1], first_ref[q0 * 32 + 2 * v1 + 1]
                re, im = re * c - im * s, re * s + im * c
            mid[v1, q0, 0, :, out_lanes] = re
            mid[v1, q0, 1, :, out_lanes] = im

    loop(0, 16, pass_one)

    def pass_two(n):
        v1, lt = lax.div(n, 2), lax.rem(n, 2)
        lanes = pl.ds(pl.multiple_of(lt * 128, 128), 128)
        im_lanes = pl.ds(pl.multiple_of(256 + lt * 128, 128), 128)
        values = dft([(mid[v1, q0, 0, :, lanes], mid[v1, q0, 1, :, lanes]) for q0 in range(8)])
        turned = []
        for v2 in range(8):
            re, im = values[v2]
            c = last_ref[0, v1, v2 : v2 + 1, lanes]
            s = last_ref[1, v1, v2 : v2 + 1, lanes]
            turned.append((re * c - im * s, re * s + im * c))
        for pair in range(4):
            rows = pl.ds(pl.multiple_of(v1 * 64 + pair * 16, 16), 16)
            for part, where in ((0, lanes), (1, im_lanes)):
                x = jnp.concatenate([turned[2 * pair][part], turned[2 * pair + 1][part]], axis=0)
                high, low = split(x)
                x_high[rows, where] = high
                x_low[rows, where] = low

    loop(0, 32, pass_two)

    def out_block(n):
        rows = pl.ds(pl.multiple_of(n * 256, 256), 256)
        x = (x_high[rows, :], x_low[rows, :])
        y = dot3(x, (dft_high_ref[...], dft_low_ref[...]), NN) * window[rows, :]
        send2[pl.ds(n * 8, 8), :, :] = y.reshape(8, 32, 128)

        def send(i):
            z = lax.rem(lax.div(me, 4) + i, 8)
            peer = 4 * z + n

            @pl.when(peer != me)
            def _():
                to_dp(send2.at[n * 8 + z], recv2.at[mine], ssem2.at[peer], rsem2.at[me], peer).start()

        loop(0, 8, send)

    loop(0, 4, out_block)
    recv2[mine] = send2[places_of(me)]

    def arrived2(i):
        peer = dp_peer(i)
        to_dp(send2.at[peer], recv2.at[peer], ssem2.at[peer], rsem2.at[peer], peer).wait_recv()

    loop(1, DP, arrived2)

    out_grad = [split(recv2[:, 8 * j : 8 * j + 8, :].reshape(COLS, 128)) for j in range(4)]
    grad_out = jnp.zeros((COLS, HID), jnp.float32)
    for j in range(4):
        grad_out += dot3(out_grad[j], split(act_two[:, 128 * j : 128 * j + 128]), NT)
    go_send[:, :, 0:HID] = grad_out.reshape(DP, 8, HID)

    def send_go(i):
        peer = dp_peer(i)
        to_dp(go_send.at[chunk_of(peer)], go_recv.at[me], ssem3.at[peer], rsem3.at[me], peer).start()

    loop(1, DP, send_go)
    go_recv[me] = go_send[mine]

    w_out_parts = split(w_out_ref[...])
    w_second_parts = split(w_second_ref[...])
    grad_second = jnp.zeros((HID, HID), jnp.float32)
    grad_first = jnp.zeros((40, HID), jnp.float32)
    for j in range(4):
        cols = slice(128 * j, 128 * j + 128)
        hidden = dot3(w_out_parts, out_grad[j], NN)
        back_two = split(hidden * cos_two[:, cols])
        grad_second += dot3(split(act_one[:, cols]), back_two, NT)
        back_one = split(dot3(w_second_parts, back_two, NN) * cos_one[:, cols])
        grad_first += dot3(split(feats[0:40, cols]), back_one, NT)
    pay[0:32, :] = jnp.concatenate([grad_second[0:32], grad_second[32:64]], axis=1)
    pay[32:48, :] = jnp.concatenate([grad_first[0:16], grad_first[16:32]], axis=1)
    pay[48:49, 0:HID] = grad_first[32:33]

    for i in range(DP):
        ar_send[i] = pay[2 * i : 2 * i + 2, :]

    def send_ar(i):
        peer = dp_peer(i)
        to_dp(ar_send.at[peer], ar_recv.at[me], ssem5.at[peer], rsem5.at[me], peer).start()

    loop(1, DP, send_ar)
    ar_recv[me] = ar_send[me]

    def arrived_go(i):
        peer = dp_peer(i)
        to_dp(go_send.at[peer], go_recv.at[peer], ssem3.at[peer], rsem3.at[peer], peer).wait_recv()

    loop(1, DP, arrived_go)
    total_out = jnp.sum(go_recv[...], axis=0)
    go_sum[...] = total_out
    go_all[mine] = total_out

    def send_go_all(i):
        peer = dp_peer(i)
        to_dp(go_sum, go_all.at[mine], ssem4.at[peer], rsem4.at[me], peer).start()

    loop(1, DP, send_go_all)
    ch_send[2:3, :] = jnp.sum(total_out * total_out, axis=0, keepdims=True)

    def arrived_ar(i):
        peer = dp_peer(i)
        to_dp(ar_send.at[peer], ar_recv.at[peer], ssem5.at[peer], rsem5.at[peer], peer).wait_recv()

    loop(1, DP, arrived_ar)
    ch_send[0:2, :] = jnp.sum(ar_recv[...], axis=0)

    def send_ch(i):
        peer = ch_peer(i)
        to_ch(ch_send, ch_recv.at[col], ssem6.at[peer], rsem6.at[col], peer).start()

    loop(1, CHAN, send_ch)
    ch_recv[col] = ch_send[...]

    def arrived_ch(i):
        peer = ch_peer(i)
        to_ch(ch_send, ch_recv.at[peer], ssem6.at[peer], rsem6.at[peer], peer).wait_recv()

    loop(1, CHAN, arrived_ch)
    ag_send[...] = jnp.sum(ch_recv[...], axis=0)

    def send_ag(i):
        peer = dp_peer(i)
        to_dp(ag_send, ag_recv.at[me], ssem7.at[peer], rsem7.at[me], peer).start()

    loop(1, DP, send_ag)
    ag_recv[me] = ag_send[...]

    def arrived_go_all(i):
        peer = dp_peer(i)
        to_dp(go_sum, go_all.at[peer], ssem4.at[peer], rsem4.at[peer], peer).wait_recv()

    loop(1, DP, arrived_go_all)
    full_out = go_all[...].reshape(COLS, 128).T[0:HID, :]

    def arrived_ag(i):
        peer = dp_peer(i)
        to_dp(ag_send, ag_recv.at[peer], ssem7.at[peer], rsem7.at[peer], peer).wait_recv()

    loop(1, DP, arrived_ag)
    for i in range(DP):
        pay[2 * i : 2 * i + 2, :] = ag_recv[i, 0:2, :]
    second = pay[0:32, :]
    first = pay[32:48, :]
    line = pay[48:49, 0:HID]
    total = (
        jnp.sum(second * second, keepdims=True)
        + jnp.sum(first * first, keepdims=True)
        + jnp.sum(line * line, keepdims=True)
        + jnp.sum(jnp.sum(ag_recv[:, 2:3, :], axis=0), keepdims=True)
    )
    scale = jnp.minimum(1.0, clip_norm / (jnp.sqrt(total) + 1e-06))
    step_out_ref[...] = adam_step(full_out, w_out_ref[...], m_out_ref[0], m_out_ref[1], scale)
    for part in range(2):
        rows, lanes = slice(32 * part, 32 * part + 32), slice(HID * part, HID * part + HID)
        step_second_ref[rows, :] = adam_step(
            second[:, lanes], w_second_ref[rows, :], m_second_ref[0, rows, :], m_second_ref[1, rows, :], scale
        )
        rows = slice(16 * part + 1, 16 * part + 17)
        step_first_ref[rows, :] = adam_step(
            first[:, lanes], w_first_ref[rows, :], m_first_ref[rows, 0, :], m_first_ref[rows, 1, :], scale
        )
    step_first_ref[0:1, :] = adam_step(
        line, w_first_ref[0:1, :], m_first_ref[0:1, 0, :], m_first_ref[0:1, 1, :], scale
    )

    sent(7)


def local(spec_u, spec_g, decay_length, w_first, w_second, w_out, moments_first, moments_second, moments_out):
    dft_high, dft_low, last, first = constants()
    f32, bf16 = jnp.float32, jnp.bfloat16
    vmem, sem = pltpu.VMEM, pltpu.SemaphoreType.DMA
    in_vmem = pl.BlockSpec(memory_space=pltpu.VMEM)
    anywhere = pl.BlockSpec(memory_space=pl.ANY)

    def pair(n):
        return [sem((n,)), sem((n,))]

    return pl.pallas_call(
        kernel,
        out_shape=(
            jax.ShapeDtypeStruct(w_first.shape, f32),
            jax.ShapeDtypeStruct(w_second.shape, f32),
            jax.ShapeDtypeStruct(w_out.shape, f32),
        ),
        in_specs=[anywhere] * 13,
        out_specs=(in_vmem,) * 3,
        scratch_shapes=[
            vmem((2, ROWS, COLS), f32), vmem((2, ROWS, COLS), f32), sem((4,)),
            vmem((1, COLS), f32), vmem((33, HID), f32), vmem((HID, HID), f32), vmem((HID, COLS), f32),
            vmem((33, 2, HID), f32), vmem((2, HID, HID), f32), vmem((2, HID, COLS), f32),
            vmem((512, 128), bf16), vmem((512, 128), bf16), vmem((2, 16, 8, 256), f32),
            pltpu.SMEM((256,), f32), sem((11,)),
            vmem((DP, 2, 8, ROWS), f32), vmem((DP, 2, 8, ROWS), f32), *pair(DP),
            vmem((16, 8, 2, 8, 256), f32), vmem((1024, 512), bf16), vmem((1024, 512), bf16),
            vmem((COLS, 128), f32), vmem((1024, 128), f32),
            vmem((128, 512), f32), vmem((128, 128), f32),
            vmem((HID, 512), f32), vmem((HID, 512), f32), vmem((HID, 512), f32), vmem((HID, 512), f32),
            vmem((DP, 32, 128), f32), vmem((DP, 32, 128), f32), *pair(DP),
            vmem((DP, 8, 128), f32), vmem((DP, 8, 128), f32), *pair(DP),
            vmem((8, 128), f32), vmem((DP, 8, 128), f32), *pair(DP),
            vmem((64, 128), f32), vmem((DP, 2, 128), f32), vmem((DP, 2, 128), f32), *pair(DP),
            vmem((4, 128), f32), vmem((CHAN, 4, 128), f32), *pair(CHAN),
            vmem((4, 128), f32), vmem((DP, 4, 128), f32), *pair(DP),
        ],
        compiler_params=pltpu.CompilerParams(
            collective_id=0, has_side_effects=True, vmem_limit_bytes=56 * 1024 * 1024
        ),
        name="hyena_step",
    )(
        spec_u, spec_g, decay_length.reshape(1, COLS), w_first, w_second, w_out,
        jnp.swapaxes(moments_first, 0, 1), moments_second, moments_out,
        jnp.asarray(dft_high), jnp.asarray(dft_low), jnp.asarray(last), jnp.asarray(first),
    )


def solution(mesh):
    return jax.shard_map(
        local,
        mesh=mesh,
        in_specs=(
            P(None, "dp", "chan"),
            P(None, "dp", "chan"),
            P("chan"),
            P(),
            P(),
            P(None, "chan"),
            P(),
            P(),
            P(None, None, "chan"),
        ),
        out_specs=(P(), P(), P(None, "chan")),
        check_vma=False,
    )
```

```python
import functools
import math

import jax
import jax.numpy as jnp
import numpy as np
from jax import lax
from jax.experimental import pallas as pl
from jax.experimental.pallas import tpu as pltpu
from jax.sharding import PartitionSpec as P

MESH = pl.DeviceIdType.MESH
HIGHEST = lax.Precision.HIGHEST

BANDS = 16
HID = 64
DP = 32
CHAN = 16
FREQS = 32768
SEQ = 16384
ROWS = 1024
COLS = 256

beta_one = 0.9
beta_two = 0.999
adam_count = 10.0
adam_eps = 1e-08
weight_decay = 0.1
clip_norm = 1.0


def adam_step(grad, weight, first, second, scale):
    g = grad * scale
    first = beta_one * first + (1.0 - beta_one) * g
    second = beta_two * second + (1.0 - beta_two) * g * g
    first_hat = first / (1.0 - beta_one**adam_count)
    second_hat = second / (1.0 - beta_two**adam_count)
    return first_hat / (jnp.sqrt(second_hat) + adam_eps) + weight_decay * weight


def split(x):
    high = x.astype(jnp.bfloat16)
    low = (x - high.astype(jnp.float32)).astype(jnp.bfloat16)
    return high, low


def dot(a, b, dims):
    return lax.dot_general(a, b, (dims, ((), ())), preferred_element_type=jnp.float32)


def stacked(x):
    return jnp.concatenate(split(x), axis=0)


def folded(x, rows):
    x = x[:rows] + x[rows:]
    return x[:, :HID] + x[:, HID:]


def three_rows(x):
    high, low = split(x)
    return jnp.concatenate([high, low, high], axis=0)


def three_lanes(x):
    high, low = split(x)
    return jnp.concatenate([high, high, low], axis=1)


def sine_cosine(x):
    turns = jnp.floor(x * (2.0 / math.pi) + 0.5)
    r = ((x - turns * 1.5703125) - turns * 4.837512969970703125e-4) - turns * 7.54978995489188216e-8
    z = r * r
    sine = r + r * z * (-1.6666654611e-1 + z * (8.3321608736e-3 - z * 1.9515295891e-4))
    cosine = 1.0 - 0.5 * z + z * z * (4.166664568298827e-2 + z * (-1.388731625493765e-3 + z * 2.443315711809948e-5))
    quarter = turns.astype(jnp.int32)
    odd = (quarter & 1) == 1
    first, second = jnp.where(odd, cosine, sine), jnp.where(odd, sine, cosine)
    return jnp.where((quarter & 2) == 2, -first, first), jnp.where(((quarter + 1) & 2) == 2, -second, second)


NN = ((1,), (0,))
NT = ((1,), (1,))


def times(z, angle_num, angle_den):
    re, im = z
    k = angle_num % angle_den
    if k == 0:
        return re, im
    if 4 * k == angle_den:
        return -im, re
    if 2 * k == angle_den:
        return -re, -im
    if 4 * k == 3 * angle_den:
        return im, -re
    if 8 * k == angle_den:
        r = math.sqrt(0.5)
        return (re - im) * r, (re + im) * r
    if 8 * k == 3 * angle_den:
        r = math.sqrt(0.5)
        return (re + im) * (-r), (re - im) * r
    c, s = math.cos(2 * math.pi * k / angle_den), math.sin(2 * math.pi * k / angle_den)
    return re * c - im * s, re * s + im * c


def dft(values):
    n = len(values)
    if n == 1:
        return values
    even, odd = dft(values[0::2]), dft(values[1::2])
    low, high = [], []
    for k in range(n // 2):
        t = times(odd[k], k, n)
        low.append((even[k][0] + t[0], even[k][1] + t[1]))
        high.append((even[k][0] - t[0], even[k][1] - t[1]))
    return low + high


def constants():
    lane = np.arange(256)[:, None] * np.arange(128)[None, :] % 256
    angle = 2.0 * np.pi / 256 * lane
    table = np.concatenate([np.cos(angle), -np.sin(angle)], axis=0).astype(np.float32)
    high = table.astype(jnp.bfloat16)
    low = (table - high.astype(np.float32)).astype(jnp.bfloat16)
    v = np.arange(16)[:, None] + 16 * np.arange(8)[None, :]
    angle = 2.0 * np.pi / FREQS * (v[:, :, None] * np.arange(256)[None, None, :])
    last = (np.stack([np.cos(angle), np.sin(angle)]) / FREQS).astype(np.float32)
    angle = 2.0 * np.pi / 128 * (np.arange(8)[:, None] * np.arange(16)[None, :])
    first = np.stack([np.cos(angle), np.sin(angle)], axis=-1).astype(np.float32)
    return high, low, last, first.reshape(-1)


def kernel(
    u_hbm, g_hbm, decay_hbm, w_first_hbm, w_second_hbm, w_out_hbm, m_first_hbm, m_second_hbm, m_out_hbm,
    dft_high_hbm, dft_low_hbm, last_hbm, first_hbm,
    step_first_ref, step_second_ref, step_out_ref,
    u_buf, g_buf, in_sem,
    decay_ref, w_first_ref, w_second_ref, w_out_ref, m_first_ref, m_second_ref, m_out_ref,
    dft_high_ref, dft_low_ref, last_ref, first_ref, small_sem,
    send1, recv1, ssem1, rsem1,
    mid, x_high, x_low, decay_rows, window,
    wf, w_rows, w_out_parts, w_second_parts, feats, act_one, cos_one, act_two, cos_two,
    send2, recv2, ssem2, rsem2,
    go_send, go_recv, ssem3, rsem3,
    go_sum, go_all, ssem4, rsem4,
    pay, ar_send, ar_recv, ssem5, rsem5,
    ch_send, ch_recv, ssem6, rsem6,
    ag_send, ag_recv, ssem7, rsem7,
):
    me = lax.axis_index("dp")
    col = lax.axis_index("chan")

    def dp_peer(i):
        return lax.rem(me + i, DP)

    def ch_peer(i):
        return lax.rem(col + i, CHAN)

    def chunk_of(device):
        return lax.rem(device, 2) * 16 + lax.div(device, 2)

    mine = chunk_of(me)
    z, x = lax.div(me, 4), lax.rem(me, 4)

    def to_dp(src, dst, ssem, rsem, peer):
        return pltpu.make_async_remote_copy(
            src_ref=src, dst_ref=dst, send_sem=ssem, recv_sem=rsem, device_id=(peer, col), device_id_type=MESH
        )

    def to_ch(src, dst, ssem, rsem, peer):
        return pltpu.make_async_remote_copy(
            src_ref=src, dst_ref=dst, send_sem=ssem, recv_sem=rsem, device_id=(me, peer), device_id_type=MESH
        )

    def loop(low, high, body):
        def wrapped(i, carry):
            body(i)
            return carry

        lax.fori_loop(low, high, wrapped, 0)

    def sent():
        def sent_dp(i):
            peer = dp_peer(i)
            copies = [
                (send1.at[peer], recv1, ssem1, rsem1), (go_sum, go_all, ssem4, rsem4),
                (ar_send.at[peer], ar_recv, ssem5, rsem5), (ag_send, ag_recv, ssem7, rsem7),
            ]
            for src, dst, ssem, rsem in copies:
                to_dp(src, dst.at[me], ssem.at[peer], rsem.at[me], peer).wait_send()

        loop(1, DP, sent_dp)

        def sent_x(i):
            n = lax.rem(x + i, 4)
            to_dp(send2.at[n], recv2.at[x], ssem2.at[n], rsem2.at[x], 4 * z + n).wait_send()
            to_dp(go_send.at[n], go_recv.at[x], ssem3.at[n], rsem3.at[x], 4 * z + n).wait_send()

        loop(1, 4, sent_x)

        def sent_ch(i):
            peer = ch_peer(i)
            to_ch(ch_send, ch_recv.at[col], ssem6.at[peer], rsem6.at[col], peer).wait_send()

        loop(1, CHAN, sent_ch)

    def in_copy(block, which):
        hbm, buf = ((u_hbm, u_buf), (g_hbm, g_buf))[which]
        lanes = pl.ds(block * 128, 128)
        return pltpu.make_async_copy(hbm.at[:, :, lanes], buf.at[:, :, lanes], in_sem.at[2 * block + which])

    for block in range(2):
        for which in range(2):
            in_copy(block, which).start()

    small = [
        pltpu.make_async_copy(src, dst, small_sem.at[n])
        for n, (src, dst) in enumerate((
            (decay_hbm, decay_ref), (w_first_hbm, w_first_ref), (w_second_hbm, w_second_ref),
            (w_out_hbm, w_out_ref), (m_first_hbm, m_first_ref), (m_second_hbm, m_second_ref),
            (m_out_hbm, m_out_ref), (dft_high_hbm, dft_high_ref), (dft_low_hbm, dft_low_ref),
            (last_hbm, last_ref), (first_hbm, first_ref),
        ))
    ]

    barrier = pltpu.get_barrier_semaphore()

    def greet_dp(i):
        pl.semaphore_signal(barrier, inc=1, device_id=(dp_peer(i), col), device_id_type=MESH)

    def greet_ch(i):
        pl.semaphore_signal(barrier, inc=1, device_id=(me, ch_peer(i)), device_id_type=MESH)

    loop(1, DP, greet_dp)
    loop(1, CHAN, greet_ch)

    for block in range(2):
        for which in range(2):
            in_copy(block, which).wait()

        def product(kt, block=block):
            rows = pl.ds(pl.multiple_of(kt * 128, 128), 128)
            lanes = pl.ds(block * 128, 128)
            u_re, u_im = u_buf[0, rows, lanes], u_buf[1, rows, lanes]
            g_re, g_im = g_buf[0, rows, lanes], g_buf[1, rows, lanes]
            re = g_re * u_re + g_im * u_im
            im = g_im * u_re - g_re * u_im
            owners = pl.ds(block * 16, 16)
            send1[owners, 0, :, rows] = re.T.reshape(16, 8, 128)
            send1[owners, 1, :, rows] = im.T.reshape(16, 8, 128)

        loop(0, ROWS // 128, product)
        if block == 0:
            pl.semaphore_wait(barrier, DP - 1 + CHAN - 1)

        def send(i, block=block):
            n = lax.rem(lax.div(me, 2) + i, 16)
            peer = 2 * n + block

            @pl.when(peer != me)
            def _():
                to_dp(send1.at[block * 16 + n], recv1.at[me], ssem1.at[peer], rsem1.at[me], peer).start()

        loop(0, 16, send)
    for copy in small:
        copy.start()
    recv1[me] = send1[mine]
    for copy in small:
        copy.wait()

    decay_rows[...] = jnp.broadcast_to(decay_ref[...], (128, COLS)).T
    decay = decay_rows[pl.ds(pl.multiple_of(mine * 8, 8), 8), :]
    lane = lax.broadcasted_iota(jnp.int32, (8, 128), 1)

    def make_window(v):
        t = lax.div(v, 8) + 16 * lax.rem(v, 8) + 128 * lane
        window[pl.ds(pl.multiple_of(v * 8, 8), 8), :] = jnp.exp(-t.astype(jnp.float32) / decay)

    loop(0, 128, make_window)

    w_rows[:, 0:HID] = w_out_ref[...].T
    w_rows[:, HID:] = jnp.zeros((COLS, 128 - HID), jnp.float32)
    met = [w_rows[pl.ds(pl.multiple_of(chunk_of(4 * z + n) * 8, 8), 8), :] for n in range(4)]
    met = jnp.concatenate(met + [jnp.zeros((96, 128), jnp.float32)], axis=0).T
    w_out_parts[...] = three_lanes(met[0:HID, 0:32])
    w_second_parts[...] = three_lanes(w_second_ref[...])

    wf[...] = jnp.zeros_like(wf)
    wf[0:32, 0:HID] = w_first_ref[1:33, :]
    wf[32:33, 0:HID] = w_first_ref[0:1, :]
    wf[HID:, 0:HID] = w_second_ref[...]
    turned = wf[...].T
    w_first_t, w_second_t = turned[0:HID, 0:48], turned[0:HID, HID:]

    def activations(n):
        cols = pl.ds(pl.multiple_of(n * 512, 512), 512)
        column = n * 512 + lax.broadcasted_iota(jnp.int32, (16, 512), 1)
        residue = column >> 7
        position = 4 * x + (residue >> 3) + 16 * (residue & 7) + 128 * (column & 127)
        band = lax.broadcasted_iota(jnp.int32, (16, 512), 0) + 1
        angle = 2.0 * math.pi / SEQ * ((band * position) & (SEQ - 1)).astype(jnp.float32)
        sine, cosine = sine_cosine(angle)
        ramp = jnp.where(band == 1, position.astype(jnp.float32) / SEQ, 0.0)
        values = jnp.concatenate([cosine, sine, ramp], axis=0)
        feats[:, cols] = stacked(values)
        pre_one = jnp.dot(w_first_t, values, precision=HIGHEST, preferred_element_type=jnp.float32)
        sine, cosine = sine_cosine(pre_one)
        act_one[:, cols] = stacked(sine)
        cos_one[:, cols] = cosine
        pre_two = jnp.dot(w_second_t, sine, precision=HIGHEST, preferred_element_type=jnp.float32)
        sine, cosine = sine_cosine(pre_two)
        act_two[:, cols] = stacked(sine)
        cos_two[:, cols] = cosine

    loop(0, 8, activations)
    go_send[...] = jnp.zeros_like(go_send)
    pay[...] = jnp.zeros_like(pay)
    ch_send[...] = jnp.zeros_like(ch_send)

    def arrived1(i):
        peer = dp_peer(i)
        to_dp(send1.at[peer], recv1.at[peer], ssem1.at[peer], rsem1.at[peer], peer).wait_recv()

    loop(1, DP, arrived1)

    def pass_one(n):
        q0, lt = lax.div(n, 2), lax.rem(n, 2)
        half, k1 = lax.div(q0, 4), lax.rem(q0, 4)
        lanes = pl.ds(pl.multiple_of(k1 * 256 + lt * 128, 128), 128)
        out_lanes = pl.ds(pl.multiple_of(lt * 128, 128), 128)
        values = dft([(recv1[2 * q + half, 0, :, lanes], recv1[2 * q + half, 1, :, lanes]) for q in range(16)])
        for v1 in range(16):
            re, im = values[v1]
            if v1 > 0:
                c, s = first_ref[q0 * 32 + 2 * v1], first_ref[q0 * 32 + 2 * v1 + 1]
                re, im = re * c - im * s, re * s + im * c
            mid[v1, q0, 0, :, out_lanes] = re
            mid[v1, q0, 1, :, out_lanes] = im

    loop(0, 16, pass_one)

    def pass_two(n):
        v1, lt = lax.div(n, 2), lax.rem(n, 2)
        lanes = pl.ds(pl.multiple_of(lt * 128, 128), 128)
        im_lanes = pl.ds(pl.multiple_of(256 + lt * 128, 128), 128)
        values = dft([(mid[v1, q0, 0, :, lanes], mid[v1, q0, 1, :, lanes]) for q0 in range(8)])
        turned = []
        for v2 in range(8):
            re, im = values[v2]
            c = last_ref[0, v1, v2 : v2 + 1, lanes]
            s = last_ref[1, v1, v2 : v2 + 1, lanes]
            turned.append((re * c - im * s, re * s + im * c))
        for pair in range(4):
            rows = pl.ds(pl.multiple_of(v1 * 64 + pair * 16, 16), 16)
            for part, where in ((0, lanes), (1, im_lanes)):
                x = jnp.concatenate([turned[2 * pair][part], turned[2 * pair + 1][part]], axis=0)
                high, low = split(x)
                x_high[rows, where] = high
                x_low[rows, where] = low

    loop(0, 32, pass_two)

    def out_block(i):
        n = lax.rem(x + 1 + i, 4)
        rows = pl.ds(pl.multiple_of(n * 256, 256), 256)
        high, low = x_high[rows, :], x_low[rows, :]
        y = dot(high, dft_high_ref[...], NN) + dot(high, dft_low_ref[...], NN) + dot(low, dft_high_ref[...], NN)
        y = y * window[rows, :]
        for v in range(32):
            send2[n, :, 128 * v : 128 * v + 128] = y[8 * v : 8 * v + 8, :]

        @pl.when(i < 3)
        def _():
            to_dp(send2.at[n], recv2.at[x], ssem2.at[n], rsem2.at[x], 4 * z + n).start()

    loop(0, 4, out_block)
    recv2[x] = send2[x]

    def x_peer(i):
        return lax.rem(x + i, 4)

    def arrived2(i):
        n = x_peer(i)
        to_dp(send2.at[n], recv2.at[n], ssem2.at[n], rsem2.at[n], 4 * z + n).wait_recv()

    loop(1, 4, arrived2)

    out_grad = recv2[...].reshape(32, 4096)
    grad_second = jnp.zeros((2 * HID, 2 * HID), jnp.float32)
    grad_first = jnp.zeros((96, 2 * HID), jnp.float32)
    for j in range(4):
        cols = slice(1024 * j, 1024 * j + 1024)
        hidden = dot(w_out_parts[...], three_rows(out_grad[:, cols]), NN)
        high, low = split(hidden * cos_two[:, cols])
        grad_second += dot(act_one[:, cols], jnp.concatenate([high, low], axis=0), NT)
        back_one = dot(w_second_parts[...], jnp.concatenate([high, low, high], axis=0), NN) * cos_one[:, cols]
        grad_first += dot(feats[:, cols], stacked(back_one), NT)
    grad_second = folded(grad_second, HID)
    grad_first = folded(grad_first, 48)
    pay[0:32, :] = jnp.concatenate([grad_second[0:32], grad_second[32:64]], axis=1)
    pay[32:48, :] = jnp.concatenate([grad_first[0:16], grad_first[16:32]], axis=1)
    pay[48:49, 0:HID] = grad_first[32:33]

    for i in range(DP):
        ar_send[i] = pay[2 * i : 2 * i + 2, :]

    def send_ar(i):
        peer = dp_peer(i)
        to_dp(ar_send.at[peer], ar_recv.at[me], ssem5.at[peer], rsem5.at[me], peer).start()

    loop(1, DP, send_ar)
    ar_recv[me] = ar_send[me]

    grad_out = jnp.zeros((2 * 32, 2 * HID), jnp.float32)
    for j in range(4):
        cols = slice(1024 * j, 1024 * j + 1024)
        grad_out += dot(stacked(out_grad[:, cols]), act_two[:, cols], NT)
    go_send[:, :, 0:HID] = folded(grad_out, 32).reshape(4, 8, HID)

    def send_go(i):
        n = x_peer(i)
        to_dp(go_send.at[n], go_recv.at[x], ssem3.at[n], rsem3.at[x], 4 * z + n).start()

    loop(1, 4, send_go)
    go_recv[x] = go_send[x]

    def arrived_go(i):
        n = x_peer(i)
        to_dp(go_send.at[n], go_recv.at[n], ssem3.at[n], rsem3.at[n], 4 * z + n).wait_recv()

    loop(1, 4, arrived_go)
    total_out = jnp.sum(go_recv[...], axis=0)
    go_sum[...] = total_out
    go_all[mine] = total_out

    def send_go_all(i):
        peer = dp_peer(i)
        to_dp(go_sum, go_all.at[mine], ssem4.at[peer], rsem4.at[me], peer).start()

    loop(1, DP, send_go_all)
    ch_send[2:3, :] = jnp.sum(total_out * total_out, axis=0, keepdims=True)

    def arrived_ar(i):
        peer = dp_peer(i)
        to_dp(ar_send.at[peer], ar_recv.at[peer], ssem5.at[peer], rsem5.at[peer], peer).wait_recv()

    loop(1, DP, arrived_ar)
    ch_send[0:2, :] = jnp.sum(ar_recv[...], axis=0)

    def send_ch(i):
        peer = ch_peer(i)
        to_ch(ch_send, ch_recv.at[col], ssem6.at[peer], rsem6.at[col], peer).start()

    loop(1, CHAN, send_ch)
    ch_recv[col] = ch_send[...]

    def arrived_ch(i):
        peer = ch_peer(i)
        to_ch(ch_send, ch_recv.at[peer], ssem6.at[peer], rsem6.at[peer], peer).wait_recv()

    loop(1, CHAN, arrived_ch)
    ag_send[...] = jnp.sum(ch_recv[...], axis=0)

    def send_ag(i):
        peer = dp_peer(i)
        to_dp(ag_send, ag_recv.at[me], ssem7.at[peer], rsem7.at[me], peer).start()

    loop(1, DP, send_ag)
    ag_recv[me] = ag_send[...]

    def arrived_go_all(i):
        peer = dp_peer(i)
        to_dp(go_sum, go_all.at[peer], ssem4.at[peer], rsem4.at[peer], peer).wait_recv()

    loop(1, DP, arrived_go_all)
    full_out = go_all[...].reshape(COLS, 128).T[0:HID, :]

    def arrived_ag(i):
        peer = dp_peer(i)
        to_dp(ag_send, ag_recv.at[peer], ssem7.at[peer], rsem7.at[peer], peer).wait_recv()

    loop(1, DP, arrived_ag)
    for i in range(DP):
        pay[2 * i : 2 * i + 2, :] = ag_recv[i, 0:2, :]
    second = pay[0:32, :]
    first = pay[32:48, :]
    line = pay[48:49, 0:HID]
    total = (
        jnp.sum(second * second, keepdims=True)
        + jnp.sum(first * first, keepdims=True)
        + jnp.sum(line * line, keepdims=True)
        + jnp.sum(jnp.sum(ag_recv[:, 2:3, :], axis=0), keepdims=True)
    )
    scale = jnp.minimum(1.0, clip_norm / (jnp.sqrt(total) + 1e-06))
    step_out_ref[...] = adam_step(full_out, w_out_ref[...], m_out_ref[0], m_out_ref[1], scale)
    for part in range(2):
        rows, lanes = slice(32 * part, 32 * part + 32), slice(HID * part, HID * part + HID)
        step_second_ref[rows, :] = adam_step(
            second[:, lanes], w_second_ref[rows, :], m_second_ref[0, rows, :], m_second_ref[1, rows, :], scale
        )
        rows = slice(16 * part + 1, 16 * part + 17)
        step_first_ref[rows, :] = adam_step(
            first[:, lanes], w_first_ref[rows, :], m_first_ref[rows, 0, :], m_first_ref[rows, 1, :], scale
        )
    step_first_ref[0:1, :] = adam_step(
        line, w_first_ref[0:1, :], m_first_ref[0:1, 0, :], m_first_ref[0:1, 1, :], scale
    )

    sent()


def local(spec_u, spec_g, decay_length, w_first, w_second, w_out, moments_first, moments_second, moments_out):
    dft_high, dft_low, last, first = constants()
    f32, bf16 = jnp.float32, jnp.bfloat16
    vmem, sem = pltpu.VMEM, pltpu.SemaphoreType.DMA
    in_vmem = pl.BlockSpec(memory_space=pltpu.VMEM)
    anywhere = pl.BlockSpec(memory_space=pl.ANY)

    def pair(n):
        return [sem((n,)), sem((n,))]

    return pl.pallas_call(
        kernel,
        out_shape=(
            jax.ShapeDtypeStruct(w_first.shape, f32),
            jax.ShapeDtypeStruct(w_second.shape, f32),
            jax.ShapeDtypeStruct(w_out.shape, f32),
        ),
        in_specs=[anywhere] * 13,
        out_specs=(in_vmem,) * 3,
        scratch_shapes=[
            vmem((2, ROWS, COLS), f32), vmem((2, ROWS, COLS), f32), sem((4,)),
            vmem((1, COLS), f32), vmem((33, HID), f32), vmem((HID, HID), f32), vmem((HID, COLS), f32),
            vmem((33, 2, HID), f32), vmem((2, HID, HID), f32), vmem((2, HID, COLS), f32),
            vmem((512, 128), bf16), vmem((512, 128), bf16), vmem((2, 16, 8, 256), f32),
            pltpu.SMEM((256,), f32), sem((11,)),
            vmem((DP, 2, 8, ROWS), f32), vmem((DP, 2, 8, ROWS), f32), *pair(DP),
            vmem((16, 8, 2, 8, 256), f32), vmem((1024, 512), bf16), vmem((1024, 512), bf16),
            vmem((COLS, 128), f32), vmem((1024, 128), f32),
            vmem((128, 128), f32), vmem((COLS, 128), f32), vmem((HID, 96), bf16), vmem((HID, 192), bf16),
            vmem((96, 4096), bf16), vmem((128, 4096), bf16), vmem((HID, 4096), f32),
            vmem((128, 4096), bf16), vmem((HID, 4096), f32),
            vmem((4, 8, 4096), f32), vmem((4, 8, 4096), f32), *pair(4),
            vmem((4, 8, 128), f32), vmem((4, 8, 128), f32), *pair(4),
            vmem((8, 128), f32), vmem((DP, 8, 128), f32), *pair(DP),
            vmem((64, 128), f32), vmem((DP, 2, 128), f32), vmem((DP, 2, 128), f32), *pair(DP),
            vmem((4, 128), f32), vmem((CHAN, 4, 128), f32), *pair(CHAN),
            vmem((4, 128), f32), vmem((DP, 4, 128), f32), *pair(DP),
        ],
        compiler_params=pltpu.CompilerParams(
            collective_id=0, has_side_effects=True, vmem_limit_bytes=56 * 1024 * 1024
        ),
        name="hyena_step",
    )(
        spec_u, spec_g, decay_length.reshape(1, COLS), w_first, w_second, w_out,
        jnp.swapaxes(moments_first, 0, 1), moments_second, moments_out,
        jnp.asarray(dft_high), jnp.asarray(dft_low), jnp.asarray(last), jnp.asarray(first),
    )


def solution(mesh):
    return jax.shard_map(
        local,
        mesh=mesh,
        in_specs=(
            P(None, "dp", "chan"),
            P(None, "dp", "chan"),
            P("chan"),
            P(),
            P(),
            P(None, "chan"),
            P(),
            P(),
            P(None, None, "chan"),
        ),
        out_specs=(P(), P(), P(None, "chan")),
        check_vma=False,
    )
```

```python
import functools
import math

import jax
import jax.numpy as jnp
import numpy as np
from jax import lax
from jax.experimental import pallas as pl
from jax.experimental.pallas import tpu as pltpu
from jax.sharding import PartitionSpec as P

MESH = pl.DeviceIdType.MESH
HIGHEST = lax.Precision.HIGHEST

BANDS = 16
HID = 64
DP = 32
CHAN = 16
FREQS = 32768
SEQ = 16384
ROWS = 1024
COLS = 256

beta_one = 0.9
beta_two = 0.999
adam_count = 10.0
adam_eps = 1e-08
weight_decay = 0.1
clip_norm = 1.0


def adam_step(grad, weight, first, second, scale):
    g = grad * scale
    first = beta_one * first + (1.0 - beta_one) * g
    second = beta_two * second + (1.0 - beta_two) * g * g
    first_hat = first / (1.0 - beta_one**adam_count)
    second_hat = second / (1.0 - beta_two**adam_count)
    return first_hat / (jnp.sqrt(second_hat) + adam_eps) + weight_decay * weight


def split(x):
    high = x.astype(jnp.bfloat16)
    low = (x - high.astype(jnp.float32)).astype(jnp.bfloat16)
    return high, low


def dot(a, b, dims):
    return lax.dot_general(a, b, (dims, ((), ())), preferred_element_type=jnp.float32)


def stacked(x):
    return jnp.concatenate(split(x), axis=0)


def folded(x, rows):
    x = x[:rows] + x[rows:]
    return x[:, :HID] + x[:, HID:]


def three_rows(x):
    high, low = split(x)
    return jnp.concatenate([high, low, high], axis=0)


def three_lanes(x):
    high, low = split(x)
    return jnp.concatenate([high, high, low], axis=1)


def sine_cosine(x):
    turns = jnp.floor(x * (2.0 / math.pi) + 0.5)
    r = ((x - turns * 1.5703125) - turns * 4.837512969970703125e-4) - turns * 7.54978995489188216e-8
    z = r * r
    sine = r + r * z * (-1.6666654611e-1 + z * (8.3321608736e-3 - z * 1.9515295891e-4))
    cosine = 1.0 - 0.5 * z + z * z * (4.166664568298827e-2 + z * (-1.388731625493765e-3 + z * 2.443315711809948e-5))
    quarter = turns.astype(jnp.int32)
    odd = (quarter & 1) == 1
    first, second = jnp.where(odd, cosine, sine), jnp.where(odd, sine, cosine)
    return jnp.where((quarter & 2) == 2, -first, first), jnp.where(((quarter + 1) & 2) == 2, -second, second)


NN = ((1,), (0,))
NT = ((1,), (1,))


def times(z, angle_num, angle_den):
    re, im = z
    k = angle_num % angle_den
    if k == 0:
        return re, im
    if 4 * k == angle_den:
        return -im, re
    if 2 * k == angle_den:
        return -re, -im
    if 4 * k == 3 * angle_den:
        return im, -re
    if 8 * k == angle_den:
        r = math.sqrt(0.5)
        return (re - im) * r, (re + im) * r
    if 8 * k == 3 * angle_den:
        r = math.sqrt(0.5)
        return (re + im) * (-r), (re - im) * r
    c, s = math.cos(2 * math.pi * k / angle_den), math.sin(2 * math.pi * k / angle_den)
    return re * c - im * s, re * s + im * c


def dft(values):
    n = len(values)
    if n == 1:
        return values
    even, odd = dft(values[0::2]), dft(values[1::2])
    low, high = [], []
    for k in range(n // 2):
        t = times(odd[k], k, n)
        low.append((even[k][0] + t[0], even[k][1] + t[1]))
        high.append((even[k][0] - t[0], even[k][1] - t[1]))
    return low + high


def constants():
    lane = np.arange(256)[:, None] * np.arange(128)[None, :] % 256
    angle = 2.0 * np.pi / 256 * lane
    table = np.concatenate([np.cos(angle), -np.sin(angle)], axis=0).astype(np.float32)
    high = table.astype(jnp.bfloat16)
    low = (table - high.astype(np.float32)).astype(jnp.bfloat16)
    v = np.arange(16)[:, None] + 16 * np.arange(8)[None, :]
    angle = 2.0 * np.pi / FREQS * (v[:, :, None] * np.arange(256)[None, None, :])
    last = (np.stack([np.cos(angle), np.sin(angle)]) / FREQS).astype(np.float32)
    angle = 2.0 * np.pi / 128 * (np.arange(8)[:, None] * np.arange(16)[None, :])
    first = np.stack([np.cos(angle), np.sin(angle)], axis=-1).astype(np.float32)
    return high, low, last, first.reshape(-1)


def kernel(
    u_hbm, g_hbm, decay_hbm, w_first_hbm, w_second_hbm, w_out_hbm, m_first_hbm, m_second_hbm, m_out_hbm,
    dft_high_hbm, dft_low_hbm, last_hbm, first_hbm,
    step_first_ref, step_second_ref, step_out_ref,
    u_buf, g_buf, in_sem,
    decay_ref, w_first_ref, w_second_ref, w_out_ref, m_first_ref, m_second_ref, m_out_ref,
    dft_high_ref, dft_low_ref, last_ref, first_ref, small_sem,
    send1, recv1, ssem1, rsem1,
    mid, x_high, x_low, decay_rows, window,
    wf, w_rows, w_out_parts, w_second_parts, feats, act_one, cos_one, act_two, cos_two,
    send2, recv2, ssem2, rsem2,
    go_send, go_recv, ssem3, rsem3,
    go_sum, go_all, ssem4, rsem4,
    pay, ar_send, ar_recv, ssem5, rsem5,
    ch_send, ch_recv, ssem6, rsem6,
    ag_send, ag_recv, ssem7, rsem7,
):
    me = lax.axis_index("dp")
    col = lax.axis_index("chan")

    def dp_peer(i):
        return lax.rem(me + i, DP)

    def ch_peer(i):
        return lax.rem(col + i, CHAN)

    def chunk_of(device):
        return lax.rem(device, 2) * 16 + lax.div(device, 2)

    mine = chunk_of(me)
    z, x = lax.div(me, 4), lax.rem(me, 4)

    def to_dp(src, dst, ssem, rsem, peer):
        return pltpu.make_async_remote_copy(
            src_ref=src, dst_ref=dst, send_sem=ssem, recv_sem=rsem, device_id=(peer, col), device_id_type=MESH
        )

    def to_ch(src, dst, ssem, rsem, peer):
        return pltpu.make_async_remote_copy(
            src_ref=src, dst_ref=dst, send_sem=ssem, recv_sem=rsem, device_id=(me, peer), device_id_type=MESH
        )

    def loop(low, high, body, unroll=False):
        def wrapped(i, carry):
            body(i)
            return carry

        lax.fori_loop(low, high, wrapped, 0, unroll=unroll)

    def sent_dp(i, src, dst, ssem, rsem):
        peer = dp_peer(i)
        to_dp(src, dst.at[me], ssem.at[peer], rsem.at[me], peer).wait_send()

    def in_copy(block, which):
        hbm, buf = ((u_hbm, u_buf), (g_hbm, g_buf))[which]
        lanes = pl.ds(block * 128, 128)
        return pltpu.make_async_copy(hbm.at[:, :, lanes], buf.at[:, :, lanes], in_sem.at[2 * block + which])

    for block in range(2):
        for which in range(2):
            in_copy(block, which).start()

    small = [
        pltpu.make_async_copy(src, dst, small_sem.at[n])
        for n, (src, dst) in enumerate((
            (decay_hbm, decay_ref), (w_first_hbm, w_first_ref), (w_second_hbm, w_second_ref),
            (w_out_hbm, w_out_ref), (m_first_hbm, m_first_ref), (m_second_hbm, m_second_ref),
            (m_out_hbm, m_out_ref), (dft_high_hbm, dft_high_ref), (dft_low_hbm, dft_low_ref),
            (last_hbm, last_ref), (first_hbm, first_ref),
        ))
    ]

    barrier = pltpu.get_barrier_semaphore()

    def greet_dp(i):
        pl.semaphore_signal(barrier, inc=1, device_id=(dp_peer(i), col), device_id_type=MESH)

    def greet_ch(i):
        pl.semaphore_signal(barrier, inc=1, device_id=(me, ch_peer(i)), device_id_type=MESH)

    loop(1, DP, greet_dp)
    loop(1, CHAN, greet_ch)

    for block in range(2):
        for which in range(2):
            in_copy(block, which).wait()

        def product(kt, block=block):
            rows = pl.ds(pl.multiple_of(kt * 128, 128), 128)
            lanes = pl.ds(block * 128, 128)
            u_re, u_im = u_buf[0, rows, lanes], u_buf[1, rows, lanes]
            g_re, g_im = g_buf[0, rows, lanes], g_buf[1, rows, lanes]
            re = g_re * u_re + g_im * u_im
            im = g_im * u_re - g_re * u_im
            owners = pl.ds(block * 16, 16)
            send1[owners, 0, :, rows] = re.T.reshape(16, 8, 128)
            send1[owners, 1, :, rows] = im.T.reshape(16, 8, 128)

        loop(0, ROWS // 128, product)
        if block == 0:
            pl.semaphore_wait(barrier, DP - 1 + CHAN - 1)

        def send(i, block=block):
            n = lax.rem(lax.div(me, 2) + i, 16)
            peer = 2 * n + block

            @pl.when(peer != me)
            def _():
                to_dp(send1.at[block * 16 + n], recv1.at[me], ssem1.at[peer], rsem1.at[me], peer).start()

        loop(0, 16, send)
    for copy in small:
        copy.start()
    recv1[me] = send1[mine]
    for copy in small:
        copy.wait()

    decay_rows[...] = jnp.broadcast_to(decay_ref[...], (128, COLS)).T
    decay = decay_rows[pl.ds(pl.multiple_of(mine * 8, 8), 8), :]
    lane = lax.broadcasted_iota(jnp.int32, (8, 128), 1)

    def make_window(v):
        t = 4 * lax.rem(lax.div(v, 8), 4) + lax.div(v, 32) + 16 * lax.rem(v, 8) + 128 * lane
        window[pl.ds(pl.multiple_of(v * 8, 8), 8), :] = jnp.exp(-t.astype(jnp.float32) / decay)

    loop(0, 128, make_window)

    w_rows[:, 0:HID] = w_out_ref[...].T
    w_rows[:, HID:] = jnp.zeros((COLS, 128 - HID), jnp.float32)
    met = [w_rows[pl.ds(pl.multiple_of(chunk_of(4 * z + n) * 8, 8), 8), :] for n in range(4)]
    met = jnp.concatenate(met + [jnp.zeros((96, 128), jnp.float32)], axis=0).T
    w_out_parts[...] = three_lanes(met[0:HID, 0:32])
    w_second_parts[...] = three_lanes(w_second_ref[...])

    wf[...] = jnp.zeros_like(wf)
    wf[0:32, 0:HID] = w_first_ref[1:33, :]
    wf[32:33, 0:HID] = w_first_ref[0:1, :]
    wf[HID:, 0:HID] = w_second_ref[...]
    turned = wf[...].T
    w_first_t, w_second_t = turned[0:HID, 0:48], turned[0:HID, HID:]

    def activations(n):
        cols = pl.ds(pl.multiple_of(n * 512, 512), 512)
        column = n * 512 + lax.broadcasted_iota(jnp.int32, (16, 512), 1)
        residue = column >> 7
        position = 4 * x + (residue >> 3) + 16 * (residue & 7) + 128 * (column & 127)
        band = lax.broadcasted_iota(jnp.int32, (16, 512), 0) + 1
        angle = 2.0 * math.pi / SEQ * ((band * position) & (SEQ - 1)).astype(jnp.float32)
        sine, cosine = sine_cosine(angle)
        ramp = jnp.where(band == 1, position.astype(jnp.float32) / SEQ, 0.0)
        values = jnp.concatenate([cosine, sine, ramp], axis=0)
        feats[:, cols] = stacked(values)
        pre_one = jnp.dot(w_first_t, values, precision=HIGHEST, preferred_element_type=jnp.float32)
        sine, cosine = sine_cosine(pre_one)
        act_one[:, cols] = stacked(sine)
        cos_one[:, cols] = cosine
        pre_two = jnp.dot(w_second_t, sine, precision=HIGHEST, preferred_element_type=jnp.float32)
        sine, cosine = sine_cosine(pre_two)
        act_two[:, cols] = stacked(sine)
        cos_two[:, cols] = cosine

    loop(0, 8, activations)
    go_send[...] = jnp.zeros_like(go_send)
    pay[...] = jnp.zeros_like(pay)
    ch_send[...] = jnp.zeros_like(ch_send)

    def arrived1(i):
        peer = dp_peer(i)
        to_dp(send1.at[peer], recv1.at[peer], ssem1.at[peer], rsem1.at[peer], peer).wait_recv()

    loop(1, DP, arrived1)

    def pass_one(n):
        q0, lt = lax.div(n, 2), lax.rem(n, 2)
        half, k1 = lax.div(q0, 4), lax.rem(q0, 4)
        lanes = pl.ds(pl.multiple_of(k1 * 256 + lt * 128, 128), 128)
        out_lanes = pl.ds(pl.multiple_of(lt * 128, 128), 128)
        values = dft([(recv1[2 * q + half, 0, :, lanes], recv1[2 * q + half, 1, :, lanes]) for q in range(16)])
        for v1 in range(16):
            re, im = values[v1]
            if v1 > 0:
                c, s = first_ref[q0 * 32 + 2 * v1], first_ref[q0 * 32 + 2 * v1 + 1]
                re, im = re * c - im * s, re * s + im * c
            mid[v1, q0, 0, :, out_lanes] = re
            mid[v1, q0, 1, :, out_lanes] = im

    loop(0, 16, pass_one)

    def pass_two(n):
        v1, lt = lax.div(n, 2), lax.rem(n, 2)
        lanes = pl.ds(pl.multiple_of(lt * 128, 128), 128)
        im_lanes = pl.ds(pl.multiple_of(256 + lt * 128, 128), 128)
        values = dft([(mid[v1, q0, 0, :, lanes], mid[v1, q0, 1, :, lanes]) for q0 in range(8)])
        turned = []
        for v2 in range(8):
            re, im = values[v2]
            c = last_ref[0, v1, v2 : v2 + 1, lanes]
            s = last_ref[1, v1, v2 : v2 + 1, lanes]
            turned.append((re * c - im * s, re * s + im * c))
        for pair in range(4):
            rows = pl.ds(pl.multiple_of(lax.rem(v1, 4) * 256 + lax.div(v1, 4) * 64 + pair * 16, 16), 16)
            for part, where in ((0, lanes), (1, im_lanes)):
                x = jnp.concatenate([turned[2 * pair][part], turned[2 * pair + 1][part]], axis=0)
                high, low = split(x)
                x_high[rows, where] = high
                x_low[rows, where] = low

    loop(0, 32, pass_two)

    def x_peer(i):
        return lax.rem(x + i, 4)

    def to_x(i, j):
        n, cols = x_peer(i), slice(1024 * j, 1024 * j + 1024)
        return to_dp(send2.at[n, :, cols], recv2.at[x, :, cols], ssem2.at[n, j], rsem2.at[x, j], 4 * z + n)

    def from_x(i, j):
        n, cols = x_peer(i), slice(1024 * j, 1024 * j + 1024)
        return to_dp(send2.at[n, :, cols], recv2.at[n, :, cols], ssem2.at[n, j], rsem2.at[n, j], 4 * z + n)

    for j in range(4):
        rows, cols = slice(256 * j, 256 * j + 256), slice(1024 * j, 1024 * j + 1024)
        high, low = x_high[rows, :], x_low[rows, :]
        y = dot(high, dft_high_ref[...], NN) + dot(high, dft_low_ref[...], NN) + dot(low, dft_high_ref[...], NN)
        y = y * window[rows, :]
        for n in range(4):
            for v in range(8):
                row, lanes = 64 * n + 8 * v, 1024 * j + 128 * v
                send2[n, :, lanes : lanes + 128] = y[row : row + 8, :]
        for i in (2, 1, 3):
            to_x(i, j).start()
        recv2[x, :, cols] = send2[x, :, cols]

    w_parts, second_parts = w_out_parts[...], w_second_parts[...]
    grad_second = jnp.zeros((2 * HID, 2 * HID), jnp.float32)
    grad_first = jnp.zeros((96, 2 * HID), jnp.float32)
    for j in range(4):
        cols = slice(1024 * j, 1024 * j + 1024)
        for i in (1, 3, 2):
            from_x(i, j).wait_recv()
        hidden = dot(w_parts, three_rows(recv2[:, :, cols].reshape(32, 1024)), NN)
        high, low = split(hidden * cos_two[:, cols])
        grad_second += dot(act_one[:, cols], jnp.concatenate([high, low], axis=0), NT)
        back_one = dot(second_parts, jnp.concatenate([high, low, high], axis=0), NN) * cos_one[:, cols]
        grad_first += dot(feats[:, cols], stacked(back_one), NT)
    grad_second = folded(grad_second, HID)
    grad_first = folded(grad_first, 48)
    pay[0:32, :] = jnp.concatenate([grad_second[0:32], grad_second[32:64]], axis=1)
    pay[32:48, :] = jnp.concatenate([grad_first[0:16], grad_first[16:32]], axis=1)
    pay[48:49, 0:HID] = grad_first[32:33]

    for i in range(DP):
        ar_send[i] = pay[2 * i : 2 * i + 2, :]

    def send_ar(i):
        peer = dp_peer(i)
        to_dp(ar_send.at[peer], ar_recv.at[me], ssem5.at[peer], rsem5.at[me], peer).start()

    loop(1, DP, send_ar, True)
    ar_recv[me] = ar_send[me]

    grad_out = jnp.zeros((2 * 32, 2 * HID), jnp.float32)
    for j in range(4):
        cols = slice(1024 * j, 1024 * j + 1024)
        grad_out += dot(stacked(recv2[:, :, cols].reshape(32, 1024)), act_two[:, cols], NT)
    go_send[:, :, 0:HID] = folded(grad_out, 32).reshape(4, 8, HID)

    def send_go(i):
        n = x_peer(i)
        to_dp(go_send.at[n], go_recv.at[x], ssem3.at[n], rsem3.at[x], 4 * z + n).start()

    loop(1, 4, send_go)
    go_recv[x] = go_send[x]

    def arrived_go(i):
        n = x_peer(i)
        to_dp(go_send.at[n], go_recv.at[n], ssem3.at[n], rsem3.at[n], 4 * z + n).wait_recv()

    loop(1, 4, arrived_go)
    total_out = jnp.sum(go_recv[...], axis=0)
    go_sum[...] = total_out
    go_all[mine] = total_out

    ch_send[2:3, :] = jnp.sum(total_out * total_out, axis=0, keepdims=True)

    def arrived_ar(i):
        peer = dp_peer(i)
        to_dp(ar_send.at[peer], ar_recv.at[peer], ssem5.at[peer], rsem5.at[peer], peer).wait_recv()

    loop(1, DP, arrived_ar, True)
    ch_send[0:2, :] = jnp.sum(ar_recv[...], axis=0)

    def send_ch(i):
        peer = ch_peer(i)
        to_ch(ch_send, ch_recv.at[col], ssem6.at[peer], rsem6.at[col], peer).start()

    loop(1, CHAN, send_ch, True)
    ch_recv[col] = ch_send[...]

    def send_go_all(i):
        peer = dp_peer(i)
        to_dp(go_sum, go_all.at[mine], ssem4.at[peer], rsem4.at[me], peer).start()

    loop(1, DP, send_go_all)

    loop(1, DP, lambda i: sent_dp(i, send1.at[dp_peer(i)], recv1, ssem1, rsem1))
    for j in range(4):
        for i in range(1, 4):
            to_x(i, j).wait_send()

    def arrived_ch(i):
        peer = ch_peer(i)
        to_ch(ch_send, ch_recv.at[peer], ssem6.at[peer], rsem6.at[peer], peer).wait_recv()

    loop(1, CHAN, arrived_ch, True)
    ag_send[...] = jnp.sum(ch_recv[...], axis=0)

    def send_ag(i):
        peer = dp_peer(i)
        to_dp(ag_send, ag_recv.at[me], ssem7.at[peer], rsem7.at[me], peer).start()

    loop(1, DP, send_ag, True)
    ag_recv[me] = ag_send[...]

    def sent_small(i):
        n = x_peer(i)
        to_dp(go_send.at[n], go_recv.at[x], ssem3.at[n], rsem3.at[x], 4 * z + n).wait_send()

    loop(1, 4, sent_small)

    def sent_ch(i):
        peer = ch_peer(i)
        to_ch(ch_send, ch_recv.at[col], ssem6.at[peer], rsem6.at[col], peer).wait_send()

    loop(1, CHAN, sent_ch)
    loop(1, DP, lambda i: sent_dp(i, ar_send.at[dp_peer(i)], ar_recv, ssem5, rsem5))
    loop(1, DP, lambda i: sent_dp(i, go_sum, go_all, ssem4, rsem4))

    def arrived_go_all(i):
        peer = dp_peer(i)
        to_dp(go_sum, go_all.at[peer], ssem4.at[peer], rsem4.at[peer], peer).wait_recv()

    loop(1, DP, lambda i: sent_dp(i, ag_send, ag_recv, ssem7, rsem7))
    loop(1, DP, arrived_go_all)
    full_out = go_all[...].reshape(COLS, 128).T[0:HID, :]

    def arrived_ag(i):
        peer = dp_peer(i)
        to_dp(ag_send, ag_recv.at[peer], ssem7.at[peer], rsem7.at[peer], peer).wait_recv()

    loop(1, DP, arrived_ag, True)
    for i in range(DP):
        pay[2 * i : 2 * i + 2, :] = ag_recv[i, 0:2, :]
    second = pay[0:32, :]
    first = pay[32:48, :]
    line = pay[48:49, 0:HID]
    total = (
        jnp.sum(second * second, keepdims=True)
        + jnp.sum(first * first, keepdims=True)
        + jnp.sum(line * line, keepdims=True)
        + jnp.sum(jnp.sum(ag_recv[:, 2:3, :], axis=0), keepdims=True)
    )
    scale = jnp.minimum(1.0, clip_norm / (jnp.sqrt(total) + 1e-06))
    step_out_ref[...] = adam_step(full_out, w_out_ref[...], m_out_ref[0], m_out_ref[1], scale)
    for part in range(2):
        rows, lanes = slice(32 * part, 32 * part + 32), slice(HID * part, HID * part + HID)
        step_second_ref[rows, :] = adam_step(
            second[:, lanes], w_second_ref[rows, :], m_second_ref[0, rows, :], m_second_ref[1, rows, :], scale
        )
        rows = slice(16 * part + 1, 16 * part + 17)
        step_first_ref[rows, :] = adam_step(
            first[:, lanes], w_first_ref[rows, :], m_first_ref[rows, 0, :], m_first_ref[rows, 1, :], scale
        )
    step_first_ref[0:1, :] = adam_step(
        line, w_first_ref[0:1, :], m_first_ref[0:1, 0, :], m_first_ref[0:1, 1, :], scale
    )


def hand_over(*refs):
    sources, results, held, sems = refs[:3], refs[3:6], refs[6:9], refs[9]
    fetch = [pltpu.make_async_copy(sources[n], held[n], sems.at[0, n]) for n in range(3)]
    write = [pltpu.make_async_copy(held[n], results[n], sems.at[1, n]) for n in range(3)]
    for copy in fetch:
        copy.start()
    for n in range(3):
        fetch[n].wait()
        write[n].start()
    for copy in write:
        copy.wait()


def local(spec_u, spec_g, decay_length, w_first, w_second, w_out, moments_first, moments_second, moments_out):
    dft_high, dft_low, last, first = constants()
    f32, bf16 = jnp.float32, jnp.bfloat16
    vmem, sem = pltpu.VMEM, pltpu.SemaphoreType.DMA
    in_vmem = pl.BlockSpec(memory_space=pltpu.VMEM)
    anywhere = pl.BlockSpec(memory_space=pl.ANY)

    def pair(n):
        return [sem((n,)), sem((n,))]

    steps = pl.pallas_call(
        kernel,
        out_shape=(
            jax.ShapeDtypeStruct(w_first.shape, f32),
            jax.ShapeDtypeStruct(w_second.shape, f32),
            jax.ShapeDtypeStruct(w_out.shape, f32),
        ),
        in_specs=[anywhere] * 13,
        out_specs=(in_vmem,) * 3,
        scratch_shapes=[
            vmem((2, ROWS, COLS), f32), vmem((2, ROWS, COLS), f32), sem((4,)),
            vmem((1, COLS), f32), vmem((33, HID), f32), vmem((HID, HID), f32), vmem((HID, COLS), f32),
            vmem((33, 2, HID), f32), vmem((2, HID, HID), f32), vmem((2, HID, COLS), f32),
            vmem((512, 128), bf16), vmem((512, 128), bf16), vmem((2, 16, 8, 256), f32),
            pltpu.SMEM((256,), f32), sem((11,)),
            vmem((DP, 2, 8, ROWS), f32), vmem((DP, 2, 8, ROWS), f32), *pair(DP),
            vmem((16, 8, 2, 8, 256), f32), vmem((1024, 512), bf16), vmem((1024, 512), bf16),
            vmem((COLS, 128), f32), vmem((1024, 128), f32),
            vmem((128, 128), f32), vmem((COLS, 128), f32), vmem((HID, 96), bf16), vmem((HID, 192), bf16),
            vmem((96, 4096), bf16), vmem((128, 4096), bf16), vmem((HID, 4096), f32),
            vmem((128, 4096), bf16), vmem((HID, 4096), f32),
            vmem((4, 8, 4096), f32), vmem((4, 8, 4096), f32), sem((4, 4)), sem((4, 4)),
            vmem((4, 8, 128), f32), vmem((4, 8, 128), f32), *pair(4),
            vmem((8, 128), f32), vmem((DP, 8, 128), f32), *pair(DP),
            vmem((64, 128), f32), vmem((DP, 2, 128), f32), vmem((DP, 2, 128), f32), *pair(DP),
            vmem((4, 128), f32), vmem((CHAN, 4, 128), f32), *pair(CHAN),
            vmem((4, 128), f32), vmem((DP, 4, 128), f32), *pair(DP),
        ],
        compiler_params=pltpu.CompilerParams(
            collective_id=0, has_side_effects=True, vmem_limit_bytes=56 * 1024 * 1024
        ),
        name="hyena_step",
    )(
        spec_u, spec_g, decay_length.reshape(1, COLS), w_first, w_second, w_out,
        jnp.swapaxes(moments_first, 0, 1), moments_second, moments_out,
        jnp.asarray(dft_high), jnp.asarray(dft_low), jnp.asarray(last), jnp.asarray(first),
    )
    return pl.pallas_call(
        hand_over,
        out_shape=[jax.ShapeDtypeStruct(step.shape, f32) for step in steps],
        in_specs=[anywhere] * 3,
        out_specs=[anywhere] * 3,
        scratch_shapes=[vmem(step.shape, f32) for step in steps] + [sem((2, 3))],
        compiler_params=pltpu.CompilerParams(vmem_limit_bytes=56 * 1024 * 1024),
        name="hand_over",
    )(*steps)


def solution(mesh):
    return jax.shard_map(
        local,
        mesh=mesh,
        in_specs=(
            P(None, "dp", "chan"),
            P(None, "dp", "chan"),
            P("chan"),
            P(),
            P(),
            P(None, "chan"),
            P(),
            P(),
            P(None, None, "chan"),
        ),
        out_specs=(P(), P(), P(None, "chan")),
        check_vma=False,
    )
```

```python
import functools
import math

import jax
import jax.numpy as jnp
import numpy as np
from jax import lax
from jax.experimental import pallas as pl
from jax.experimental.pallas import tpu as pltpu
from jax.sharding import PartitionSpec as P

MESH = pl.DeviceIdType.MESH
HIGHEST = lax.Precision.HIGHEST

BANDS = 16
HID = 64
DP = 32
CHAN = 16
FREQS = 32768
SEQ = 16384
ROWS = 1024
COLS = 256

beta_one = 0.9
beta_two = 0.999
adam_count = 10.0
adam_eps = 1e-08
weight_decay = 0.1
clip_norm = 1.0


def adam_step(grad, weight, first, second, scale):
    g = grad * scale
    first = beta_one * first + (1.0 - beta_one) * g
    second = beta_two * second + (1.0 - beta_two) * g * g
    first_hat = first / (1.0 - beta_one**adam_count)
    second_hat = second / (1.0 - beta_two**adam_count)
    return first_hat / (jnp.sqrt(second_hat) + adam_eps) + weight_decay * weight


def split(x):
    high = x.astype(jnp.bfloat16)
    low = (x - high.astype(jnp.float32)).astype(jnp.bfloat16)
    return high, low


def dot(a, b, dims):
    return lax.dot_general(a, b, (dims, ((), ())), preferred_element_type=jnp.float32)


def stacked(x):
    return jnp.concatenate(split(x), axis=0)


def folded(x, rows):
    x = x[:rows] + x[rows:]
    return x[:, :HID] + x[:, HID:]


def three_rows(x):
    high, low = split(x)
    return jnp.concatenate([high, low, high], axis=0)


def three_lanes(x):
    high, low = split(x)
    return jnp.concatenate([high, high, low], axis=1)


def sine_cosine(x):
    turns = jnp.floor(x * (2.0 / math.pi) + 0.5)
    r = ((x - turns * 1.5703125) - turns * 4.837512969970703125e-4) - turns * 7.54978995489188216e-8
    z = r * r
    sine = r + r * z * (-1.6666654611e-1 + z * (8.3321608736e-3 - z * 1.9515295891e-4))
    cosine = 1.0 - 0.5 * z + z * z * (4.166664568298827e-2 + z * (-1.388731625493765e-3 + z * 2.443315711809948e-5))
    quarter = turns.astype(jnp.int32)
    odd = (quarter & 1) == 1
    first, second = jnp.where(odd, cosine, sine), jnp.where(odd, sine, cosine)
    return jnp.where((quarter & 2) == 2, -first, first), jnp.where(((quarter + 1) & 2) == 2, -second, second)


NN = ((1,), (0,))
NT = ((1,), (1,))


def times(z, angle_num, angle_den):
    re, im = z
    k = angle_num % angle_den
    if k == 0:
        return re, im
    if 4 * k == angle_den:
        return -im, re
    if 2 * k == angle_den:
        return -re, -im
    if 4 * k == 3 * angle_den:
        return im, -re
    if 8 * k == angle_den:
        r = math.sqrt(0.5)
        return (re - im) * r, (re + im) * r
    if 8 * k == 3 * angle_den:
        r = math.sqrt(0.5)
        return (re + im) * (-r), (re - im) * r
    c, s = math.cos(2 * math.pi * k / angle_den), math.sin(2 * math.pi * k / angle_den)
    return re * c - im * s, re * s + im * c


def dft(values):
    n = len(values)
    if n == 1:
        return values
    even, odd = dft(values[0::2]), dft(values[1::2])
    low, high = [], []
    for k in range(n // 2):
        t = times(odd[k], k, n)
        low.append((even[k][0] + t[0], even[k][1] + t[1]))
        high.append((even[k][0] - t[0], even[k][1] - t[1]))
    return low + high


def constants():
    lane = np.arange(256)[:, None] * np.arange(128)[None, :] % 256
    angle = 2.0 * np.pi / 256 * lane
    table = np.concatenate([np.cos(angle), -np.sin(angle)], axis=0).astype(np.float32)
    high = table.astype(jnp.bfloat16)
    low = (table - high.astype(np.float32)).astype(jnp.bfloat16)
    v = np.arange(16)[:, None] + 16 * np.arange(8)[None, :]
    angle = 2.0 * np.pi / FREQS * (v[:, :, None] * np.arange(256)[None, None, :])
    last = (np.stack([np.cos(angle), np.sin(angle)]) / FREQS).astype(np.float32)
    angle = 2.0 * np.pi / 128 * (np.arange(8)[:, None] * np.arange(16)[None, :])
    first = np.stack([np.cos(angle), np.sin(angle)], axis=-1).astype(np.float32)
    return high, low, last, first.reshape(-1)


def kernel(
    u_hbm, g_hbm, decay_hbm, w_first_hbm, w_second_hbm, w_out_hbm, m_first_hbm, m_second_hbm, m_out_hbm,
    dft_high_hbm, dft_low_hbm, last_hbm, first_hbm,
    step_first_ref, step_second_ref, step_out_ref,
    u_buf, g_buf, in_sem,
    decay_ref, w_first_ref, w_second_ref, w_out_ref, m_first_ref, m_second_ref, m_out_ref,
    dft_high_ref, dft_low_ref, last_ref, first_ref, small_sem,
    send1, recv1, ssem1, rsem1,
    mid, x_high, x_low, decay_rows, window,
    wf, w_rows, w_mine, w_theirs, ssem8, rsem8, w_out_parts, w_second_parts, feats, act_one, cos_one, act_two, cos_two,
    own2, send2, recv2, ssem2, rsem2,
    go_send, go_recv, ssem3, rsem3,
    go_sum, go_all, ssem4, rsem4,
    pay, ar_send, ar_recv, ssem5, rsem5,
    ch_send, ch_recv, ssem6, rsem6,
    ag_send, ag_recv, ssem7, rsem7,
):
    me = lax.axis_index("dp")
    col = lax.axis_index("chan")

    def dp_peer(i):
        return lax.rem(me + i, DP)

    def ch_peer(i):
        return lax.rem(col + i, CHAN)

    def chunk_of(device):
        return lax.rem(device, 2) * 16 + lax.div(device, 2)

    mine = chunk_of(me)
    core = lax.rem(col, 2)
    sibling = col + 1 - 2 * core

    def to_dp(src, dst, ssem, rsem, peer):
        return pltpu.make_async_remote_copy(
            src_ref=src, dst_ref=dst, send_sem=ssem, recv_sem=rsem, device_id=(peer, col), device_id_type=MESH
        )

    def to_ch(src, dst, ssem, rsem, peer):
        return pltpu.make_async_remote_copy(
            src_ref=src, dst_ref=dst, send_sem=ssem, recv_sem=rsem, device_id=(me, peer), device_id_type=MESH
        )

    def loop(low, high, body, unroll=False):
        def wrapped(i, carry):
            body(i)
            return carry

        lax.fori_loop(low, high, wrapped, 0, unroll=unroll)

    def sent_dp(i, src, dst, ssem, rsem):
        peer = dp_peer(i)
        to_dp(src, dst.at[me], ssem.at[peer], rsem.at[me], peer).wait_send()

    def in_copy(block, which):
        hbm, buf = ((u_hbm, u_buf), (g_hbm, g_buf))[which]
        lanes = pl.ds(block * 128, 128)
        return pltpu.make_async_copy(hbm.at[:, :, lanes], buf.at[:, :, lanes], in_sem.at[2 * block + which])

    for block in range(2):
        for which in range(2):
            in_copy(block, which).start()

    small = [
        pltpu.make_async_copy(src, dst, small_sem.at[n])
        for n, (src, dst) in enumerate((
            (decay_hbm, decay_ref), (w_first_hbm, w_first_ref), (w_second_hbm, w_second_ref),
            (w_out_hbm, w_out_ref), (m_first_hbm, m_first_ref), (m_second_hbm, m_second_ref),
            (m_out_hbm, m_out_ref), (dft_high_hbm, dft_high_ref), (dft_low_hbm, dft_low_ref),
            (last_hbm, last_ref), (first_hbm, first_ref),
        ))
    ]

    barrier = pltpu.get_barrier_semaphore()

    def greet_dp(i):
        pl.semaphore_signal(barrier, inc=1, device_id=(dp_peer(i), col), device_id_type=MESH)

    def greet_ch(i):
        pl.semaphore_signal(barrier, inc=1, device_id=(me, ch_peer(i)), device_id_type=MESH)

    loop(1, DP, greet_dp)
    loop(1, CHAN, greet_ch)

    for block in range(2):
        for which in range(2):
            in_copy(block, which).wait()

        def product(kt, block=block):
            rows = pl.ds(pl.multiple_of(kt * 128, 128), 128)
            lanes = pl.ds(block * 128, 128)
            u_re, u_im = u_buf[0, rows, lanes], u_buf[1, rows, lanes]
            g_re, g_im = g_buf[0, rows, lanes], g_buf[1, rows, lanes]
            re = g_re * u_re + g_im * u_im
            im = g_im * u_re - g_re * u_im
            owners = pl.ds(block * 16, 16)
            send1[owners, 0, :, rows] = re.T.reshape(16, 8, 128)
            send1[owners, 1, :, rows] = im.T.reshape(16, 8, 128)

        loop(0, ROWS // 128, product)
        if block == 0:
            pl.semaphore_wait(barrier, DP - 1 + CHAN - 1)

        def send(i, block=block):
            n = lax.rem(lax.div(me, 2) + i, 16)
            peer = 2 * n + block

            @pl.when(peer != me)
            def _():
                to_dp(send1.at[block * 16 + n], recv1.at[me], ssem1.at[peer], rsem1.at[me], peer).start()

        loop(0, 16, send)
    for copy in small:
        copy.start()
    recv1[me] = send1[mine]
    for copy in small:
        copy.wait()

    decay_rows[...] = jnp.broadcast_to(decay_ref[...], (128, COLS)).T
    decay = decay_rows[pl.ds(pl.multiple_of(mine * 8, 8), 8), :]
    lane = lax.broadcasted_iota(jnp.int32, (8, 128), 1)

    def make_window(v):
        t = lax.div(v, 8) + 16 * lax.rem(v, 8) + 128 * lane
        window[pl.ds(pl.multiple_of(v * 8, 8), 8), :] = jnp.exp(-t.astype(jnp.float32) / decay)

    loop(0, 128, make_window)

    w_rows[:, 0:HID] = w_out_ref[...].T
    w_rows[:, HID:] = jnp.zeros((COLS, 128 - HID), jnp.float32)
    w_mine[...] = w_rows[pl.ds(pl.multiple_of(mine * 8, 8), 8), :]
    w_copy = to_ch(w_mine, w_theirs, ssem8.at[0], rsem8.at[0], sibling)
    w_copy.start()
    w_second_parts[...] = three_lanes(w_second_ref[...])

    wf[...] = jnp.zeros_like(wf)
    wf[0:32, 0:HID] = w_first_ref[1:33, :]
    wf[32:33, 0:HID] = w_first_ref[0:1, :]
    wf[HID:, 0:HID] = w_second_ref[...]
    turned = wf[...].T
    w_first_t, w_second_t = turned[0:HID, 0:48], turned[0:HID, HID:]

    def activations(n):
        cols = pl.ds(pl.multiple_of(n * 512, 512), 512)
        column = n * 512 + lax.broadcasted_iota(jnp.int32, (16, 512), 1)
        residue = column >> 7
        position = 8 * core + (residue >> 3) + 16 * (residue & 7) + 128 * (column & 127)
        band = lax.broadcasted_iota(jnp.int32, (16, 512), 0) + 1
        angle = 2.0 * math.pi / SEQ * ((band * position) & (SEQ - 1)).astype(jnp.float32)
        sine, cosine = sine_cosine(angle)
        ramp = jnp.where(band == 1, position.astype(jnp.float32) / SEQ, 0.0)
        values = jnp.concatenate([cosine, sine, ramp], axis=0)
        feats[:, cols] = stacked(values)
        pre_one = jnp.dot(w_first_t, values, precision=HIGHEST, preferred_element_type=jnp.float32)
        sine, cosine = sine_cosine(pre_one)
        act_one[:, cols] = stacked(sine)
        cos_one[:, cols] = cosine
        pre_two = jnp.dot(w_second_t, sine, precision=HIGHEST, preferred_element_type=jnp.float32)
        sine, cosine = sine_cosine(pre_two)
        act_two[:, cols] = stacked(sine)
        cos_two[:, cols] = cosine

    loop(0, 16, activations)
    w_copy.wait()
    met = jnp.concatenate([w_mine[...], w_theirs[...], jnp.zeros((112, 128), jnp.float32)], axis=0).T
    w_out_parts[...] = three_lanes(met[0:HID, 0:16])
    go_send[...] = jnp.zeros_like(go_send)
    pay[...] = jnp.zeros_like(pay)
    ch_send[...] = jnp.zeros_like(ch_send)

    def arrived1(i):
        peer = dp_peer(i)
        to_dp(send1.at[peer], recv1.at[peer], ssem1.at[peer], rsem1.at[peer], peer).wait_recv()

    loop(1, DP, arrived1)

    def pass_one(n):
        q0, lt = lax.div(n, 2), lax.rem(n, 2)
        half, k1 = lax.div(q0, 4), lax.rem(q0, 4)
        lanes = pl.ds(pl.multiple_of(k1 * 256 + lt * 128, 128), 128)
        out_lanes = pl.ds(pl.multiple_of(lt * 128, 128), 128)
        values = dft([(recv1[2 * q + half, 0, :, lanes], recv1[2 * q + half, 1, :, lanes]) for q in range(16)])
        for v1 in range(16):
            re, im = values[v1]
            if v1 > 0:
                c, s = first_ref[q0 * 32 + 2 * v1], first_ref[q0 * 32 + 2 * v1 + 1]
                re, im = re * c - im * s, re * s + im * c
            mid[v1, q0, 0, :, out_lanes] = re
            mid[v1, q0, 1, :, out_lanes] = im

    loop(0, 16, pass_one)

    def pass_two(n):
        v1, lt = lax.div(n, 2), lax.rem(n, 2)
        lanes = pl.ds(pl.multiple_of(lt * 128, 128), 128)
        im_lanes = pl.ds(pl.multiple_of(256 + lt * 128, 128), 128)
        values = dft([(mid[v1, q0, 0, :, lanes], mid[v1, q0, 1, :, lanes]) for q0 in range(8)])
        turned = []
        for v2 in range(8):
            re, im = values[v2]
            c = last_ref[0, v1, v2 : v2 + 1, lanes]
            s = last_ref[1, v1, v2 : v2 + 1, lanes]
            turned.append((re * c - im * s, re * s + im * c))
        for pair in range(4):
            rows = pl.ds(pl.multiple_of(v1 * 64 + pair * 16, 16), 16)
            for part, where in ((0, lanes), (1, im_lanes)):
                x = jnp.concatenate([turned[2 * pair][part], turned[2 * pair + 1][part]], axis=0)
                high, low = split(x)
                x_high[rows, where] = high
                x_low[rows, where] = low

    loop(0, 32, pass_two)

    def places(part, half, out):
        rows = pl.ds(pl.multiple_of(part * 512 + half * 256, 256), 256)
        high, low = x_high[rows, :], x_low[rows, :]
        y = dot(high, dft_high_ref[...], NN) + dot(high, dft_low_ref[...], NN) + dot(low, dft_high_ref[...], NN)
        y = y * window[rows, :]
        for v in range(32):
            lanes = 4096 * half + 128 * v
            out[:, lanes : lanes + 128] = y[8 * v : 8 * v + 8, :]

    halves = []
    for half in range(2):
        places(1 - core, half, send2)
        cols = slice(4096 * half, 4096 * half + 4096)
        halves.append(to_ch(send2.at[:, cols], recv2.at[:, cols], ssem2.at[half], rsem2.at[half], sibling))
        halves[half].start()
    for half in range(2):
        places(core, half, own2)

    def met_here(cols):
        return jnp.concatenate([own2[:, cols], recv2[:, cols]], axis=0)

    w_parts, second_parts = w_out_parts[...], w_second_parts[...]
    grad_second = jnp.zeros((2 * HID, 2 * HID), jnp.float32)
    grad_first = jnp.zeros((96, 2 * HID), jnp.float32)
    for j in range(8):
        cols = slice(1024 * j, 1024 * j + 1024)
        if j % 4 == 0:
            halves[j // 4].wait_recv()
        hidden = dot(w_parts, three_rows(met_here(cols)), NN)
        high, low = split(hidden * cos_two[:, cols])
        grad_second += dot(act_one[:, cols], jnp.concatenate([high, low], axis=0), NT)
        back_one = dot(second_parts, jnp.concatenate([high, low, high], axis=0), NN) * cos_one[:, cols]
        grad_first += dot(feats[:, cols], stacked(back_one), NT)
    grad_second = folded(grad_second, HID)
    grad_first = folded(grad_first, 48)
    pay[0:32, :] = jnp.concatenate([grad_second[0:32], grad_second[32:64]], axis=1)
    pay[32:48, :] = jnp.concatenate([grad_first[0:16], grad_first[16:32]], axis=1)
    pay[48:49, 0:HID] = grad_first[32:33]

    for i in range(DP):
        ar_send[i] = pay[2 * i : 2 * i + 2, :]

    def send_ar(i):
        peer = dp_peer(i)
        to_dp(ar_send.at[peer], ar_recv.at[me], ssem5.at[peer], rsem5.at[me], peer).start()

    loop(1, DP, send_ar, True)
    ar_recv[me] = ar_send[me]

    grad_out = jnp.zeros((2 * 16, 2 * HID), jnp.float32)
    for j in range(8):
        cols = slice(1024 * j, 1024 * j + 1024)
        grad_out += dot(stacked(met_here(cols)), act_two[:, cols], NT)
    go_send[:, :, 0:HID] = folded(grad_out, 16).reshape(2, 8, HID)
    go_copy = to_ch(go_send.at[1], go_recv, ssem3.at[0], rsem3.at[0], sibling)
    go_copy.start()
    go_copy.wait()
    total_out = go_send[0] + go_recv[...]
    go_sum[...] = total_out
    go_all[mine] = total_out

    ch_send[2:3, :] = jnp.sum(total_out * total_out, axis=0, keepdims=True)

    def arrived_ar(i):
        peer = dp_peer(i)
        to_dp(ar_send.at[peer], ar_recv.at[peer], ssem5.at[peer], rsem5.at[peer], peer).wait_recv()

    loop(1, DP, arrived_ar, True)
    ch_send[0:2, :] = jnp.sum(ar_recv[...], axis=0)

    def send_ch(i):
        peer = ch_peer(i)
        to_ch(ch_send, ch_recv.at[col], ssem6.at[peer], rsem6.at[col], peer).start()

    loop(1, CHAN, send_ch, True)
    ch_recv[col] = ch_send[...]

    def send_go_all(i):
        peer = dp_peer(i)
        to_dp(go_sum, go_all.at[mine], ssem4.at[peer], rsem4.at[me], peer).start()

    loop(1, DP, send_go_all)

    loop(1, DP, lambda i: sent_dp(i, send1.at[dp_peer(i)], recv1, ssem1, rsem1))
    for half in range(2):
        halves[half].wait_send()

    def arrived_ch(i):
        peer = ch_peer(i)
        to_ch(ch_send, ch_recv.at[peer], ssem6.at[peer], rsem6.at[peer], peer).wait_recv()

    loop(1, CHAN, arrived_ch, True)
    ag_send[...] = jnp.sum(ch_recv[...], axis=0)

    def send_ag(i):
        peer = dp_peer(i)
        to_dp(ag_send, ag_recv.at[me], ssem7.at[peer], rsem7.at[me], peer).start()

    loop(1, DP, send_ag, True)
    ag_recv[me] = ag_send[...]

    def sent_ch(i):
        peer = ch_peer(i)
        to_ch(ch_send, ch_recv.at[col], ssem6.at[peer], rsem6.at[col], peer).wait_send()

    loop(1, CHAN, sent_ch)
    loop(1, DP, lambda i: sent_dp(i, ar_send.at[dp_peer(i)], ar_recv, ssem5, rsem5))
    loop(1, DP, lambda i: sent_dp(i, go_sum, go_all, ssem4, rsem4))

    def arrived_go_all(i):
        peer = dp_peer(i)
        to_dp(go_sum, go_all.at[peer], ssem4.at[peer], rsem4.at[peer], peer).wait_recv()

    loop(1, DP, lambda i: sent_dp(i, ag_send, ag_recv, ssem7, rsem7))
    loop(1, DP, arrived_go_all)
    full_out = go_all[...].reshape(COLS, 128).T[0:HID, :]

    def arrived_ag(i):
        peer = dp_peer(i)
        to_dp(ag_send, ag_recv.at[peer], ssem7.at[peer], rsem7.at[peer], peer).wait_recv()

    loop(1, DP, arrived_ag, True)
    for i in range(DP):
        pay[2 * i : 2 * i + 2, :] = ag_recv[i, 0:2, :]
    second = pay[0:32, :]
    first = pay[32:48, :]
    line = pay[48:49, 0:HID]
    total = (
        jnp.sum(second * second, keepdims=True)
        + jnp.sum(first * first, keepdims=True)
        + jnp.sum(line * line, keepdims=True)
        + jnp.sum(jnp.sum(ag_recv[:, 2:3, :], axis=0), keepdims=True)
    )
    scale = jnp.minimum(1.0, clip_norm / (jnp.sqrt(total) + 1e-06))
    step_out_ref[...] = adam_step(full_out, w_out_ref[...], m_out_ref[0], m_out_ref[1], scale)
    for part in range(2):
        rows, lanes = slice(32 * part, 32 * part + 32), slice(HID * part, HID * part + HID)
        step_second_ref[rows, :] = adam_step(
            second[:, lanes], w_second_ref[rows, :], m_second_ref[0, rows, :], m_second_ref[1, rows, :], scale
        )
        rows = slice(16 * part + 1, 16 * part + 17)
        step_first_ref[rows, :] = adam_step(
            first[:, lanes], w_first_ref[rows, :], m_first_ref[rows, 0, :], m_first_ref[rows, 1, :], scale
        )
    step_first_ref[0:1, :] = adam_step(
        line, w_first_ref[0:1, :], m_first_ref[0:1, 0, :], m_first_ref[0:1, 1, :], scale
    )


def hand_over(*refs):
    sources, results, held, sems = refs[:3], refs[3:6], refs[6:9], refs[9]
    fetch = [pltpu.make_async_copy(sources[n], held[n], sems.at[0, n]) for n in range(3)]
    write = [pltpu.make_async_copy(held[n], results[n], sems.at[1, n]) for n in range(3)]
    for copy in fetch:
        copy.start()
    for n in range(3):
        fetch[n].wait()
        write[n].start()
    for copy in write:
        copy.wait()


def local(spec_u, spec_g, decay_length, w_first, w_second, w_out, moments_first, moments_second, moments_out):
    dft_high, dft_low, last, first = constants()
    f32, bf16 = jnp.float32, jnp.bfloat16
    vmem, sem = pltpu.VMEM, pltpu.SemaphoreType.DMA
    in_vmem = pl.BlockSpec(memory_space=pltpu.VMEM)
    anywhere = pl.BlockSpec(memory_space=pl.ANY)

    def pair(n):
        return [sem((n,)), sem((n,))]

    steps = pl.pallas_call(
        kernel,
        out_shape=(
            jax.ShapeDtypeStruct(w_first.shape, f32),
            jax.ShapeDtypeStruct(w_second.shape, f32),
            jax.ShapeDtypeStruct(w_out.shape, f32),
        ),
        in_specs=[anywhere] * 13,
        out_specs=(in_vmem,) * 3,
        scratch_shapes=[
            vmem((2, ROWS, COLS), f32), vmem((2, ROWS, COLS), f32), sem((4,)),
            vmem((1, COLS), f32), vmem((33, HID), f32), vmem((HID, HID), f32), vmem((HID, COLS), f32),
            vmem((33, 2, HID), f32), vmem((2, HID, HID), f32), vmem((2, HID, COLS), f32),
            vmem((512, 128), bf16), vmem((512, 128), bf16), vmem((2, 16, 8, 256), f32),
            pltpu.SMEM((256,), f32), sem((11,)),
            vmem((DP, 2, 8, ROWS), f32), vmem((DP, 2, 8, ROWS), f32), *pair(DP),
            vmem((16, 8, 2, 8, 256), f32), vmem((1024, 512), bf16), vmem((1024, 512), bf16),
            vmem((COLS, 128), f32), vmem((1024, 128), f32),
            vmem((128, 128), f32), vmem((COLS, 128), f32), vmem((8, 128), f32), vmem((8, 128), f32), *pair(1),
            vmem((HID, 48), bf16), vmem((HID, 192), bf16),
            vmem((96, 8192), bf16), vmem((128, 8192), bf16), vmem((HID, 8192), f32),
            vmem((128, 8192), bf16), vmem((HID, 8192), f32),
            vmem((8, 8192), f32), vmem((8, 8192), f32), vmem((8, 8192), f32), *pair(2),
            vmem((2, 8, 128), f32), vmem((8, 128), f32), *pair(1),
            vmem((8, 128), f32), vmem((DP, 8, 128), f32), *pair(DP),
            vmem((64, 128), f32), vmem((DP, 2, 128), f32), vmem((DP, 2, 128), f32), *pair(DP),
            vmem((4, 128), f32), vmem((CHAN, 4, 128), f32), *pair(CHAN),
            vmem((4, 128), f32), vmem((DP, 4, 128), f32), *pair(DP),
        ],
        compiler_params=pltpu.CompilerParams(
            collective_id=0, has_side_effects=True, vmem_limit_bytes=56 * 1024 * 1024
        ),
        name="hyena_step",
    )(
        spec_u, spec_g, decay_length.reshape(1, COLS), w_first, w_second, w_out,
        jnp.swapaxes(moments_first, 0, 1), moments_second, moments_out,
        jnp.asarray(dft_high), jnp.asarray(dft_low), jnp.asarray(last), jnp.asarray(first),
    )
    return pl.pallas_call(
        hand_over,
        out_shape=[jax.ShapeDtypeStruct(step.shape, f32) for step in steps],
        in_specs=[anywhere] * 3,
        out_specs=[anywhere] * 3,
        scratch_shapes=[vmem(step.shape, f32) for step in steps] + [sem((2, 3))],
        compiler_params=pltpu.CompilerParams(vmem_limit_bytes=56 * 1024 * 1024),
        name="hand_over",
    )(*steps)


def solution(mesh):
    return jax.shard_map(
        local,
        mesh=mesh,
        in_specs=(
            P(None, "dp", "chan"),
            P(None, "dp", "chan"),
            P("chan"),
            P(),
            P(),
            P(None, "chan"),
            P(),
            P(),
            P(None, None, "chan"),
        ),
        out_specs=(P(), P(), P(None, "chan")),
        check_vma=False,
    )
```

```python
import functools
import math

import jax
import jax.numpy as jnp
import numpy as np
from jax import lax
from jax.experimental import pallas as pl
from jax.experimental.pallas import tpu as pltpu
from jax.sharding import PartitionSpec as P

MESH = pl.DeviceIdType.MESH
HIGHEST = lax.Precision.HIGHEST

BANDS = 16
HID = 64
DP = 32
FREQS = 32768
SEQ = 16384
ROWS = 1024
COLS = 256

beta_one = 0.9
beta_two = 0.999
adam_count = 10.0
adam_eps = 1e-08
weight_decay = 0.1
clip_norm = 1.0


def adam_step(grad, weight, first, second, scale):
    g = grad * scale
    first = beta_one * first + (1.0 - beta_one) * g
    second = beta_two * second + (1.0 - beta_two) * g * g
    first_hat = first / (1.0 - beta_one**adam_count)
    second_hat = second / (1.0 - beta_two**adam_count)
    return first_hat / (jnp.sqrt(second_hat) + adam_eps) + weight_decay * weight


def split(x):
    high = x.astype(jnp.bfloat16)
    low = (x - high.astype(jnp.float32)).astype(jnp.bfloat16)
    return high, low


def dot(a, b, dims):
    return lax.dot_general(a, b, (dims, ((), ())), preferred_element_type=jnp.float32)


def stacked(x):
    return jnp.concatenate(split(x), axis=0)


def folded(x, rows):
    x = x[:rows] + x[rows:]
    return x[:, :HID] + x[:, HID:]


def three_rows(x):
    high, low = split(x)
    return jnp.concatenate([high, low, high], axis=0)


def three_lanes(x):
    high, low = split(x)
    return jnp.concatenate([high, high, low], axis=1)


def sine_cosine(x):
    turns = jnp.floor(x * (2.0 / math.pi) + 0.5)
    r = ((x - turns * 1.5703125) - turns * 4.837512969970703125e-4) - turns * 7.54978995489188216e-8
    z = r * r
    sine = r + r * z * (-1.6666654611e-1 + z * (8.3321608736e-3 - z * 1.9515295891e-4))
    cosine = 1.0 - 0.5 * z + z * z * (4.166664568298827e-2 + z * (-1.388731625493765e-3 + z * 2.443315711809948e-5))
    quarter = turns.astype(jnp.int32)
    odd = (quarter & 1) == 1
    first, second = jnp.where(odd, cosine, sine), jnp.where(odd, sine, cosine)
    return jnp.where((quarter & 2) == 2, -first, first), jnp.where(((quarter + 1) & 2) == 2, -second, second)


NN = ((1,), (0,))
NT = ((1,), (1,))


def times(z, angle_num, angle_den):
    re, im = z
    k = angle_num % angle_den
    if k == 0:
        return re, im
    if 4 * k == angle_den:
        return -im, re
    if 2 * k == angle_den:
        return -re, -im
    if 4 * k == 3 * angle_den:
        return im, -re
    if 8 * k == angle_den:
        r = math.sqrt(0.5)
        return (re - im) * r, (re + im) * r
    if 8 * k == 3 * angle_den:
        r = math.sqrt(0.5)
        return (re + im) * (-r), (re - im) * r
    c, s = math.cos(2 * math.pi * k / angle_den), math.sin(2 * math.pi * k / angle_den)
    return re * c - im * s, re * s + im * c


def dft(values):
    n = len(values)
    if n == 1:
        return values
    even, odd = dft(values[0::2]), dft(values[1::2])
    low, high = [], []
    for k in range(n // 2):
        t = times(odd[k], k, n)
        low.append((even[k][0] + t[0], even[k][1] + t[1]))
        high.append((even[k][0] - t[0], even[k][1] - t[1]))
    return low + high


def constants():
    lane = np.arange(256)[:, None] * np.arange(128)[None, :] % 256
    angle = 2.0 * np.pi / 256 * lane
    table = np.concatenate([np.cos(angle), -np.sin(angle)], axis=0).astype(np.float32)
    high = table.astype(jnp.bfloat16)
    low = (table - high.astype(np.float32)).astype(jnp.bfloat16)
    v = np.arange(16)[:, None] + 16 * np.arange(8)[None, :]
    angle = 2.0 * np.pi / FREQS * (v[:, :, None] * np.arange(256)[None, None, :])
    last = (np.stack([np.cos(angle), np.sin(angle)]) / FREQS).astype(np.float32)
    angle = 2.0 * np.pi / 128 * (np.arange(8)[:, None] * np.arange(16)[None, :])
    first = np.stack([np.cos(angle), np.sin(angle)], axis=-1).astype(np.float32)
    return high, low, last, first.reshape(-1)


def kernel(
    u_hbm, g_hbm, decay_hbm, w_first_hbm, w_second_hbm, w_out_hbm, m_first_hbm, m_second_hbm, m_out_hbm,
    dft_high_hbm, dft_low_hbm, last_hbm, first_hbm,
    step_first_ref, step_second_ref, step_out_ref,
    u_buf, g_buf, in_sem,
    decay_ref, w_first_ref, w_second_ref, w_out_ref, m_first_ref, m_second_ref, m_out_ref,
    dft_high_ref, dft_low_ref, last_ref, first_ref, small_sem,
    send1, recv1, ssem1, rsem1,
    mid, x_high, x_low, decay_rows, window,
    wf, w_rows, w_mine, w_theirs, ssem8, rsem8, w_out_parts, w_second_parts, feats, act_one, cos_one, act_two, cos_two,
    own2, send2, recv2, ssem2, rsem2,
    go_send, go_recv, ssem3, rsem3,
    go_sum, go_all, ssem4, rsem4,
    pay, ar_send, ar_recv, ssem5, rsem5,
    z_send, z_recv, ssem6, rsem6,
    y_send, y_recv, ssem9, rsem9,
    ag_send, ag_recv, ssem7, rsem7,
):
    me = lax.axis_index("dp")
    col = lax.axis_index("chan")

    def dp_peer(i):
        return lax.rem(me + i, DP)

    def chunk_of(device):
        return lax.rem(device, 2) * 16 + lax.div(device, 2)

    mine = chunk_of(me)
    z, x = lax.div(me, 4), lax.rem(me, 4)
    y, core = lax.div(col, 2), lax.rem(col, 2)
    member = 2 * x + core
    sibling = col + 1 - 2 * core

    def to_dp(src, dst, ssem, rsem, peer):
        return pltpu.make_async_remote_copy(
            src_ref=src, dst_ref=dst, send_sem=ssem, recv_sem=rsem, device_id=(peer, col), device_id_type=MESH
        )

    def to_member(src, dst, ssem, rsem, peer):
        return pltpu.make_async_remote_copy(
            src_ref=src, dst_ref=dst, send_sem=ssem, recv_sem=rsem,
            device_id=(4 * z + lax.div(peer, 2), 2 * y + lax.rem(peer, 2)), device_id_type=MESH,
        )

    def to_ch(src, dst, ssem, rsem, peer):
        return pltpu.make_async_remote_copy(
            src_ref=src, dst_ref=dst, send_sem=ssem, recv_sem=rsem, device_id=(me, peer), device_id_type=MESH
        )

    def loop(low, high, body, unroll=False):
        def wrapped(i, carry):
            body(i)
            return carry

        lax.fori_loop(low, high, wrapped, 0, unroll=unroll)

    def sent_dp(i, src, dst, ssem, rsem):
        peer = dp_peer(i)
        to_dp(src, dst.at[me], ssem.at[peer], rsem.at[me], peer).wait_send()

    def in_copy(block, which):
        hbm, buf = ((u_hbm, u_buf), (g_hbm, g_buf))[which]
        lanes = pl.ds(block * 128, 128)
        return pltpu.make_async_copy(hbm.at[:, :, lanes], buf.at[:, :, lanes], in_sem.at[2 * block + which])

    for block in range(2):
        for which in range(2):
            in_copy(block, which).start()

    small = [
        pltpu.make_async_copy(src, dst, small_sem.at[n])
        for n, (src, dst) in enumerate((
            (decay_hbm, decay_ref), (w_first_hbm, w_first_ref), (w_second_hbm, w_second_ref),
            (w_out_hbm, w_out_ref), (m_first_hbm, m_first_ref), (m_second_hbm, m_second_ref),
            (m_out_hbm, m_out_ref), (dft_high_hbm, dft_high_ref), (dft_low_hbm, dft_low_ref),
            (last_hbm, last_ref), (first_hbm, first_ref),
        ))
    ]

    barrier = pltpu.get_barrier_semaphore()

    def greet_dp(i):
        pl.semaphore_signal(barrier, inc=1, device_id=(dp_peer(i), col), device_id_type=MESH)

    def greet(dp, chan):
        pl.semaphore_signal(barrier, inc=1, device_id=(dp, chan), device_id_type=MESH)

    for i in sorted(range(1, DP), key=lambda i: -min(i, DP - i)):
        greet_dp(i)
    for i in (4, 3, 5, 2, 6, 1, 7):
        greet(me, 2 * lax.rem(y + i, 8) + core)
    for i in (2, 1, 3):
        greet(4 * z + lax.rem(x + i, 4), sibling)
    greet(me, sibling)

    for block in range(2):
        for which in range(2):
            in_copy(block, which).wait()

        def product(kt, block=block):
            rows = pl.ds(pl.multiple_of(kt * 128, 128), 128)
            lanes = pl.ds(block * 128, 128)
            u_re, u_im = u_buf[0, rows, lanes], u_buf[1, rows, lanes]
            g_re, g_im = g_buf[0, rows, lanes], g_buf[1, rows, lanes]
            re = g_re * u_re + g_im * u_im
            im = g_im * u_re - g_re * u_im
            owners = pl.ds(block * 16, 16)
            send1[owners, 0, :, rows] = re.T.reshape(16, 8, 128)
            send1[owners, 1, :, rows] = im.T.reshape(16, 8, 128)

        loop(0, ROWS // 128, product)
        if block == 0:
            pl.semaphore_wait(barrier, DP - 1 + 7 + 4)

        def send(i, block=block):
            n = lax.rem(lax.div(me, 2) + i, 16)
            peer = 2 * n + block

            @pl.when(peer != me)
            def _():
                to_dp(send1.at[block * 16 + n], recv1.at[me], ssem1.at[peer], rsem1.at[me], peer).start()

        loop(0, 16, send)
    for copy in small:
        copy.start()
    recv1[me] = send1[mine]
    for copy in small:
        copy.wait()

    decay_rows[...] = jnp.broadcast_to(decay_ref[...], (128, COLS)).T
    decay = decay_rows[pl.ds(pl.multiple_of(mine * 8, 8), 8), :]
    lane = lax.broadcasted_iota(jnp.int32, (8, 128), 1)

    def make_window(v):
        t = lax.div(v, 8) + 16 * lax.rem(v, 8) + 128 * lane
        window[pl.ds(pl.multiple_of(v * 8, 8), 8), :] = jnp.exp(-t.astype(jnp.float32) / decay)

    loop(0, 128, make_window)

    w_rows[:, 0:HID] = w_out_ref[...].T
    w_rows[:, HID:] = jnp.zeros((COLS, 128 - HID), jnp.float32)
    w_mine[...] = w_rows[pl.ds(pl.multiple_of(mine * 8, 8), 8), :]
    w_copy = to_ch(w_mine, w_theirs, ssem8.at[0], rsem8.at[0], sibling)
    w_copy.start()
    w_second_parts[...] = three_lanes(w_second_ref[...])

    wf[...] = jnp.zeros_like(wf)
    wf[0:32, 0:HID] = w_first_ref[1:33, :]
    wf[32:33, 0:HID] = w_first_ref[0:1, :]
    wf[HID:, 0:HID] = w_second_ref[...]
    turned = wf[...].T
    w_first_t, w_second_t = turned[0:HID, 0:48], turned[0:HID, HID:]

    def activations(n):
        cols = pl.ds(pl.multiple_of(n * 512, 512), 512)
        column = n * 512 + lax.broadcasted_iota(jnp.int32, (16, 512), 1)
        residue = column >> 7
        position = 8 * core + (residue >> 3) + 16 * (residue & 7) + 128 * (column & 127)
        band = lax.broadcasted_iota(jnp.int32, (16, 512), 0) + 1
        angle = 2.0 * math.pi / SEQ * ((band * position) & (SEQ - 1)).astype(jnp.float32)
        sine, cosine = sine_cosine(angle)
        ramp = jnp.where(band == 1, position.astype(jnp.float32) / SEQ, 0.0)
        values = jnp.concatenate([cosine, sine, ramp], axis=0)
        feats[:, cols] = stacked(values)
        pre_one = jnp.dot(w_first_t, values, precision=HIGHEST, preferred_element_type=jnp.float32)
        sine, cosine = sine_cosine(pre_one)
        act_one[:, cols] = stacked(sine)
        cos_one[:, cols] = cosine
        pre_two = jnp.dot(w_second_t, sine, precision=HIGHEST, preferred_element_type=jnp.float32)
        sine, cosine = sine_cosine(pre_two)
        act_two[:, cols] = stacked(sine)
        cos_two[:, cols] = cosine

    loop(0, 16, activations)
    w_copy.wait()
    met = jnp.concatenate([w_mine[...], w_theirs[...], jnp.zeros((112, 128), jnp.float32)], axis=0).T
    w_out_parts[...] = three_lanes(met[0:HID, 0:16])
    go_send[...] = jnp.zeros_like(go_send)
    ar_send[...] = jnp.zeros_like(ar_send)
    pay[...] = jnp.zeros_like(pay)

    def arrived1(i):
        peer = dp_peer(i)
        to_dp(send1.at[peer], recv1.at[peer], ssem1.at[peer], rsem1.at[peer], peer).wait_recv()

    loop(1, DP, arrived1, True)

    def pass_one(n):
        q0, lt = lax.div(n, 2), lax.rem(n, 2)
        half, k1 = lax.div(q0, 4), lax.rem(q0, 4)
        lanes = pl.ds(pl.multiple_of(k1 * 256 + lt * 128, 128), 128)
        out_lanes = pl.ds(pl.multiple_of(lt * 128, 128), 128)
        values = dft([(recv1[2 * q + half, 0, :, lanes], recv1[2 * q + half, 1, :, lanes]) for q in range(16)])
        for v1 in range(16):
            re, im = values[v1]
            if v1 > 0:
                c, s = first_ref[q0 * 32 + 2 * v1], first_ref[q0 * 32 + 2 * v1 + 1]
                re, im = re * c - im * s, re * s + im * c
            mid[v1, q0, 0, :, out_lanes] = re
            mid[v1, q0, 1, :, out_lanes] = im

    loop(0, 16, pass_one)

    def pass_two(n):
        v1, lt = lax.div(n, 2), lax.rem(n, 2)
        lanes = pl.ds(pl.multiple_of(lt * 128, 128), 128)
        im_lanes = pl.ds(pl.multiple_of(256 + lt * 128, 128), 128)
        values = dft([(mid[v1, q0, 0, :, lanes], mid[v1, q0, 1, :, lanes]) for q0 in range(8)])
        turned = []
        for v2 in range(8):
            re, im = values[v2]
            c = last_ref[0, v1, v2 : v2 + 1, lanes]
            s = last_ref[1, v1, v2 : v2 + 1, lanes]
            turned.append((re * c - im * s, re * s + im * c))
        for pair in range(4):
            rows = pl.ds(pl.multiple_of(v1 * 64 + pair * 16, 16), 16)
            for part, where in ((0, lanes), (1, im_lanes)):
                x = jnp.concatenate([turned[2 * pair][part], turned[2 * pair + 1][part]], axis=0)
                high, low = split(x)
                x_high[rows, where] = high
                x_low[rows, where] = low

    loop(0, 32, pass_two)

    def places(part, half, out):
        rows = pl.ds(pl.multiple_of(part * 512 + half * 256, 256), 256)
        high, low = x_high[rows, :], x_low[rows, :]
        y = dot(high, dft_high_ref[...], NN) + dot(high, dft_low_ref[...], NN) + dot(low, dft_high_ref[...], NN)
        y = y * window[rows, :]
        for v in range(32):
            lanes = 4096 * half + 128 * v
            out[:, lanes : lanes + 128] = y[8 * v : 8 * v + 8, :]

    halves = []
    for half in range(2):
        places(1 - core, half, send2)
        cols = slice(4096 * half, 4096 * half + 4096)
        halves.append(to_ch(send2.at[:, cols], recv2.at[:, cols], ssem2.at[half], rsem2.at[half], sibling))
        halves[half].start()
    for half in range(2):
        places(core, half, own2)

    def met_here(cols):
        return jnp.concatenate([own2[:, cols], recv2[:, cols]], axis=0)

    w_parts, second_parts = w_out_parts[...], w_second_parts[...]
    grad_second = jnp.zeros((2 * HID, 2 * HID), jnp.float32)
    grad_first = jnp.zeros((96, 2 * HID), jnp.float32)
    for j in range(8):
        cols = slice(1024 * j, 1024 * j + 1024)
        if j % 4 == 0:
            halves[j // 4].wait_recv()
        hidden = dot(w_parts, three_rows(met_here(cols)), NN)
        high, low = split(hidden * cos_two[:, cols])
        grad_second += dot(act_one[:, cols], jnp.concatenate([high, low], axis=0), NT)
        back_one = dot(second_parts, jnp.concatenate([high, low, high], axis=0), NN) * cos_one[:, cols]
        grad_first += dot(feats[:, cols], stacked(back_one), NT)
    grad_second = folded(grad_second, HID)
    grad_first = folded(grad_first, 48)

    pay[0:32, :] = jnp.concatenate([grad_second[0:32], grad_second[32:64]], axis=1)
    pay[32:48, :] = jnp.concatenate([grad_first[0:16], grad_first[16:32]], axis=1)
    pay[48:49, 0:HID] = grad_first[32:33]
    for i in range(8):
        ar_send[i, 0:7, :] = pay[7 * i : 7 * i + 7, :]

    def ring(i, at):
        return lax.rem(at + i, 8)

    def add_copy(i):
        peer = ring(i, member)
        return to_member(ar_send.at[peer], ar_recv.at[member], ssem5.at[peer], rsem5.at[member], peer)

    def add_arrival(i):
        peer = ring(i, member)
        return to_member(ar_send.at[peer], ar_recv.at[peer], ssem5.at[peer], rsem5.at[peer], peer)

    def z_copy(i):
        peer = ring(i, z)
        return to_dp(z_send, z_recv.at[z], ssem6.at[peer], rsem6.at[z], 4 * peer + x)

    def z_arrival(i):
        peer = ring(i, z)
        return to_dp(z_send, z_recv.at[peer], ssem6.at[peer], rsem6.at[peer], 4 * peer + x)

    def y_copy(i):
        peer = ring(i, y)
        return to_ch(y_send, y_recv.at[y], ssem9.at[peer], rsem9.at[y], 2 * peer + core)

    def y_arrival(i):
        peer = ring(i, y)
        return to_ch(y_send, y_recv.at[peer], ssem9.at[peer], rsem9.at[peer], 2 * peer + core)

    def share_copy(i):
        peer = ring(i, member)
        return to_member(ag_send, ag_recv.at[member], ssem7.at[peer], rsem7.at[member], peer)

    def share_arrival(i):
        peer = ring(i, member)
        return to_member(ag_send, ag_recv.at[peer], ssem7.at[peer], rsem7.at[peer], peer)

    others = (4, 3, 5, 2, 6, 1, 7)
    for i in others:
        add_copy(i).start()
    ar_recv[member] = ar_send[member]

    grad_out = jnp.zeros((2 * 16, 2 * HID), jnp.float32)
    for j in range(8):
        cols = slice(1024 * j, 1024 * j + 1024)
        grad_out += dot(stacked(met_here(cols)), act_two[:, cols], NT)
    go_send[:, :, 0:HID] = folded(grad_out, 16).reshape(2, 8, HID)
    go_copy = to_ch(go_send.at[1], go_recv, ssem3.at[0], rsem3.at[0], sibling)
    go_copy.start()
    go_copy.wait()
    total_out = go_send[0] + go_recv[...]
    go_sum[...] = total_out
    go_all[mine] = total_out


    for i in others:
        add_arrival(i).wait_recv()
    z_send[...] = jnp.sum(ar_recv[...], axis=0)
    z_send[7:8, :] = jnp.sum(total_out * total_out, axis=0, keepdims=True)
    for i in others:
        z_copy(i).start()
    z_recv[z] = z_send[...]

    def send_go_all(i):
        peer = dp_peer(i)
        to_dp(go_sum, go_all.at[mine], ssem4.at[peer], rsem4.at[me], peer).start()

    loop(1, DP, send_go_all)

    loop(1, DP, lambda i: sent_dp(i, send1.at[dp_peer(i)], recv1, ssem1, rsem1))
    for half in range(2):
        halves[half].wait_send()

    for i in others:
        z_arrival(i).wait_recv()
    y_send[...] = jnp.sum(z_recv[...], axis=0)
    for i in others:
        y_copy(i).start()
    y_recv[y] = y_send[...]
    for i in others:
        add_copy(i).wait_send()
        z_copy(i).wait_send()
    for i in others:
        y_arrival(i).wait_recv()
    ag_send[...] = jnp.sum(y_recv[...], axis=0)
    for i in others:
        share_copy(i).start()
    ag_recv[member] = ag_send[...]
    for i in others:
        y_copy(i).wait_send()
        share_copy(i).wait_send()
    loop(1, DP, lambda i: sent_dp(i, go_sum, go_all, ssem4, rsem4))

    def arrived_go_all(i):
        peer = dp_peer(i)
        to_dp(go_sum, go_all.at[peer], ssem4.at[peer], rsem4.at[peer], peer).wait_recv()

    loop(1, DP, arrived_go_all)
    full_out = go_all[...].reshape(COLS, 128).T[0:HID, :]

    for i in others:
        share_arrival(i).wait_recv()
    blocks = ag_recv[...]
    squares = jnp.sum(jnp.sum(blocks * blocks, axis=0)[0:7], axis=0, keepdims=True)
    squares += jnp.sum(blocks, axis=0)[7:8]
    total = jnp.sum(squares, axis=1, keepdims=True)
    scale = jnp.minimum(1.0, clip_norm / (jnp.sqrt(total) + 1e-06))
    for i in range(7):
        pay[7 * i : 7 * i + 7, :] = ag_recv[i, 0:7, :]
    second = pay[0:32, :]
    first = pay[32:48, :]
    line = pay[48:49, 0:HID]
    step_out_ref[...] = adam_step(full_out, w_out_ref[...], m_out_ref[0], m_out_ref[1], scale)
    for part in range(2):
        rows, lanes = slice(32 * part, 32 * part + 32), slice(HID * part, HID * part + HID)
        step_second_ref[rows, :] = adam_step(
            second[:, lanes], w_second_ref[rows, :], m_second_ref[0, rows, :], m_second_ref[1, rows, :], scale
        )
        rows = slice(16 * part + 1, 16 * part + 17)
        step_first_ref[rows, :] = adam_step(
            first[:, lanes], w_first_ref[rows, :], m_first_ref[rows, 0, :], m_first_ref[rows, 1, :], scale
        )
    step_first_ref[0:1, :] = adam_step(
        line, w_first_ref[0:1, :], m_first_ref[0:1, 0, :], m_first_ref[0:1, 1, :], scale
    )


def hand_over(*refs):
    sources, results, held, sems = refs[:3], refs[3:6], refs[6:9], refs[9]
    fetch = [pltpu.make_async_copy(sources[n], held[n], sems.at[0, n]) for n in range(3)]
    write = [pltpu.make_async_copy(held[n], results[n], sems.at[1, n]) for n in range(3)]
    for copy in fetch:
        copy.start()
    for n in range(3):
        fetch[n].wait()
        write[n].start()
    for copy in write:
        copy.wait()


def local(spec_u, spec_g, decay_length, w_first, w_second, w_out, moments_first, moments_second, moments_out):
    dft_high, dft_low, last, first = constants()
    f32, bf16 = jnp.float32, jnp.bfloat16
    vmem, sem = pltpu.VMEM, pltpu.SemaphoreType.DMA
    in_vmem = pl.BlockSpec(memory_space=pltpu.VMEM)
    anywhere = pl.BlockSpec(memory_space=pl.ANY)

    def pair(n):
        return [sem((n,)), sem((n,))]

    steps = pl.pallas_call(
        kernel,
        out_shape=(
            jax.ShapeDtypeStruct(w_first.shape, f32),
            jax.ShapeDtypeStruct(w_second.shape, f32),
            jax.ShapeDtypeStruct(w_out.shape, f32),
        ),
        in_specs=[anywhere] * 13,
        out_specs=(in_vmem,) * 3,
        scratch_shapes=[
            vmem((2, ROWS, COLS), f32), vmem((2, ROWS, COLS), f32), sem((4,)),
            vmem((1, COLS), f32), vmem((33, HID), f32), vmem((HID, HID), f32), vmem((HID, COLS), f32),
            vmem((33, 2, HID), f32), vmem((2, HID, HID), f32), vmem((2, HID, COLS), f32),
            vmem((512, 128), bf16), vmem((512, 128), bf16), vmem((2, 16, 8, 256), f32),
            pltpu.SMEM((256,), f32), sem((11,)),
            vmem((DP, 2, 8, ROWS), f32), vmem((DP, 2, 8, ROWS), f32), *pair(DP),
            vmem((16, 8, 2, 8, 256), f32), vmem((1024, 512), bf16), vmem((1024, 512), bf16),
            vmem((COLS, 128), f32), vmem((1024, 128), f32),
            vmem((128, 128), f32), vmem((COLS, 128), f32), vmem((8, 128), f32), vmem((8, 128), f32), *pair(1),
            vmem((HID, 48), bf16), vmem((HID, 192), bf16),
            vmem((96, 8192), bf16), vmem((128, 8192), bf16), vmem((HID, 8192), f32),
            vmem((128, 8192), bf16), vmem((HID, 8192), f32),
            vmem((8, 8192), f32), vmem((8, 8192), f32), vmem((8, 8192), f32), *pair(2),
            vmem((2, 8, 128), f32), vmem((8, 128), f32), *pair(1),
            vmem((8, 128), f32), vmem((DP, 8, 128), f32), *pair(DP),
            vmem((64, 128), f32), vmem((8, 8, 128), f32), vmem((8, 8, 128), f32), *pair(8),
            vmem((8, 128), f32), vmem((8, 8, 128), f32), *pair(8),
            vmem((8, 128), f32), vmem((8, 8, 128), f32), *pair(8),
            vmem((8, 128), f32), vmem((8, 8, 128), f32), *pair(8),
        ],
        compiler_params=pltpu.CompilerParams(
            collective_id=0, has_side_effects=True, vmem_limit_bytes=56 * 1024 * 1024
        ),
        name="hyena_step",
    )(
        spec_u, spec_g, decay_length.reshape(1, COLS), w_first, w_second, w_out,
        jnp.swapaxes(moments_first, 0, 1), moments_second, moments_out,
        jnp.asarray(dft_high), jnp.asarray(dft_low), jnp.asarray(last), jnp.asarray(first),
    )
    return pl.pallas_call(
        hand_over,
        out_shape=[jax.ShapeDtypeStruct(step.shape, f32) for step in steps],
        in_specs=[anywhere] * 3,
        out_specs=[anywhere] * 3,
        scratch_shapes=[vmem(step.shape, f32) for step in steps] + [sem((2, 3))],
        compiler_params=pltpu.CompilerParams(vmem_limit_bytes=56 * 1024 * 1024),
        name="hand_over",
    )(*steps)


def solution(mesh):
    return jax.shard_map(
        local,
        mesh=mesh,
        in_specs=(
            P(None, "dp", "chan"),
            P(None, "dp", "chan"),
            P("chan"),
            P(),
            P(),
            P(None, "chan"),
            P(),
            P(),
            P(None, None, "chan"),
        ),
        out_specs=(P(), P(), P(None, "chan")),
        check_vma=False,
    )
```

```python
import functools
import math

import jax
import jax.numpy as jnp
import numpy as np
from jax import lax
from jax.experimental import pallas as pl
from jax.experimental.pallas import tpu as pltpu
from jax.sharding import PartitionSpec as P

MESH = pl.DeviceIdType.MESH
HIGHEST = lax.Precision.HIGHEST

BANDS = 16
HID = 64
DP = 32
FREQS = 32768
SEQ = 16384
ROWS = 1024
COLS = 256

beta_one = 0.9
beta_two = 0.999
adam_count = 10.0
adam_eps = 1e-08
weight_decay = 0.1
clip_norm = 1.0


def adam_step(grad, weight, first, second, scale):
    g = grad * scale
    first = beta_one * first + (1.0 - beta_one) * g
    second = beta_two * second + (1.0 - beta_two) * g * g
    first_hat = first / (1.0 - beta_one**adam_count)
    second_hat = second / (1.0 - beta_two**adam_count)
    return first_hat / (jnp.sqrt(second_hat) + adam_eps) + weight_decay * weight


def split(x):
    high = x.astype(jnp.bfloat16)
    low = (x - high.astype(jnp.float32)).astype(jnp.bfloat16)
    return high, low


def dot(a, b, dims):
    return lax.dot_general(a, b, (dims, ((), ())), preferred_element_type=jnp.float32)


def stacked(x):
    return jnp.concatenate(split(x), axis=0)


def folded(x, rows):
    x = x[:rows] + x[rows:]
    return x[:, :HID] + x[:, HID:]


def three_rows(x):
    high, low = split(x)
    return jnp.concatenate([high, low, high], axis=0)


def three_lanes(x):
    high, low = split(x)
    return jnp.concatenate([high, high, low], axis=1)


def sine_cosine(x):
    turns = jnp.floor(x * (2.0 / math.pi) + 0.5)
    r = ((x - turns * 1.5703125) - turns * 4.837512969970703125e-4) - turns * 7.54978995489188216e-8
    z = r * r
    sine = r + r * z * (-1.6666654611e-1 + z * (8.3321608736e-3 - z * 1.9515295891e-4))
    cosine = 1.0 - 0.5 * z + z * z * (4.166664568298827e-2 + z * (-1.388731625493765e-3 + z * 2.443315711809948e-5))
    quarter = turns.astype(jnp.int32)
    odd = (quarter & 1) == 1
    first, second = jnp.where(odd, cosine, sine), jnp.where(odd, sine, cosine)
    return jnp.where((quarter & 2) == 2, -first, first), jnp.where(((quarter + 1) & 2) == 2, -second, second)


NN = ((1,), (0,))
NT = ((1,), (1,))


def times(z, angle_num, angle_den):
    re, im = z
    k = angle_num % angle_den
    if k == 0:
        return re, im
    if 4 * k == angle_den:
        return -im, re
    if 2 * k == angle_den:
        return -re, -im
    if 4 * k == 3 * angle_den:
        return im, -re
    if 8 * k == angle_den:
        r = math.sqrt(0.5)
        return (re - im) * r, (re + im) * r
    if 8 * k == 3 * angle_den:
        r = math.sqrt(0.5)
        return (re + im) * (-r), (re - im) * r
    c, s = math.cos(2 * math.pi * k / angle_den), math.sin(2 * math.pi * k / angle_den)
    return re * c - im * s, re * s + im * c


def dft(values):
    n = len(values)
    if n == 1:
        return values
    even, odd = dft(values[0::2]), dft(values[1::2])
    low, high = [], []
    for k in range(n // 2):
        t = times(odd[k], k, n)
        low.append((even[k][0] + t[0], even[k][1] + t[1]))
        high.append((even[k][0] - t[0], even[k][1] - t[1]))
    return low + high


def constants():
    lane = np.arange(256)[:, None] * np.arange(128)[None, :] % 256
    angle = 2.0 * np.pi / 256 * lane
    table = np.concatenate([np.cos(angle), -np.sin(angle)], axis=0).astype(np.float32)
    high = table.astype(jnp.bfloat16)
    low = (table - high.astype(np.float32)).astype(jnp.bfloat16)
    v = np.arange(16)[:, None] + 16 * np.arange(8)[None, :]
    angle = 2.0 * np.pi / FREQS * (v[:, :, None] * np.arange(256)[None, None, :])
    last = (np.stack([np.cos(angle), np.sin(angle)]) / FREQS).astype(np.float32)
    angle = 2.0 * np.pi / 128 * (np.arange(8)[:, None] * np.arange(16)[None, :])
    first = np.stack([np.cos(angle), np.sin(angle)], axis=-1).astype(np.float32)
    return np.concatenate([high, low], axis=1), last, first.reshape(-1)


def kernel(
    u_hbm, g_hbm, decay_hbm, w_first_hbm, w_second_hbm, w_out_hbm, m_first_hbm, m_second_hbm, m_out_hbm,
    dft_hbm, last_hbm, first_hbm,
    step_first_ref, step_second_ref, step_out_ref,
    u_buf, g_buf, in_sem,
    decay_ref, w_first_ref, w_second_ref, w_out_ref, m_first_ref, m_second_ref, m_out_ref,
    dft_ref, last_ref, first_ref, small_sem,
    send1, recv1, ssem1, rsem1,
    mid, x_high, x_low, decay_rows, window,
    wf, w_rows, w_mine, w_theirs, ssem8, rsem8, w_out_parts, w_second_parts, feats, act_one, cos_one, act_two, cos_two,
    own2, send2, recv2, ssem2, rsem2,
    go_send, go_recv, ssem3, rsem3,
    go_sum, go_all, ssem4, rsem4,
    pay, ar_send, ar_recv, ssem5, rsem5,
    z_send, z_recv, ssem6, rsem6,
    y_send, y_recv, ssem9, rsem9,
    ag_send, ag_recv, ssem7, rsem7,
):
    me = lax.axis_index("dp")
    col = lax.axis_index("chan")

    def dp_peer(i):
        return lax.rem(me + i, DP)

    def chunk_of(device):
        return lax.rem(device, 2) * 16 + lax.div(device, 2)

    mine = chunk_of(me)
    z, x = lax.div(me, 4), lax.rem(me, 4)
    y, core = lax.div(col, 2), lax.rem(col, 2)
    member = 2 * x + core
    sibling = col + 1 - 2 * core

    def to_dp(src, dst, ssem, rsem, peer):
        return pltpu.make_async_remote_copy(
            src_ref=src, dst_ref=dst, send_sem=ssem, recv_sem=rsem, device_id=(peer, col), device_id_type=MESH
        )

    def to_member(src, dst, ssem, rsem, peer):
        return pltpu.make_async_remote_copy(
            src_ref=src, dst_ref=dst, send_sem=ssem, recv_sem=rsem,
            device_id=(4 * z + lax.div(peer, 2), 2 * y + lax.rem(peer, 2)), device_id_type=MESH,
        )

    def to_ch(src, dst, ssem, rsem, peer):
        return pltpu.make_async_remote_copy(
            src_ref=src, dst_ref=dst, send_sem=ssem, recv_sem=rsem, device_id=(me, peer), device_id_type=MESH
        )

    def loop(low, high, body, unroll=False):
        def wrapped(i, carry):
            body(i)
            return carry

        lax.fori_loop(low, high, wrapped, 0, unroll=unroll)

    def sent_dp(i, src, dst, ssem, rsem):
        peer = dp_peer(i)
        to_dp(src, dst.at[me], ssem.at[peer], rsem.at[me], peer).wait_send()

    def in_copy(block, which):
        hbm, buf = ((u_hbm, u_buf), (g_hbm, g_buf))[which]
        lanes = pl.ds(block * 128, 128)
        return pltpu.make_async_copy(hbm.at[:, :, lanes], buf.at[:, :, lanes], in_sem.at[2 * block + which])

    for block in range(2):
        for which in range(2):
            in_copy(block, which).start()

    small = [
        pltpu.make_async_copy(src, dst, small_sem.at[n])
        for n, (src, dst) in enumerate((
            (decay_hbm, decay_ref), (w_first_hbm, w_first_ref), (w_second_hbm, w_second_ref),
            (w_out_hbm, w_out_ref), (m_first_hbm, m_first_ref), (m_second_hbm, m_second_ref),
            (m_out_hbm, m_out_ref), (dft_hbm, dft_ref),
            (last_hbm, last_ref), (first_hbm, first_ref),
        ))
    ]

    barrier = pltpu.get_barrier_semaphore()

    def greet_dp(i):
        pl.semaphore_signal(barrier, inc=1, device_id=(dp_peer(i), col), device_id_type=MESH)

    def greet(dp, chan):
        pl.semaphore_signal(barrier, inc=1, device_id=(dp, chan), device_id_type=MESH)

    for i in sorted(range(1, DP), key=lambda i: -min(i, DP - i)):
        greet_dp(i)
    for i in (4, 3, 5, 2, 6, 1, 7):
        greet(me, 2 * lax.rem(y + i, 8) + core)
    for i in (2, 1, 3):
        greet(4 * z + lax.rem(x + i, 4), sibling)
    greet(me, sibling)

    for block in range(2):
        for which in range(2):
            in_copy(block, which).wait()

        def product(kt, block=block):
            rows = pl.ds(pl.multiple_of(kt * 128, 128), 128)
            lanes = pl.ds(block * 128, 128)
            u_re, u_im = u_buf[0, rows, lanes], u_buf[1, rows, lanes]
            g_re, g_im = g_buf[0, rows, lanes], g_buf[1, rows, lanes]
            re = g_re * u_re + g_im * u_im
            im = g_im * u_re - g_re * u_im
            owners = pl.ds(block * 16, 16)
            send1[owners, 0, :, rows] = re.T.reshape(16, 8, 128)
            send1[owners, 1, :, rows] = im.T.reshape(16, 8, 128)

        loop(0, ROWS // 128, product)
        if block == 0:
            pl.semaphore_wait(barrier, DP - 1 + 7 + 4)

        def send(i, block=block):
            n = lax.rem(lax.div(me, 2) + i, 16)
            peer = 2 * n + block

            @pl.when(peer != me)
            def _():
                to_dp(send1.at[block * 16 + n], recv1.at[me], ssem1.at[peer], rsem1.at[me], peer).start()

        loop(0, 16, send)
    for copy in small:
        copy.start()
    recv1[me] = send1[mine]
    for copy in small:
        copy.wait()

    decay_rows[...] = jnp.broadcast_to(decay_ref[...], (128, COLS)).T
    decay = decay_rows[pl.ds(pl.multiple_of(mine * 8, 8), 8), :]
    lane = lax.broadcasted_iota(jnp.int32, (8, 128), 1)

    def make_window(v):
        t = lax.div(v, 8) + 16 * lax.rem(v, 8) + 128 * lane
        window[pl.ds(pl.multiple_of(v * 8, 8), 8), :] = jnp.exp(-t.astype(jnp.float32) / decay)

    loop(0, 128, make_window)

    w_rows[:, 0:HID] = w_out_ref[...].T
    w_rows[:, HID:] = jnp.zeros((COLS, 128 - HID), jnp.float32)
    w_mine[...] = w_rows[pl.ds(pl.multiple_of(mine * 8, 8), 8), :]
    w_copy = to_ch(w_mine, w_theirs, ssem8.at[0], rsem8.at[0], sibling)
    w_copy.start()
    w_second_parts[...] = three_lanes(w_second_ref[...])

    wf[...] = jnp.zeros_like(wf)
    wf[0:32, 0:HID] = w_first_ref[1:33, :]
    wf[32:33, 0:HID] = w_first_ref[0:1, :]
    wf[HID:, 0:HID] = w_second_ref[...]
    turned = wf[...].T
    w_first_t, w_second_t = turned[0:HID, 0:48], turned[0:HID, HID:]

    def activations(n):
        cols = pl.ds(pl.multiple_of(n * 512, 512), 512)
        column = n * 512 + lax.broadcasted_iota(jnp.int32, (16, 512), 1)
        residue = column >> 7
        position = 8 * core + (residue >> 3) + 16 * (residue & 7) + 128 * (column & 127)
        band = lax.broadcasted_iota(jnp.int32, (16, 512), 0) + 1
        angle = 2.0 * math.pi / SEQ * ((band * position) & (SEQ - 1)).astype(jnp.float32)
        sine, cosine = sine_cosine(angle)
        ramp = jnp.where(band == 1, position.astype(jnp.float32) / SEQ, 0.0)
        values = jnp.concatenate([cosine, sine, ramp], axis=0)
        feats[:, cols] = stacked(values)
        pre_one = jnp.dot(w_first_t, values, precision=HIGHEST, preferred_element_type=jnp.float32)
        sine, cosine = sine_cosine(pre_one)
        act_one[:, cols] = stacked(sine)
        cos_one[:, cols] = cosine
        pre_two = jnp.dot(w_second_t, sine, precision=HIGHEST, preferred_element_type=jnp.float32)
        sine, cosine = sine_cosine(pre_two)
        act_two[:, cols] = stacked(sine)
        cos_two[:, cols] = cosine

    loop(0, 16, activations)
    w_copy.wait()
    met = jnp.concatenate([w_mine[...], w_theirs[...], jnp.zeros((112, 128), jnp.float32)], axis=0).T
    w_out_parts[...] = three_lanes(met[0:HID, 0:16])
    go_send[...] = jnp.zeros_like(go_send)
    ar_send[...] = jnp.zeros_like(ar_send)
    pay[...] = jnp.zeros_like(pay)

    def arrived1(i):
        peer = dp_peer(i)
        to_dp(send1.at[peer], recv1.at[peer], ssem1.at[peer], rsem1.at[peer], peer).wait_recv()

    loop(1, DP, arrived1, True)

    def pass_one(n):
        q0, lt = lax.div(n, 2), lax.rem(n, 2)
        half, k1 = lax.div(q0, 4), lax.rem(q0, 4)
        lanes = pl.ds(pl.multiple_of(k1 * 256 + lt * 128, 128), 128)
        out_lanes = pl.ds(pl.multiple_of(lt * 128, 128), 128)
        values = dft([(recv1[2 * q + half, 0, :, lanes], recv1[2 * q + half, 1, :, lanes]) for q in range(16)])
        for v1 in range(16):
            re, im = values[v1]
            if v1 > 0:
                c, s = first_ref[q0 * 32 + 2 * v1], first_ref[q0 * 32 + 2 * v1 + 1]
                re, im = re * c - im * s, re * s + im * c
            mid[v1, q0, 0, :, out_lanes] = re
            mid[v1, q0, 1, :, out_lanes] = im

    loop(0, 16, pass_one)

    def pass_two(n):
        v1, lt = lax.div(n, 2), lax.rem(n, 2)
        lanes = pl.ds(pl.multiple_of(lt * 128, 128), 128)
        im_lanes = pl.ds(pl.multiple_of(256 + lt * 128, 128), 128)
        values = dft([(mid[v1, q0, 0, :, lanes], mid[v1, q0, 1, :, lanes]) for q0 in range(8)])
        turned = []
        last_cos, last_sin = last_ref[0, v1, :, lanes], last_ref[1, v1, :, lanes]
        for v2 in range(8):
            re, im = values[v2]
            c, s = last_cos[v2 : v2 + 1], last_sin[v2 : v2 + 1]
            turned.append((re * c - im * s, re * s + im * c))
        for pair in range(4):
            rows = pl.ds(pl.multiple_of(v1 * 64 + pair * 16, 16), 16)
            for part, where in ((0, lanes), (1, im_lanes)):
                x = jnp.concatenate([turned[2 * pair][part], turned[2 * pair + 1][part]], axis=0)
                high, low = split(x)
                x_high[rows, where] = high
                x_low[rows, where] = low

    loop(0, 32, pass_two)

    def places(part, half, out):
        rows = pl.ds(pl.multiple_of(part * 512 + half * 256, 256), 256)
        high, low = x_high[rows, :], x_low[rows, :]
        both = dot(high, dft_ref[...], NN)
        y = both[:, :128] + both[:, 128:] + dot(low, dft_ref[:, :128], NN)
        y = y * window[rows, :]
        for v in range(32):
            lanes = 4096 * half + 128 * v
            out[:, lanes : lanes + 128] = y[8 * v : 8 * v + 8, :]

    halves = []
    for half in range(2):
        places(1 - core, half, send2)
        cols = slice(4096 * half, 4096 * half + 4096)
        halves.append(to_ch(send2.at[:, cols], recv2.at[:, cols], ssem2.at[half], rsem2.at[half], sibling))
        halves[half].start()
    for half in range(2):
        places(core, half, own2)

    def met_here(cols):
        return jnp.concatenate([own2[:, cols], recv2[:, cols]], axis=0)

    w_parts, second_parts = w_out_parts[...], w_second_parts[...]
    grad_second = jnp.zeros((2 * HID, 2 * HID), jnp.float32)
    grad_first = jnp.zeros((96, 2 * HID), jnp.float32)
    for j in range(8):
        cols = slice(1024 * j, 1024 * j + 1024)
        if j % 4 == 0:
            halves[j // 4].wait_recv()
        hidden = dot(w_parts, three_rows(met_here(cols)), NN)
        high, low = split(hidden * cos_two[:, cols])
        grad_second += dot(act_one[:, cols], jnp.concatenate([high, low], axis=0), NT)
        back_one = dot(second_parts, jnp.concatenate([high, low, high], axis=0), NN) * cos_one[:, cols]
        grad_first += dot(feats[:, cols], stacked(back_one), NT)
    grad_second = folded(grad_second, HID)
    grad_first = folded(grad_first, 48)

    pay[0:32, :] = jnp.concatenate([grad_second[0:32], grad_second[32:64]], axis=1)
    pay[32:48, :] = jnp.concatenate([grad_first[0:16], grad_first[16:32]], axis=1)
    pay[48:49, 0:HID] = grad_first[32:33]
    for i in range(8):
        ar_send[i, 0:7, :] = pay[7 * i : 7 * i + 7, :]

    def ring(i, at):
        return lax.rem(at + i, 8)

    def add_copy(i):
        peer = ring(i, member)
        return to_member(ar_send.at[peer], ar_recv.at[member], ssem5.at[peer], rsem5.at[member], peer)

    def add_arrival(i):
        peer = ring(i, member)
        return to_member(ar_send.at[peer], ar_recv.at[peer], ssem5.at[peer], rsem5.at[peer], peer)

    def z_copy(i):
        peer = ring(i, z)
        return to_dp(z_send, z_recv.at[z], ssem6.at[peer], rsem6.at[z], 4 * peer + x)

    def z_arrival(i):
        peer = ring(i, z)
        return to_dp(z_send, z_recv.at[peer], ssem6.at[peer], rsem6.at[peer], 4 * peer + x)

    def y_copy(i):
        peer = ring(i, y)
        return to_ch(y_send, y_recv.at[y], ssem9.at[peer], rsem9.at[y], 2 * peer + core)

    def y_arrival(i):
        peer = ring(i, y)
        return to_ch(y_send, y_recv.at[peer], ssem9.at[peer], rsem9.at[peer], 2 * peer + core)

    def share_copy(i):
        peer = ring(i, member)
        return to_member(ag_send, ag_recv.at[member], ssem7.at[peer], rsem7.at[member], peer)

    def share_arrival(i):
        peer = ring(i, member)
        return to_member(ag_send, ag_recv.at[peer], ssem7.at[peer], rsem7.at[peer], peer)

    others = (4, 3, 5, 2, 6, 1, 7)
    for i in others:
        add_copy(i).start()
    ar_recv[member] = ar_send[member]

    grad_out = jnp.zeros((2 * 16, 2 * HID), jnp.float32)
    for j in range(8):
        cols = slice(1024 * j, 1024 * j + 1024)
        grad_out += dot(stacked(met_here(cols)), act_two[:, cols], NT)
    go_send[:, :, 0:HID] = folded(grad_out, 16).reshape(2, 8, HID)
    go_copy = to_ch(go_send.at[1], go_recv, ssem3.at[0], rsem3.at[0], sibling)
    go_copy.start()
    go_copy.wait()
    total_out = go_send[0] + go_recv[...]
    go_sum[...] = total_out
    go_all[mine] = total_out


    for i in others:
        add_arrival(i).wait_recv()
    out_squares = jnp.sum(total_out * total_out, axis=0, keepdims=True)
    row = lax.broadcasted_iota(jnp.int32, (8, 128), 0)
    z_send[...] = jnp.where(row == 7, out_squares, jnp.sum(ar_recv[...], axis=0))
    for i in others:
        z_copy(i).start()
    z_recv[z] = z_send[...]

    loop(1, DP, lambda i: sent_dp(i, send1.at[dp_peer(i)], recv1, ssem1, rsem1))
    for half in range(2):
        halves[half].wait_send()

    for i in others:
        z_arrival(i).wait_recv()
    y_send[...] = jnp.sum(z_recv[...], axis=0)
    for i in others:
        y_copy(i).start()
    y_recv[y] = y_send[...]

    def send_go_all(i):
        peer = dp_peer(i)
        to_dp(go_sum, go_all.at[mine], ssem4.at[peer], rsem4.at[me], peer).start()

    loop(1, DP, send_go_all)

    for i in others:
        add_copy(i).wait_send()
        z_copy(i).wait_send()
    for i in others:
        y_arrival(i).wait_recv()
    ag_send[...] = jnp.sum(y_recv[...], axis=0)
    for i in others:
        share_copy(i).start()
    ag_recv[member] = ag_send[...]
    for i in others:
        y_copy(i).wait_send()
        share_copy(i).wait_send()
    loop(1, DP, lambda i: sent_dp(i, go_sum, go_all, ssem4, rsem4))

    def arrived_go_all(i):
        peer = dp_peer(i)
        to_dp(go_sum, go_all.at[peer], ssem4.at[peer], rsem4.at[peer], peer).wait_recv()

    loop(1, DP, arrived_go_all)
    full_out = go_all[...].reshape(COLS, 128).T[0:HID, :]

    for i in others:
        share_arrival(i).wait_recv()
    blocks = ag_recv[...]
    squares = jnp.sum(jnp.sum(blocks * blocks, axis=0)[0:7], axis=0, keepdims=True)
    squares += jnp.sum(blocks, axis=0)[7:8]
    total = jnp.sum(squares, axis=1, keepdims=True)
    scale = jnp.minimum(1.0, clip_norm / (jnp.sqrt(total) + 1e-06))
    for i in range(7):
        pay[7 * i : 7 * i + 7, :] = ag_recv[i, 0:7, :]
    second = pay[0:32, :]
    first = pay[32:48, :]
    line = pay[48:49, 0:HID]
    step_out_ref[...] = adam_step(full_out, w_out_ref[...], m_out_ref[0], m_out_ref[1], scale)
    for part in range(2):
        rows, lanes = slice(32 * part, 32 * part + 32), slice(HID * part, HID * part + HID)
        step_second_ref[rows, :] = adam_step(
            second[:, lanes], w_second_ref[rows, :], m_second_ref[0, rows, :], m_second_ref[1, rows, :], scale
        )
        rows = slice(16 * part + 1, 16 * part + 17)
        step_first_ref[rows, :] = adam_step(
            first[:, lanes], w_first_ref[rows, :], m_first_ref[rows, 0, :], m_first_ref[rows, 1, :], scale
        )
    step_first_ref[0:1, :] = adam_step(
        line, w_first_ref[0:1, :], m_first_ref[0:1, 0, :], m_first_ref[0:1, 1, :], scale
    )


def hand_over(*refs):
    sources, results, held, sems = refs[:3], refs[3:6], refs[6:9], refs[9]
    fetch = [pltpu.make_async_copy(sources[n], held[n], sems.at[0, n]) for n in range(3)]
    write = [pltpu.make_async_copy(held[n], results[n], sems.at[1, n]) for n in range(3)]
    for copy in fetch:
        copy.start()
    for n in range(3):
        fetch[n].wait()
        write[n].start()
    for copy in write:
        copy.wait()


def local(spec_u, spec_g, decay_length, w_first, w_second, w_out, moments_first, moments_second, moments_out):
    dft_parts, last, first = constants()
    f32, bf16 = jnp.float32, jnp.bfloat16
    vmem, sem = pltpu.VMEM, pltpu.SemaphoreType.DMA
    in_vmem = pl.BlockSpec(memory_space=pltpu.VMEM)
    anywhere = pl.BlockSpec(memory_space=pl.ANY)

    def pair(n):
        return [sem((n,)), sem((n,))]

    steps = pl.pallas_call(
        kernel,
        out_shape=(
            jax.ShapeDtypeStruct(w_first.shape, f32),
            jax.ShapeDtypeStruct(w_second.shape, f32),
            jax.ShapeDtypeStruct(w_out.shape, f32),
        ),
        in_specs=[anywhere] * 12,
        out_specs=(in_vmem,) * 3,
        scratch_shapes=[
            vmem((2, ROWS, COLS), f32), vmem((2, ROWS, COLS), f32), sem((4,)),
            vmem((1, COLS), f32), vmem((33, HID), f32), vmem((HID, HID), f32), vmem((HID, COLS), f32),
            vmem((33, 2, HID), f32), vmem((2, HID, HID), f32), vmem((2, HID, COLS), f32),
            vmem((512, 256), bf16), vmem((2, 16, 8, 256), f32), pltpu.SMEM((256,), f32), sem((10,)),
            vmem((DP, 2, 8, ROWS), f32), vmem((DP, 2, 8, ROWS), f32), *pair(DP),
            vmem((16, 8, 2, 8, 256), f32), vmem((1024, 512), bf16), vmem((1024, 512), bf16),
            vmem((COLS, 128), f32), vmem((1024, 128), f32),
            vmem((128, 128), f32), vmem((COLS, 128), f32), vmem((8, 128), f32), vmem((8, 128), f32), *pair(1),
            vmem((HID, 48), bf16), vmem((HID, 192), bf16),
            vmem((96, 8192), bf16), vmem((128, 8192), bf16), vmem((HID, 8192), f32),
            vmem((128, 8192), bf16), vmem((HID, 8192), f32),
            vmem((8, 8192), f32), vmem((8, 8192), f32), vmem((8, 8192), f32), *pair(2),
            vmem((2, 8, 128), f32), vmem((8, 128), f32), *pair(1),
            vmem((8, 128), f32), vmem((DP, 8, 128), f32), *pair(DP),
            vmem((64, 128), f32), vmem((8, 8, 128), f32), vmem((8, 8, 128), f32), *pair(8),
            vmem((8, 128), f32), vmem((8, 8, 128), f32), *pair(8),
            vmem((8, 128), f32), vmem((8, 8, 128), f32), *pair(8),
            vmem((8, 128), f32), vmem((8, 8, 128), f32), *pair(8),
        ],
        compiler_params=pltpu.CompilerParams(
            collective_id=0, has_side_effects=True, vmem_limit_bytes=56 * 1024 * 1024
        ),
        name="hyena_step",
    )(
        spec_u, spec_g, decay_length.reshape(1, COLS), w_first, w_second, w_out,
        jnp.swapaxes(moments_first, 0, 1), moments_second, moments_out,
        jnp.asarray(dft_parts), jnp.asarray(last), jnp.asarray(first),
    )
    return pl.pallas_call(
        hand_over,
        out_shape=[jax.ShapeDtypeStruct(step.shape, f32) for step in steps],
        in_specs=[anywhere] * 3,
        out_specs=[anywhere] * 3,
        scratch_shapes=[vmem(step.shape, f32) for step in steps] + [sem((2, 3))],
        compiler_params=pltpu.CompilerParams(vmem_limit_bytes=56 * 1024 * 1024),
        name="hand_over",
    )(*steps)


def solution(mesh):
    return jax.shard_map(
        local,
        mesh=mesh,
        in_specs=(
            P(None, "dp", "chan"),
            P(None, "dp", "chan"),
            P("chan"),
            P(),
            P(),
            P(None, "chan"),
            P(),
            P(),
            P(None, None, "chan"),
        ),
        out_specs=(P(), P(), P(None, "chan")),
        check_vma=False,
    )
```

```python
import functools
import math

import jax
import jax.numpy as jnp
import numpy as np
from jax import lax
from jax.experimental import pallas as pl
from jax.experimental.pallas import tpu as pltpu
from jax.sharding import PartitionSpec as P

MESH = pl.DeviceIdType.MESH
HIGHEST = lax.Precision.HIGHEST

BANDS = 16
HID = 64
DP = 32
FREQS = 32768
SEQ = 16384
ROWS = 1024
COLS = 256

beta_one = 0.9
beta_two = 0.999
adam_count = 10.0
adam_eps = 1e-08
weight_decay = 0.1
clip_norm = 1.0


def adam_step(grad, weight, first, second, scale):
    g = grad * scale
    first = beta_one * first + (1.0 - beta_one) * g
    second = beta_two * second + (1.0 - beta_two) * g * g
    first_hat = first / (1.0 - beta_one**adam_count)
    second_hat = second / (1.0 - beta_two**adam_count)
    return first_hat / (jnp.sqrt(second_hat) + adam_eps) + weight_decay * weight


def split(x):
    high = x.astype(jnp.bfloat16)
    low = (x - high.astype(jnp.float32)).astype(jnp.bfloat16)
    return high, low


def dot(a, b, dims):
    return lax.dot_general(a, b, (dims, ((), ())), preferred_element_type=jnp.float32)


def stacked(x):
    return jnp.concatenate(split(x), axis=0)


def folded(x, rows):
    x = x[:rows] + x[rows:]
    return x[:, :HID] + x[:, HID:]


def three_rows(x):
    high, low = split(x)
    return jnp.concatenate([high, low, high], axis=0)


def three_lanes(x):
    high, low = split(x)
    return jnp.concatenate([high, high, low], axis=1)


def sine_cosine(x):
    turns = jnp.floor(x * (2.0 / math.pi) + 0.5)
    r = ((x - turns * 1.5703125) - turns * 4.837512969970703125e-4) - turns * 7.54978995489188216e-8
    z = r * r
    sine = r + r * z * (-1.6666654611e-1 + z * (8.3321608736e-3 - z * 1.9515295891e-4))
    cosine = 1.0 - 0.5 * z + z * z * (4.166664568298827e-2 + z * (-1.388731625493765e-3 + z * 2.443315711809948e-5))
    quarter = turns.astype(jnp.int32)
    odd = (quarter & 1) == 1
    first, second = jnp.where(odd, cosine, sine), jnp.where(odd, sine, cosine)
    return jnp.where((quarter & 2) == 2, -first, first), jnp.where(((quarter + 1) & 2) == 2, -second, second)


NN = ((1,), (0,))
NT = ((1,), (1,))


def times(z, angle_num, angle_den):
    re, im = z
    k = angle_num % angle_den
    if k == 0:
        return re, im
    if 4 * k == angle_den:
        return -im, re
    if 2 * k == angle_den:
        return -re, -im
    if 4 * k == 3 * angle_den:
        return im, -re
    if 8 * k == angle_den:
        r = math.sqrt(0.5)
        return (re - im) * r, (re + im) * r
    if 8 * k == 3 * angle_den:
        r = math.sqrt(0.5)
        return (re + im) * (-r), (re - im) * r
    c, s = math.cos(2 * math.pi * k / angle_den), math.sin(2 * math.pi * k / angle_den)
    return re * c - im * s, re * s + im * c


def dft(values):
    n = len(values)
    if n == 1:
        return values
    even, odd = dft(values[0::2]), dft(values[1::2])
    low, high = [], []
    for k in range(n // 2):
        t = times(odd[k], k, n)
        low.append((even[k][0] + t[0], even[k][1] + t[1]))
        high.append((even[k][0] - t[0], even[k][1] - t[1]))
    return low + high


def constants():
    lane = np.arange(256)[:, None] * np.arange(128)[None, :] % 256
    angle = 2.0 * np.pi / 256 * lane
    table = np.concatenate([np.cos(angle), -np.sin(angle)], axis=0).astype(np.float32)
    high = table.astype(jnp.bfloat16)
    low = (table - high.astype(np.float32)).astype(jnp.bfloat16)
    v = np.arange(16)[:, None] + 16 * np.arange(8)[None, :]
    angle = 2.0 * np.pi / FREQS * (v[:, :, None] * np.arange(256)[None, None, :])
    last = (np.stack([np.cos(angle), np.sin(angle)]) / FREQS).astype(np.float32)
    angle = 2.0 * np.pi / 128 * (np.arange(8)[:, None] * np.arange(16)[None, :])
    first = np.stack([np.cos(angle), np.sin(angle)], axis=-1).astype(np.float32)
    return np.concatenate([high, low], axis=1), last, first.reshape(-1)


def kernel(
    u_hbm, g_hbm, decay_hbm, w_first_hbm, w_second_hbm, w_out_hbm, m_first_hbm, m_second_hbm, m_out_hbm,
    dft_hbm, last_hbm, first_hbm,
    step_first_ref, step_second_ref, step_out_ref,
    u_buf, g_buf, in_sem,
    decay_ref, w_first_ref, w_second_ref, w_out_ref, m_first_ref, m_second_ref, m_out_ref,
    dft_ref, last_ref, first_ref, small_sem,
    send1, recv1, ssem1, rsem1,
    mid, x_high, x_low, decay_rows, window,
    wf, w_rows, w_mine, w_theirs, ssem8, rsem8, w_out_parts, w_second_parts, feats, act_one, cos_one, act_two, cos_two,
    own2, send2, recv2, ssem2, rsem2,
    go_send, go_recv, ssem3, rsem3,
    go_sum, go_all, ssem4, rsem4,
    pay, ar_send, ar_recv, ssem5, rsem5,
    z_send, z_recv, ssem6, rsem6,
    y_send, y_recv, ssem9, rsem9,
    ag_send, ag_recv, ssem7, rsem7,
):
    me = lax.axis_index("dp")
    col = lax.axis_index("chan")

    def dp_peer(i):
        return lax.rem(me + i, DP)

    def chunk_of(device):
        return lax.rem(device, 2) * 16 + lax.div(device, 2)

    mine = chunk_of(me)
    z, x = lax.div(me, 4), lax.rem(me, 4)
    y, core = lax.div(col, 2), lax.rem(col, 2)
    member = 2 * x + core
    sibling = col + 1 - 2 * core

    def to_dp(src, dst, ssem, rsem, peer):
        return pltpu.make_async_remote_copy(
            src_ref=src, dst_ref=dst, send_sem=ssem, recv_sem=rsem, device_id=(peer, col), device_id_type=MESH
        )

    def to_member(src, dst, ssem, rsem, peer):
        return pltpu.make_async_remote_copy(
            src_ref=src, dst_ref=dst, send_sem=ssem, recv_sem=rsem,
            device_id=(4 * z + lax.div(peer, 2), 2 * y + lax.rem(peer, 2)), device_id_type=MESH,
        )

    def to_ch(src, dst, ssem, rsem, peer):
        return pltpu.make_async_remote_copy(
            src_ref=src, dst_ref=dst, send_sem=ssem, recv_sem=rsem, device_id=(me, peer), device_id_type=MESH
        )

    def loop(low, high, body, unroll=False):
        def wrapped(i, carry):
            body(i)
            return carry

        lax.fori_loop(low, high, wrapped, 0, unroll=unroll)

    def sent_dp(i, src, dst, ssem, rsem):
        peer = dp_peer(i)
        to_dp(src, dst.at[me], ssem.at[peer], rsem.at[me], peer).wait_send()

    def in_copy(block, which):
        hbm, buf = ((u_hbm, u_buf), (g_hbm, g_buf))[which]
        lanes = pl.ds(block * 128, 128)
        return pltpu.make_async_copy(hbm.at[:, :, lanes], buf.at[:, :, lanes], in_sem.at[2 * block + which])

    for block in range(2):
        for which in range(2):
            in_copy(block, which).start()

    small = [
        pltpu.make_async_copy(src, dst, small_sem.at[n])
        for n, (src, dst) in enumerate((
            (decay_hbm, decay_ref), (w_first_hbm, w_first_ref), (w_second_hbm, w_second_ref),
            (w_out_hbm, w_out_ref), (m_first_hbm, m_first_ref), (m_second_hbm, m_second_ref),
            (m_out_hbm, m_out_ref), (dft_hbm, dft_ref),
            (last_hbm, last_ref), (first_hbm, first_ref),
        ))
    ]

    barrier = pltpu.get_barrier_semaphore()

    def greet_dp(i):
        pl.semaphore_signal(barrier, inc=1, device_id=(dp_peer(i), col), device_id_type=MESH)

    def greet(dp, chan):
        pl.semaphore_signal(barrier, inc=1, device_id=(dp, chan), device_id_type=MESH)

    for i in sorted(range(1, DP), key=lambda i: -min(i, DP - i)):
        greet_dp(i)
    for i in (4, 3, 5, 2, 6, 1, 7):
        greet(me, 2 * lax.rem(y + i, 8) + core)
    for i in (2, 1, 3):
        greet(4 * z + lax.rem(x + i, 4), sibling)
    greet(me, sibling)

    for block in range(2):
        for which in range(2):
            in_copy(block, which).wait()

        def product(kt, block=block):
            rows = pl.ds(pl.multiple_of(kt * 128, 128), 128)
            lanes = pl.ds(block * 128, 128)
            u_re, u_im = u_buf[0, rows, lanes], u_buf[1, rows, lanes]
            g_re, g_im = g_buf[0, rows, lanes], g_buf[1, rows, lanes]
            re = g_re * u_re + g_im * u_im
            im = g_im * u_re - g_re * u_im
            owners = pl.ds(block * 16, 16)
            send1[owners, 0, :, rows] = re.T.reshape(16, 8, 128)
            send1[owners, 1, :, rows] = im.T.reshape(16, 8, 128)

        loop(0, ROWS // 128, product)
        if block == 0:
            pl.semaphore_wait(barrier, DP - 1 + 7 + 4)

        def send(i, block=block):
            n = lax.rem(lax.div(me, 2) + i, 16)
            peer = 2 * n + block

            @pl.when(peer != me)
            def _():
                to_dp(send1.at[block * 16 + n], recv1.at[me], ssem1.at[peer], rsem1.at[me], peer).start()

        loop(0, 16, send)
    for copy in small:
        copy.start()
    recv1[me] = send1[mine]
    for copy in small:
        copy.wait()

    decay_rows[...] = jnp.broadcast_to(decay_ref[...], (128, COLS)).T
    decay = decay_rows[pl.ds(pl.multiple_of(mine * 8, 8), 8), :]
    lane = lax.broadcasted_iota(jnp.int32, (8, 128), 1)

    def make_window(v):
        t = lax.div(v, 8) + 16 * lax.rem(v, 8) + 128 * lane
        window[pl.ds(pl.multiple_of(v * 8, 8), 8), :] = jnp.exp(-t.astype(jnp.float32) / decay)

    loop(0, 128, make_window)

    w_rows[:, 0:HID] = w_out_ref[...].T
    w_rows[:, HID:] = jnp.zeros((COLS, 128 - HID), jnp.float32)
    w_mine[...] = w_rows[pl.ds(pl.multiple_of(mine * 8, 8), 8), :]
    w_copy = to_ch(w_mine, w_theirs, ssem8.at[0], rsem8.at[0], sibling)
    w_copy.start()
    w_second_parts[...] = three_lanes(w_second_ref[...])

    wf[...] = jnp.zeros_like(wf)
    wf[0:32, 0:HID] = w_first_ref[1:33, :]
    wf[32:33, 0:HID] = w_first_ref[0:1, :]
    wf[HID:, 0:HID] = w_second_ref[...]
    turned = wf[...].T
    w_first_t, w_second_t = turned[0:HID, 0:48], turned[0:HID, HID:]

    def activations(n):
        cols = pl.ds(pl.multiple_of(n * 512, 512), 512)
        column = n * 512 + lax.broadcasted_iota(jnp.int32, (16, 512), 1)
        residue = column >> 7
        position = 8 * core + (residue >> 3) + 16 * (residue & 7) + 128 * (column & 127)
        band = lax.broadcasted_iota(jnp.int32, (16, 512), 0) + 1
        angle = 2.0 * math.pi / SEQ * ((band * position) & (SEQ - 1)).astype(jnp.float32)
        sine, cosine = sine_cosine(angle)
        ramp = jnp.where(band == 1, position.astype(jnp.float32) / SEQ, 0.0)
        values = jnp.concatenate([cosine, sine, ramp], axis=0)
        feats[:, cols] = stacked(values)
        pre_one = jnp.dot(w_first_t, values, precision=HIGHEST, preferred_element_type=jnp.float32)
        sine, cosine = sine_cosine(pre_one)
        act_one[:, cols] = stacked(sine)
        cos_one[:, cols] = cosine
        pre_two = jnp.dot(w_second_t, sine, precision=HIGHEST, preferred_element_type=jnp.float32)
        sine, cosine = sine_cosine(pre_two)
        act_two[:, cols] = stacked(sine)
        cos_two[:, cols] = cosine

    loop(0, 16, activations)
    w_copy.wait()
    met = jnp.concatenate([w_mine[...], w_theirs[...], jnp.zeros((112, 128), jnp.float32)], axis=0).T
    w_out_parts[...] = three_lanes(met[0:HID, 0:16])
    go_send[...] = jnp.zeros_like(go_send)
    ar_send[...] = jnp.zeros_like(ar_send)
    pay[...] = jnp.zeros_like(pay)

    def arrived1(i):
        peer = dp_peer(i)
        to_dp(send1.at[peer], recv1.at[peer], ssem1.at[peer], rsem1.at[peer], peer).wait_recv()

    loop(1, DP, arrived1, True)

    def pass_one(n):
        q0, lt = lax.div(n, 2), lax.rem(n, 2)
        half, k1 = lax.div(q0, 4), lax.rem(q0, 4)
        lanes = pl.ds(pl.multiple_of(k1 * 256 + lt * 128, 128), 128)
        out_lanes = pl.ds(pl.multiple_of(lt * 128, 128), 128)
        values = dft([(recv1[2 * q + half, 0, :, lanes], recv1[2 * q + half, 1, :, lanes]) for q in range(16)])
        for v1 in range(16):
            re, im = values[v1]
            if v1 > 0:
                c, s = first_ref[q0 * 32 + 2 * v1], first_ref[q0 * 32 + 2 * v1 + 1]
                re, im = re * c - im * s, re * s + im * c
            mid[v1, q0, 0, :, out_lanes] = re
            mid[v1, q0, 1, :, out_lanes] = im

    def both_one(n):
        pass_one(2 * n)
        pass_one(2 * n + 1)

    loop(0, 8, both_one)

    def pass_two(n):
        v1, lt = lax.div(n, 2), lax.rem(n, 2)
        lanes = pl.ds(pl.multiple_of(lt * 128, 128), 128)
        im_lanes = pl.ds(pl.multiple_of(256 + lt * 128, 128), 128)
        values = dft([(mid[v1, q0, 0, :, lanes], mid[v1, q0, 1, :, lanes]) for q0 in range(8)])
        turned = []
        last_cos, last_sin = last_ref[0, v1, :, lanes], last_ref[1, v1, :, lanes]
        for v2 in range(8):
            re, im = values[v2]
            c, s = last_cos[v2 : v2 + 1], last_sin[v2 : v2 + 1]
            turned.append((re * c - im * s, re * s + im * c))
        for pair in range(4):
            rows = pl.ds(pl.multiple_of(v1 * 64 + pair * 16, 16), 16)
            for part, where in ((0, lanes), (1, im_lanes)):
                x = jnp.concatenate([turned[2 * pair][part], turned[2 * pair + 1][part]], axis=0)
                high, low = split(x)
                x_high[rows, where] = high
                x_low[rows, where] = low

    def both_two(n):
        pass_two(2 * n)
        pass_two(2 * n + 1)

    loop(0, 16, both_two)

    def places(part, half, out):
        rows = pl.ds(pl.multiple_of(part * 512 + half * 256, 256), 256)
        high, low = x_high[rows, :], x_low[rows, :]
        both = dot(high, dft_ref[...], NN)
        y = both[:, :128] + both[:, 128:] + dot(low, dft_ref[:, :128], NN)
        y = y * window[rows, :]
        for v in range(32):
            lanes = 4096 * half + 128 * v
            out[:, lanes : lanes + 128] = y[8 * v : 8 * v + 8, :]

    halves = []
    for half in range(2):
        places(1 - core, half, send2)
        cols = slice(4096 * half, 4096 * half + 4096)
        halves.append(to_ch(send2.at[:, cols], recv2.at[:, cols], ssem2.at[half], rsem2.at[half], sibling))
        halves[half].start()
    for half in range(2):
        places(core, half, own2)

    def met_here(cols):
        return jnp.concatenate([own2[:, cols], recv2[:, cols]], axis=0)

    w_parts, second_parts = w_out_parts[...], w_second_parts[...]
    grad_second = jnp.zeros((2 * HID, 2 * HID), jnp.float32)
    grad_first = jnp.zeros((96, 2 * HID), jnp.float32)
    for j in range(8):
        cols = slice(1024 * j, 1024 * j + 1024)
        if j % 4 == 0:
            halves[j // 4].wait_recv()
        hidden = dot(w_parts, three_rows(met_here(cols)), NN)
        high, low = split(hidden * cos_two[:, cols])
        grad_second += dot(act_one[:, cols], jnp.concatenate([high, low], axis=0), NT)
        back_one = dot(second_parts, jnp.concatenate([high, low, high], axis=0), NN) * cos_one[:, cols]
        grad_first += dot(feats[:, cols], stacked(back_one), NT)
    grad_second = folded(grad_second, HID)
    grad_first = folded(grad_first, 48)

    pay[0:32, :] = jnp.concatenate([grad_second[0:32], grad_second[32:64]], axis=1)
    pay[32:48, :] = jnp.concatenate([grad_first[0:16], grad_first[16:32]], axis=1)
    pay[48:49, 0:HID] = grad_first[32:33]
    for i in range(8):
        ar_send[i, 0:7, :] = pay[7 * i : 7 * i + 7, :]

    def ring(i, at):
        return lax.rem(at + i, 8)

    def add_copy(i):
        peer = ring(i, member)
        return to_member(ar_send.at[peer], ar_recv.at[member], ssem5.at[peer], rsem5.at[member], peer)

    def add_arrival(i):
        peer = ring(i, member)
        return to_member(ar_send.at[peer], ar_recv.at[peer], ssem5.at[peer], rsem5.at[peer], peer)

    def z_copy(i):
        peer = ring(i, z)
        return to_dp(z_send, z_recv.at[z], ssem6.at[peer], rsem6.at[z], 4 * peer + x)

    def z_arrival(i):
        peer = ring(i, z)
        return to_dp(z_send, z_recv.at[peer], ssem6.at[peer], rsem6.at[peer], 4 * peer + x)

    def y_copy(i):
        peer = ring(i, y)
        return to_ch(y_send, y_recv.at[y], ssem9.at[peer], rsem9.at[y], 2 * peer + core)

    def y_arrival(i):
        peer = ring(i, y)
        return to_ch(y_send, y_recv.at[peer], ssem9.at[peer], rsem9.at[peer], 2 * peer + core)

    def share_copy(i):
        peer = ring(i, member)
        return to_member(ag_send, ag_recv.at[member], ssem7.at[peer], rsem7.at[member], peer)

    def share_arrival(i):
        peer = ring(i, member)
        return to_member(ag_send, ag_recv.at[peer], ssem7.at[peer], rsem7.at[peer], peer)

    others = (4, 3, 5, 2, 6, 1, 7)
    for i in others:
        add_copy(i).start()
    ar_recv[member] = ar_send[member]

    grad_out = jnp.zeros((2 * 16, 2 * HID), jnp.float32)
    for j in range(8):
        cols = slice(1024 * j, 1024 * j + 1024)
        grad_out += dot(stacked(met_here(cols)), act_two[:, cols], NT)
    go_send[:, :, 0:HID] = folded(grad_out, 16).reshape(2, 8, HID)
    go_copy = to_ch(go_send.at[1], go_recv, ssem3.at[0], rsem3.at[0], sibling)
    go_copy.start()
    go_copy.wait()
    total_out = go_send[0] + go_recv[...]
    go_sum[...] = total_out
    go_all[mine] = total_out


    for i in others:
        add_arrival(i).wait_recv()
    out_squares = jnp.sum(total_out * total_out, axis=0, keepdims=True)
    row = lax.broadcasted_iota(jnp.int32, (8, 128), 0)
    z_send[...] = jnp.where(row == 7, out_squares, jnp.sum(ar_recv[...], axis=0))
    for i in others:
        z_copy(i).start()
    z_recv[z] = z_send[...]

    loop(1, DP, lambda i: sent_dp(i, send1.at[dp_peer(i)], recv1, ssem1, rsem1))
    for half in range(2):
        halves[half].wait_send()

    for i in others:
        z_arrival(i).wait_recv()
    y_send[...] = jnp.sum(z_recv[...], axis=0)
    for i in others:
        y_copy(i).start()
    y_recv[y] = y_send[...]

    def send_go_all(i):
        peer = dp_peer(i)
        to_dp(go_sum, go_all.at[mine], ssem4.at[peer], rsem4.at[me], peer).start()

    loop(1, DP, send_go_all)

    for i in others:
        add_copy(i).wait_send()
        z_copy(i).wait_send()
    for i in others:
        y_arrival(i).wait_recv()
    ag_send[...] = jnp.sum(y_recv[...], axis=0)
    for i in others:
        share_copy(i).start()
    ag_recv[member] = ag_send[...]
    for i in others:
        y_copy(i).wait_send()
        share_copy(i).wait_send()
    loop(1, DP, lambda i: sent_dp(i, go_sum, go_all, ssem4, rsem4))

    def arrived_go_all(i):
        peer = dp_peer(i)
        to_dp(go_sum, go_all.at[peer], ssem4.at[peer], rsem4.at[peer], peer).wait_recv()

    loop(1, DP, arrived_go_all)
    full_out = go_all[...].reshape(COLS, 128).T[0:HID, :]

    for i in others:
        share_arrival(i).wait_recv()
    blocks = ag_recv[...]
    squares = jnp.sum(jnp.sum(blocks * blocks, axis=0)[0:7], axis=0, keepdims=True)
    squares += jnp.sum(blocks, axis=0)[7:8]
    total = jnp.sum(squares, axis=1, keepdims=True)
    scale = jnp.minimum(1.0, clip_norm / (jnp.sqrt(total) + 1e-06))
    for i in range(7):
        pay[7 * i : 7 * i + 7, :] = ag_recv[i, 0:7, :]
    second = pay[0:32, :]
    first = pay[32:48, :]
    line = pay[48:49, 0:HID]
    step_out_ref[...] = adam_step(full_out, w_out_ref[...], m_out_ref[0], m_out_ref[1], scale)
    for part in range(2):
        rows, lanes = slice(32 * part, 32 * part + 32), slice(HID * part, HID * part + HID)
        step_second_ref[rows, :] = adam_step(
            second[:, lanes], w_second_ref[rows, :], m_second_ref[0, rows, :], m_second_ref[1, rows, :], scale
        )
        rows = slice(16 * part + 1, 16 * part + 17)
        step_first_ref[rows, :] = adam_step(
            first[:, lanes], w_first_ref[rows, :], m_first_ref[rows, 0, :], m_first_ref[rows, 1, :], scale
        )
    step_first_ref[0:1, :] = adam_step(
        line, w_first_ref[0:1, :], m_first_ref[0:1, 0, :], m_first_ref[0:1, 1, :], scale
    )


def hand_over(*refs):
    sources, results, held, sems = refs[:3], refs[3:6], refs[6:9], refs[9]
    fetch = [pltpu.make_async_copy(sources[n], held[n], sems.at[0, n]) for n in range(3)]
    write = [pltpu.make_async_copy(held[n], results[n], sems.at[1, n]) for n in range(3)]
    for copy in fetch:
        copy.start()
    for n in range(3):
        fetch[n].wait()
        write[n].start()
    for copy in write:
        copy.wait()


def local(spec_u, spec_g, decay_length, w_first, w_second, w_out, moments_first, moments_second, moments_out):
    dft_parts, last, first = constants()
    f32, bf16 = jnp.float32, jnp.bfloat16
    vmem, sem = pltpu.VMEM, pltpu.SemaphoreType.DMA
    in_vmem = pl.BlockSpec(memory_space=pltpu.VMEM)
    anywhere = pl.BlockSpec(memory_space=pl.ANY)

    def pair(n):
        return [sem((n,)), sem((n,))]

    steps = pl.pallas_call(
        kernel,
        out_shape=(
            jax.ShapeDtypeStruct(w_first.shape, f32),
            jax.ShapeDtypeStruct(w_second.shape, f32),
            jax.ShapeDtypeStruct(w_out.shape, f32),
        ),
        in_specs=[anywhere] * 12,
        out_specs=(in_vmem,) * 3,
        scratch_shapes=[
            vmem((2, ROWS, COLS), f32), vmem((2, ROWS, COLS), f32), sem((4,)),
            vmem((1, COLS), f32), vmem((33, HID), f32), vmem((HID, HID), f32), vmem((HID, COLS), f32),
            vmem((33, 2, HID), f32), vmem((2, HID, HID), f32), vmem((2, HID, COLS), f32),
            vmem((512, 256), bf16), vmem((2, 16, 8, 256), f32), pltpu.SMEM((256,), f32), sem((10,)),
            vmem((DP, 2, 8, ROWS), f32), vmem((DP, 2, 8, ROWS), f32), *pair(DP),
            vmem((16, 8, 2, 8, 256), f32), vmem((1024, 512), bf16), vmem((1024, 512), bf16),
            vmem((COLS, 128), f32), vmem((1024, 128), f32),
            vmem((128, 128), f32), vmem((COLS, 128), f32), vmem((8, 128), f32), vmem((8, 128), f32), *pair(1),
            vmem((HID, 48), bf16), vmem((HID, 192), bf16),
            vmem((96, 8192), bf16), vmem((128, 8192), bf16), vmem((HID, 8192), f32),
            vmem((128, 8192), bf16), vmem((HID, 8192), f32),
            vmem((8, 8192), f32), vmem((8, 8192), f32), vmem((8, 8192), f32), *pair(2),
            vmem((2, 8, 128), f32), vmem((8, 128), f32), *pair(1),
            vmem((8, 128), f32), vmem((DP, 8, 128), f32), *pair(DP),
            vmem((64, 128), f32), vmem((8, 8, 128), f32), vmem((8, 8, 128), f32), *pair(8),
            vmem((8, 128), f32), vmem((8, 8, 128), f32), *pair(8),
            vmem((8, 128), f32), vmem((8, 8, 128), f32), *pair(8),
            vmem((8, 128), f32), vmem((8, 8, 128), f32), *pair(8),
        ],
        compiler_params=pltpu.CompilerParams(
            collective_id=0, has_side_effects=True, vmem_limit_bytes=56 * 1024 * 1024
        ),
        name="hyena_step",
    )(
        spec_u, spec_g, decay_length.reshape(1, COLS), w_first, w_second, w_out,
        jnp.swapaxes(moments_first, 0, 1), moments_second, moments_out,
        jnp.asarray(dft_parts), jnp.asarray(last), jnp.asarray(first),
    )
    return pl.pallas_call(
        hand_over,
        out_shape=[jax.ShapeDtypeStruct(step.shape, f32) for step in steps],
        in_specs=[anywhere] * 3,
        out_specs=[anywhere] * 3,
        scratch_shapes=[vmem(step.shape, f32) for step in steps] + [sem((2, 3))],
        compiler_params=pltpu.CompilerParams(vmem_limit_bytes=56 * 1024 * 1024),
        name="hand_over",
    )(*steps)


def solution(mesh):
    return jax.shard_map(
        local,
        mesh=mesh,
        in_specs=(
            P(None, "dp", "chan"),
            P(None, "dp", "chan"),
            P("chan"),
            P(),
            P(),
            P(None, "chan"),
            P(),
            P(),
            P(None, None, "chan"),
        ),
        out_specs=(P(), P(), P(None, "chan")),
        check_vma=False,
    )
```
